32 devices in a mesh: shard: 8 (over z, x), tensor: 4 (over y, core).
Axes of the slice: x: 2, y: 2, z: 4, core: 2. Of those that a mesh axis runs over, the one named last changes fastest.
Arguments:
- gradient: bfloat16 [768, 3072], P('shard', 'tensor'), may hold values from -12 to 12
- moment_one: float32 [768, 3072], P('shard', 'tensor'), may hold values from -6 to 6
- moment_two: float32 [768, 3072], P('shard', 'tensor'), may hold values from 0.5 to 8
- stat_left: float32 [768, 768], P('shard'), may hold values from -1 to 3, as said below
- stat_right: float32 [3072, 3072], P('shard', 'tensor'), may hold values from -1 to 3, as said below
- basis_left: float32 [768, 768], P('shard'), may hold values from -3 to 25, as said below
- basis_right: float32 [3072, 3072], P('shard', 'tensor'), may hold values from -3 to 47, as said below
Outputs:
- update: bfloat16 [768, 3072], P('shard', 'tensor')
- new_moment_one: float32 [768, 3072], P('shard', 'tensor')
- new_moment_two: float32 [768, 3072], P('shard', 'tensor')
- new_stat_left: float32 [768, 768], P('shard')
- new_stat_right: float32 [3072, 3072], P('shard', 'tensor')
- new_basis_left: float32 [768, 768], P('shard')
- new_basis_right: float32 [3072, 3072], P('shard', 'tensor')
The draws below stay inside these ranges and needn't reach their ends.
Inputs may be any that keep to these rules, and one draw needn't show every extreme that they name: `stat_left`: symmetric and positive definite. `stat_right`: symmetric and positive definite. `basis_left`: full rank. `basis_right`: full rank.
All inputs are finite; a program needn't handle non-finite values.
Results may differ from the reference program's by a relative error of at most 0.011.
Values may be sent and summed in bfloat16 or wider, within the bound.
No kernel may reach another device: no remote copies, remote signals or barrier semaphores. Data moves between devices by JAX's collectives and lax.ppermute only.
A program may use at most 64 MiB of HBM per device.

```python
import math
import jax
import jax.numpy as jnp
from jax import lax

D = 768
FF = 3072
NS_STEPS = 2


def statistic_matrix(key, matrix_order):
    level_key, noise_key = jax.random.split(key)
    levels = jnp.exp(jax.random.uniform(level_key, (matrix_order,), jnp.float32, math.log(0.25), math.log(2.0)))
    noise_field = jnp.clip(jax.random.normal(noise_key, (matrix_order, matrix_order), jnp.float32), -4.0, 4.0)
    scaled = noise_field * (0.1 / math.sqrt(matrix_order))
    identity = jnp.eye(matrix_order, dtype=jnp.float32)
    return (scaled + scaled.T) * 0.70710678 + identity * levels[None, :]


def basis_matrix(key, matrix_order):
    noise_field = jnp.clip(jax.random.normal(key, (matrix_order, matrix_order), jnp.float32), -4.0, 4.0)
    identity = jnp.eye(matrix_order, dtype=jnp.float32)
    return identity * (0.8 * math.sqrt(matrix_order)) + 0.6 * noise_field


def draw_stat_left(key, part):
    return statistic_matrix(jax.random.fold_in(key, 11), D)


def draw_stat_right(key, part):
    return statistic_matrix(jax.random.fold_in(key, 12), FF)


def draw_basis_left(key, part):
    return basis_matrix(jax.random.fold_in(key, 13), D)


def draw_basis_right(key, part):
    return basis_matrix(jax.random.fold_in(key, 14), FF)


def raised(array, own_key, source, target, blocks, factor):
    owner, partner = [(jnp.arange(array.shape[position]) // (array.shape[position] // blocks)).reshape([-1 if axis == position else 1 for axis in range(array.ndim)]) for position in (source, target)]
    chosen = jax.random.permutation(own_key, blocks)[partner]
    strong = (owner == chosen) | (owner == (partner + blocks // 2) % blocks)
    return jnp.where(strong, factor * array, array)


def level_of(stream_key, shape, cuts, smallest, top_value):
    loudness, own = 1.0, jax.random.fold_in(stream_key, 6)
    for dim, parts in cuts:
        draws = jnp.exp(jax.random.uniform(jax.random.fold_in(own, dim), (parts,), jnp.float32, smallest / len(cuts), top_value / len(cuts)))
        loudness = loudness * jnp.repeat(draws, shape[dim] // parts).reshape([-1 if axis == dim else 1 for axis in range(len(shape))])
    return loudness


def noise(own_key, shape, scale, most, pieces=(), kind=jnp.bfloat16):
    result = scale * jax.random.normal(own_key, shape, jnp.float32)
    if pieces:
        result = result * level_of(own_key, shape, pieces, -0.22, 0.18)
    return jnp.clip(result, -most, most).astype(kind)


def gaussian_with(own_key, extent, width, most, cuts, heavy, held_as=jnp.bfloat16):
    entries = width * jax.random.normal(own_key, extent, jnp.float32)
    if cuts:
        entries = entries * level_of(own_key, extent, cuts, -0.22, 0.18)
    return jnp.clip(raised(entries, jax.random.fold_in(own_key, 3), *heavy), -most, most).astype(held_as)


def setup_inputs(seed: int = 0) -> dict:
    keys = jax.random.split(jax.random.key(seed), 8)
    gradient = gaussian_with(keys[0], (D, FF), 2.0, 12.0, ((0, 8), (1, 4)), (0, 1, 8, 2.0))
    moment_one = noise(keys[1], (D, FF), 1.0, 6.0, ((0, 8), (1, 4)), jnp.float32)
    moment_two = jnp.clip(jnp.exp(math.log(8.0) - 2.7725887 * jax.random.uniform(keys[2], (D, FF), jnp.float32) ** level_of(keys[2], (D, FF), ((0, 8), (1, 4)), -0.2, 0.2)), 0.5, 8.0)
    stat_left = draw_stat_left(jax.random.fold_in(keys[7], 71), 0)
    stat_right = draw_stat_right(jax.random.fold_in(keys[7], 71), 0)
    basis_left = draw_basis_left(jax.random.fold_in(keys[7], 71), 0)
    basis_right = draw_basis_right(jax.random.fold_in(keys[7], 71), 0)
    return dict(gradient=gradient, moment_one=moment_one, moment_two=moment_two, stat_left=stat_left, stat_right=stat_right, basis_left=basis_left, basis_right=basis_right)


beta_one = 0.95
beta_two = 0.95
beta_stat = 0.95
correction = 1.0 - 0.95 ** 10
adam_eps = 1e-08
highest = lax.Precision.HIGHEST

def blend_stat(previous, product, divisor):
    return beta_stat * previous + (1.0 - beta_stat) * (product / divisor)

def adam_moments(rotated, moment_one, moment_two):
    first_moment = beta_one * moment_one + (1.0 - beta_one) * rotated
    second_moment = beta_two * moment_two + (1.0 - beta_two) * (rotated * rotated)
    direction = (first_moment / correction / (jnp.sqrt(second_moment / correction) + adam_eps)).astype(jnp.bfloat16)
    return (first_moment, second_moment, direction)

def reference(gradient, moment_one, moment_two, stat_left, stat_right, basis_left, basis_right):
    left_q = basis_left / math.sqrt(D)
    right_q = basis_right / math.sqrt(FF)
    left_qb = left_q.astype(jnp.bfloat16)
    right_qb = right_q.astype(jnp.bfloat16)
    new_stat_left = blend_stat(stat_left, jnp.dot(gradient, gradient.T, preferred_element_type=jnp.float32), FF)
    new_stat_right = blend_stat(stat_right, jnp.dot(gradient.T, gradient, preferred_element_type=jnp.float32), D)
    half_rotated = jnp.dot(left_qb.T, gradient, preferred_element_type=jnp.float32).astype(jnp.bfloat16)
    rotated = jnp.dot(half_rotated, right_qb, preferred_element_type=jnp.float32)
    new_moment_one, new_moment_two, direction = adam_moments(rotated, moment_one, moment_two)
    back_half = jnp.dot(left_qb, direction, preferred_element_type=jnp.float32).astype(jnp.bfloat16)
    update = jnp.dot(back_half, right_qb.T, preferred_element_type=jnp.float32).astype(jnp.bfloat16)
    power_left = jnp.dot(new_stat_left, left_q, precision=highest, preferred_element_type=jnp.float32)
    iterate_left = power_left * (math.sqrt(D) / (4.0 * jnp.sqrt(jnp.sum(power_left * power_left))))
    for iteration in range(NS_STEPS):
        gram_left = jnp.dot(iterate_left.T, iterate_left, precision=highest, preferred_element_type=jnp.float32)
        iterate_left = 1.5 * iterate_left - 0.5 * jnp.dot(iterate_left, gram_left, precision=highest, preferred_element_type=jnp.float32)
    power_right = jnp.dot(new_stat_right, right_q, precision=highest, preferred_element_type=jnp.float32)
    iterate_right = power_right * (math.sqrt(FF) / (4.0 * jnp.sqrt(jnp.sum(power_right * power_right))))
    identity = jnp.eye(FF, dtype=jnp.float32)
    for iteration in range(NS_STEPS):
        rounded_iterate = iterate_right.astype(jnp.bfloat16)
        gram_right = jnp.dot(rounded_iterate.T, rounded_iterate, preferred_element_type=jnp.float32)
        mixing = (1.5 * identity - 0.5 * gram_right).astype(jnp.bfloat16)
        iterate_right = jnp.dot(rounded_iterate, mixing, preferred_element_type=jnp.float32)
    return (update, new_moment_one, new_moment_two, new_stat_left, new_stat_right, iterate_left * math.sqrt(D), iterate_right * math.sqrt(FF))
```

```python
import math

import jax
import jax.numpy as jnp
from jax import lax
from jax.experimental import pallas as pl
from jax.experimental.pallas import tpu as pltpu
from jax.sharding import PartitionSpec as P

D = 768
FF = 3072
NS_STEPS = 2


beta_one = 0.95
beta_two = 0.95
beta_stat = 0.95
correction = 1.0 - 0.95**10
adam_eps = 1e-08
highest = lax.Precision.HIGHEST


def blend_stat(previous, product, divisor):
    return beta_stat * previous + (1.0 - beta_stat) * (product / divisor)


def adam_moments(rotated, moment_one, moment_two):
    first_moment = beta_one * moment_one + (1.0 - beta_one) * rotated
    second_moment = beta_two * moment_two + (1.0 - beta_two) * (rotated * rotated)
    direction = (
        first_moment / correction / (jnp.sqrt(second_moment / correction) + adam_eps)
    ).astype(jnp.bfloat16)
    return (first_moment, second_moment, direction)


def local_general(gradient, moment_one, moment_two, stat_left, stat_right, basis_left, basis_right):
    rows_left = gradient.shape[0]
    rows_right = stat_right.shape[0]
    cols_right = stat_right.shape[1]
    shard_pos = lax.axis_index("shard")
    tensor_pos = lax.axis_index("tensor")
    row_start = shard_pos * rows_left
    grad_cols = lax.all_gather(gradient, "shard", axis=0, tiled=True)
    left_terms = jnp.dot(gradient, grad_cols.T, preferred_element_type=jnp.float32)
    gram_rows = lax.psum(left_terms.astype(jnp.bfloat16), "tensor").astype(jnp.float32)
    new_stat_left = blend_stat(stat_left, gram_rows, FF)
    grad_whole = lax.all_gather(grad_cols, "tensor", axis=1, tiled=True)
    picked = lax.dynamic_slice_in_dim(grad_whole, shard_pos * rows_right, rows_right, 1)
    gram_block = jnp.dot(picked.T, grad_cols, preferred_element_type=jnp.float32)
    new_stat_right = blend_stat(stat_right, gram_block, D)
    basis_all = lax.all_gather(basis_left, "shard", axis=0, tiled=True)
    left_q_all = basis_all / math.sqrt(D)
    left_qb_all = left_q_all.astype(jnp.bfloat16)
    left_qb_own = lax.dynamic_slice_in_dim(left_qb_all, row_start, rows_left, 0)
    left_cols_own = lax.dynamic_slice_in_dim(left_qb_all, row_start, rows_left, 1)
    half_rotated = jnp.dot(left_cols_own.T, grad_cols, preferred_element_type=jnp.float32).astype(
        jnp.bfloat16
    )
    right_q = basis_right / math.sqrt(FF)
    right_qb = right_q.astype(jnp.bfloat16)
    right_cols_b = lax.all_gather(right_qb, "shard", axis=0, tiled=True)
    half_full = lax.all_gather(half_rotated, "tensor", axis=1, tiled=True)
    rotated = jnp.dot(half_full, right_cols_b, preferred_element_type=jnp.float32)
    new_moment_one, new_moment_two, direction = adam_moments(rotated, moment_one, moment_two)
    back_half = jnp.dot(
        left_qb_own,
        lax.all_gather(direction, "shard", axis=0, tiled=True),
        preferred_element_type=jnp.float32,
    ).astype(jnp.bfloat16)
    back_terms = jnp.dot(back_half, right_cols_b.T, preferred_element_type=jnp.float32)
    update = lax.psum_scatter(back_terms, "tensor", scatter_dimension=1, tiled=True).astype(
        jnp.bfloat16
    )
    stat_rows = lax.all_gather(new_stat_right, "tensor", axis=1, tiled=True)
    power_right = jnp.dot(
        stat_rows,
        lax.all_gather(right_q, "shard", axis=0, tiled=True),
        precision=highest,
        preferred_element_type=jnp.float32,
    )
    power_left = jnp.dot(
        new_stat_left, left_q_all, precision=highest, preferred_element_type=jnp.float32
    )
    local_left = jnp.sum(power_left * power_left)
    local_right = jnp.sum(power_right * power_right)
    total_left = lax.psum(local_left, "shard")
    total_right = lax.psum(local_right, ("shard", "tensor"))
    iterate_left = power_left * (math.sqrt(D) / (4.0 * jnp.sqrt(total_left)))
    for iteration in range(NS_STEPS):
        partial_gram = jnp.dot(
            iterate_left.T, iterate_left, precision=highest, preferred_element_type=jnp.float32
        )
        gram_left = lax.psum(partial_gram.astype(jnp.bfloat16), "shard").astype(jnp.float32)
        iterate_left = 1.5 * iterate_left - 0.5 * jnp.dot(
            iterate_left, gram_left, precision=highest, preferred_element_type=jnp.float32
        )
    iterate_right = power_right * (math.sqrt(FF) / (4.0 * jnp.sqrt(total_right)))
    row_ids = shard_pos * rows_right + lax.broadcasted_iota(jnp.int32, (rows_right, cols_right), 0)
    col_ids = tensor_pos * cols_right + lax.broadcasted_iota(jnp.int32, (rows_right, cols_right), 1)
    identity_tile = (row_ids == col_ids).astype(jnp.float32)
    for iteration in range(NS_STEPS):
        rounded_iterate = iterate_right.astype(jnp.bfloat16)
        iterate_rows = lax.all_gather(rounded_iterate, "tensor", axis=1, tiled=True)
        gram_right = lax.psum_scatter(
            jnp.dot(iterate_rows.T, rounded_iterate, preferred_element_type=jnp.float32).astype(
                jnp.bfloat16
            ),
            "shard",
            scatter_dimension=0,
            tiled=True,
        ).astype(jnp.float32)
        mixing = (1.5 * identity_tile - 0.5 * gram_right).astype(jnp.bfloat16)
        iterate_right = jnp.dot(
            iterate_rows,
            lax.all_gather(mixing, "shard", axis=0, tiled=True),
            preferred_element_type=jnp.float32,
        )
    return (
        update,
        new_moment_one,
        new_moment_two,
        new_stat_left,
        new_stat_right,
        iterate_left * math.sqrt(D),
        iterate_right * math.sqrt(FF),
    )


BF = jnp.bfloat16
F32 = jnp.float32
AXES = ("shard", "tensor")
PATTERN = (4, 2, 2, 2)


def dot_nn(a, b):
    return jnp.dot(a, b, preferred_element_type=F32)


def dot_nt(a, b):
    return lax.dot_general(a, b, (((1,), (1,)), ((), ())), preferred_element_type=F32)


def dot_tn(a, b):
    return lax.dot_general(a, b, (((0,), (0,)), ((), ())), preferred_element_type=F32)


def pairs(move):
    nz, nx, ny, nc = PATTERN
    out = []
    for z in range(nz):
        for x in range(nx):
            for y in range(ny):
                for c in range(nc):
                    to = move(z, x, y, c)
                    if 0 <= to[0] < nz:
                        source = ((z * nx + x) * ny + y) * nc + c
                        target = ((to[0] * nx + to[1]) * ny + to[2]) * nc + to[3]
                        out.append((source, target))
    return out


def swap_x(a):
    return lax.ppermute(a, AXES, pairs(lambda z, x, y, c: (z, 1 - x, y, c)))


def swap_y(a):
    return lax.ppermute(a, AXES, pairs(lambda z, x, y, c: (z, x, 1 - y, c)))


def swap_core(a):
    return lax.ppermute(a, AXES, pairs(lambda z, x, y, c: (z, x, y, 1 - c)))


def step_z(a, by, first, last):
    full = pairs(lambda z, x, y, c: (z + by if first <= z <= last else -1, x, y, c))
    return lax.ppermute(a, AXES, full)


def gather_z(a, z):
    up1 = step_z(a, 1, 0, 2)
    down1 = step_z(a, -1, 1, 3)
    up2 = step_z(up1, 1, 1, 2)
    down2 = step_z(down1, -1, 1, 2)
    up3 = step_z(up2, 1, 2, 2)
    down3 = step_z(down2, -1, 1, 1)
    near = jnp.where(z % 2 == 0, down1, up1)
    mid = jnp.where(z == 0, down2, jnp.where(z == 1, down1, jnp.where(z == 2, up1, up2)))
    far = jnp.where(z == 0, down3, jnp.where(z == 1, down2, jnp.where(z == 2, up2, up3)))
    return [a, near, mid, far]


def places_z(z):
    near = z + 1 - 2 * (z % 2)
    mid = jnp.where(z == 0, 2, jnp.where(z == 1, 2, 1))
    far = jnp.where(z < 2, 3, 0)
    return [z, near, mid, far]


def put(whole, part, row, col):
    return lax.dynamic_update_slice(whole, part, (row, col))


def gather_rows_zx(a, z, x):
    rows = a.shape[0]
    whole = jnp.zeros((8 * rows, a.shape[1]), a.dtype)
    for block, place in zip(gather_z(a, z), places_z(z)):
        whole = put(whole, block, (2 * place + x) * rows, 0)
        whole = put(whole, swap_x(block), (2 * place + 1 - x) * rows, 0)
    return whole


def gather_rows_xz(a, z, x):
    rows = a.shape[0]
    other = swap_x(a)
    pair = jnp.where(x == 0, jnp.concatenate([a, other]), jnp.concatenate([other, a]))
    whole = jnp.zeros((8 * rows, a.shape[1]), a.dtype)
    for block, place in zip(gather_z(pair, z), places_z(z)):
        whole = put(whole, block, 2 * place * rows, 0)
    return whole


def gather_cols(a, y, core):
    cols = a.shape[1]
    far = swap_y(a)
    whole = jnp.zeros((a.shape[0], 4 * cols), a.dtype)
    whole = put(whole, a, 0, (2 * y + core) * cols)
    whole = put(whole, swap_core(a), 0, (2 * y + 1 - core) * cols)
    whole = put(whole, far, 0, (2 - 2 * y + core) * cols)
    whole = put(whole, swap_core(far), 0, (3 - 2 * y - core) * cols)
    return whole


def gather_slabs(a, z):
    half = a.shape[0] // 2
    slabs = []
    for block in gather_z(a, z):
        over_x = swap_x(block)
        over_y = swap_y(block)
        diagonal = jnp.concatenate([swap_y(over_x[:half]), swap_x(over_y[half:])])
        slab = jnp.concatenate(
            [
                jnp.concatenate([block, over_y], axis=1),
                jnp.concatenate([over_x, diagonal], axis=1),
            ]
        )
        slabs.append((slab, swap_core(slab)))
    return slabs


def refresh_kernel(scale_ref, *refs):
    slabs = refs[:8]
    rows_ref, out_ref, whole, inner, held, total, first, sems = refs[8:]
    size = whole.shape[0]
    tall = size // 4
    wide = size // 2
    square = scale_ref[0]

    def copy(k):
        return pltpu.make_async_copy(
            slabs[k],
            whole.at[pl.ds((k // 2) * tall, tall), pl.ds((k % 2) * wide, wide)],
            sems.at[k],
        )

    for k in range(8):
        copy(k).start()
    held[...] = rows_ref[...]
    total[...] = rows_ref[...].astype(F32)

    def one_pass(i, carry):
        def towards(j, carry):
            @pl.when(i == 0)
            def _():
                for k in range(4):

                    @pl.when(j == k)
                    def _():
                        copy(2 * k).wait()
                        copy(2 * k + 1).wait()

            span = pl.ds(pl.multiple_of(j * tall, tall), tall)
            inner[:, span] = dot_nt(held[...], whole[span, :]).astype(BF)
            return carry

        lax.fori_loop(0, 4, towards, 0)
        keep = jnp.where(i == 1, 0.0, 1.5)
        take = jnp.where(i == 1, square, -0.5 * square)

        def back(j, carry):
            chunk = jnp.where(i == 3, 2 * j, j)
            span = pl.ds(pl.multiple_of(chunk * tall, tall), tall)
            value = keep * total[:, span] + take * dot_nn(inner[...], whole[:, span])
            total[:, span] = value
            held[:, span] = value.astype(BF)

            @pl.when(i == 0)
            def _():
                first[:, span] = value

            return carry

        lax.fori_loop(0, jnp.where(i == 3, 2, 4), back, 0)
        return carry

    lax.fori_loop(0, 4, one_pass, 0)
    last = scale_ref[1]
    for k in range(2):
        span = slice(2 * k * tall, (2 * k + 1) * tall)
        out_ref[:, k * tall : (k + 1) * tall] = last * (
            1.5 * first[:, span] - 0.5 * total[:, span]
        )


def refresh_rows(scales, slabs, rows):
    size = rows.shape[1]
    count = rows.shape[0]
    return pl.pallas_call(
        refresh_kernel,
        out_shape=jax.ShapeDtypeStruct((count, size // 2), F32),
        in_specs=[pl.BlockSpec(memory_space=pltpu.SMEM)]
        + [pl.BlockSpec(memory_space=pl.ANY)] * 8
        + [pl.BlockSpec(memory_space=pltpu.VMEM)],
        out_specs=pl.BlockSpec(memory_space=pltpu.VMEM),
        scratch_shapes=[
            pltpu.VMEM((size, size), BF),
            pltpu.VMEM((count, size), BF),
            pltpu.VMEM((count, size), BF),
            pltpu.VMEM((count, size), F32),
            pltpu.VMEM((count, size), F32),
            pltpu.SemaphoreType.DMA((8,)),
        ],
        compiler_params=pltpu.CompilerParams(vmem_limit_bytes=48 * 2**20),
        cost_estimate=pl.CostEstimate(
            flops=15 * count * size * size, bytes_accessed=2 * size * size, transcendentals=0
        ),
    )(scales, *[part for pair in slabs for part in pair], rows)


def local_pattern(gradient, moment_one, moment_two, stat_left, stat_right, basis_left, basis_right):
    rows_left = gradient.shape[0]
    rows_right = stat_right.shape[0]
    cols_right = stat_right.shape[1]
    shard_pos = lax.axis_index("shard")
    tensor_pos = lax.axis_index("tensor")
    z, x = shard_pos // 2, shard_pos % 2
    y, core = tensor_pos // 2, tensor_pos % 2

    left_b = (basis_left / math.sqrt(D)).astype(BF)
    right_b = (basis_right / math.sqrt(FF)).astype(BF)
    stat_b = stat_right.astype(BF)

    both = gather_rows_zx(jnp.concatenate([gradient, left_b], axis=1), z, x)
    grad_cols, left_all = both[:, :cols_right], both[:, cols_right:]
    right_cols = gather_rows_zx(right_b, z, x)
    grad_whole = gather_cols(grad_cols, y, core)
    stat_rows = gather_cols(stat_b, y, core)

    share = (1.0 - beta_stat) / D
    picked = lax.dynamic_slice_in_dim(grad_whole, shard_pos * rows_right, rows_right, 1)
    carried = dot_nn(grad_whole, right_cols).astype(BF)
    power_right = beta_stat * dot_nn(stat_rows, right_cols) + share * dot_tn(picked, carried)
    new_stat_right = blend_stat(stat_right, dot_tn(picked, grad_cols), D)
    slabs = gather_slabs(power_right.astype(BF), z)

    left_cols_own = lax.dynamic_slice_in_dim(left_all, shard_pos * rows_left, rows_left, 1)
    left_rows_own = lax.dynamic_slice_in_dim(left_all, shard_pos * rows_left, rows_left, 0)
    rotated = dot_tn(left_cols_own, carried)
    new_moment_one, new_moment_two, direction = adam_moments(rotated, moment_one, moment_two)
    direction_cols = gather_rows_xz(direction, z, x)
    back_half = dot_nn(left_rows_own, direction_cols).astype(BF)
    back_terms = dot_nt(back_half, right_cols)
    width = 2 * cols_right
    away = lax.dynamic_slice_in_dim(back_terms, (1 - y) * width, width, 1).astype(BF)
    near = lax.dynamic_slice_in_dim(back_terms, y * width, width, 1) + swap_y(away).astype(F32)
    away = lax.dynamic_slice_in_dim(near, (1 - core) * cols_right, cols_right, 1).astype(BF)
    near = lax.dynamic_slice_in_dim(near, core * cols_right, cols_right, 1)
    update = (near + swap_core(away).astype(F32)).astype(BF)

    grad_rows = lax.dynamic_slice_in_dim(grad_whole, shard_pos * rows_left, rows_left, 0)
    new_stat_left = blend_stat(stat_left, dot_nt(grad_rows, grad_whole), FF)
    power_left = dot_nn(new_stat_left.astype(BF), left_all)
    power_all = gather_rows_xz(power_left.astype(BF), z, x)
    total_left = jnp.sum(jnp.square(power_all.astype(F32)))
    square_left = D / (16.0 * total_left)
    keep = power_left
    value = power_left
    for turn in range(4):
        across = dot_nt(value.astype(BF), power_all).astype(BF)
        moved = square_left * dot_nn(across, power_all)
        value = moved if turn == 1 else 1.5 * value - 0.5 * moved
        if turn == 0:
            keep = value
    value = 1.5 * keep - 0.5 * value
    new_basis_left = value * (math.sqrt(D) * jnp.sqrt(square_left))

    total_right = sum(jnp.sum(jnp.square(part.astype(F32))) for pair in slabs for part in pair)
    square_right = FF / (16.0 * total_right)
    half = rows_right // 2
    own = jnp.concatenate([part[:rows_right] for part in slabs[0]], axis=1)
    own = lax.dynamic_slice_in_dim(own, core * half, half, 0)
    scales = jnp.stack([square_right, math.sqrt(FF) * jnp.sqrt(square_right)])
    fresh = refresh_rows(scales, slabs, own)
    mine = fresh[:, :cols_right]
    theirs = swap_core(fresh[:, cols_right:])
    new_basis_right = jnp.where(
        core == 0, jnp.concatenate([mine, theirs]), jnp.concatenate([theirs, mine])
    )
    return (
        update,
        new_moment_one,
        new_moment_two,
        new_stat_left,
        new_stat_right,
        new_basis_left,
        new_basis_right,
    )


def solution(mesh):
    nz, nx, ny, nc = PATTERN
    fits = (mesh.shape["shard"], mesh.shape["tensor"]) == (nz * nx, ny * nc)
    local = local_pattern if fits else local_general
    placed = (
        P("shard", "tensor"),
        P("shard", "tensor"),
        P("shard", "tensor"),
        P("shard", None),
        P("shard", "tensor"),
        P("shard", None),
        P("shard", "tensor"),
    )
    return jax.shard_map(
        local,
        mesh=mesh,
        in_specs=placed,
        out_specs=(
            P("shard", "tensor"),
            P("shard", "tensor"),
            P("shard", "tensor"),
            P("shard", None),
            P("shard", "tensor"),
            P("shard", None),
            P("shard", "tensor"),
        ),
        check_vma=False,
    )
```

```python
import functools
import math

import jax
import jax.numpy as jnp
from jax import lax
from jax.experimental import pallas as pl
from jax.experimental.pallas import tpu as pltpu
from jax.sharding import PartitionSpec as P

D = 768
FF = 3072
NS_STEPS = 2


beta_one = 0.95
beta_two = 0.95
beta_stat = 0.95
correction = 1.0 - 0.95**10
adam_eps = 1e-08
highest = lax.Precision.HIGHEST


def blend_stat(previous, product, divisor):
    return beta_stat * previous + (1.0 - beta_stat) * (product / divisor)


def adam_moments(rotated, moment_one, moment_two):
    first_moment = beta_one * moment_one + (1.0 - beta_one) * rotated
    second_moment = beta_two * moment_two + (1.0 - beta_two) * (rotated * rotated)
    direction = (
        first_moment / correction / (jnp.sqrt(second_moment / correction) + adam_eps)
    ).astype(jnp.bfloat16)
    return (first_moment, second_moment, direction)


def local_general(gradient, moment_one, moment_two, stat_left, stat_right, basis_left, basis_right):
    rows_left = gradient.shape[0]
    rows_right = stat_right.shape[0]
    cols_right = stat_right.shape[1]
    shard_pos = lax.axis_index("shard")
    tensor_pos = lax.axis_index("tensor")
    row_start = shard_pos * rows_left
    grad_cols = lax.all_gather(gradient, "shard", axis=0, tiled=True)
    left_terms = jnp.dot(gradient, grad_cols.T, preferred_element_type=jnp.float32)
    gram_rows = lax.psum(left_terms.astype(jnp.bfloat16), "tensor").astype(jnp.float32)
    new_stat_left = blend_stat(stat_left, gram_rows, FF)
    grad_whole = lax.all_gather(grad_cols, "tensor", axis=1, tiled=True)
    picked = lax.dynamic_slice_in_dim(grad_whole, shard_pos * rows_right, rows_right, 1)
    gram_block = jnp.dot(picked.T, grad_cols, preferred_element_type=jnp.float32)
    new_stat_right = blend_stat(stat_right, gram_block, D)
    basis_all = lax.all_gather(basis_left, "shard", axis=0, tiled=True)
    left_q_all = basis_all / math.sqrt(D)
    left_qb_all = left_q_all.astype(jnp.bfloat16)
    left_qb_own = lax.dynamic_slice_in_dim(left_qb_all, row_start, rows_left, 0)
    left_cols_own = lax.dynamic_slice_in_dim(left_qb_all, row_start, rows_left, 1)
    half_rotated = jnp.dot(left_cols_own.T, grad_cols, preferred_element_type=jnp.float32).astype(
        jnp.bfloat16
    )
    right_q = basis_right / math.sqrt(FF)
    right_qb = right_q.astype(jnp.bfloat16)
    right_cols_b = lax.all_gather(right_qb, "shard", axis=0, tiled=True)
    half_full = lax.all_gather(half_rotated, "tensor", axis=1, tiled=True)
    rotated = jnp.dot(half_full, right_cols_b, preferred_element_type=jnp.float32)
    new_moment_one, new_moment_two, direction = adam_moments(rotated, moment_one, moment_two)
    back_half = jnp.dot(
        left_qb_own,
        lax.all_gather(direction, "shard", axis=0, tiled=True),
        preferred_element_type=jnp.float32,
    ).astype(jnp.bfloat16)
    back_terms = jnp.dot(back_half, right_cols_b.T, preferred_element_type=jnp.float32)
    update = lax.psum_scatter(back_terms, "tensor", scatter_dimension=1, tiled=True).astype(
        jnp.bfloat16
    )
    stat_rows = lax.all_gather(new_stat_right, "tensor", axis=1, tiled=True)
    power_right = jnp.dot(
        stat_rows,
        lax.all_gather(right_q, "shard", axis=0, tiled=True),
        precision=highest,
        preferred_element_type=jnp.float32,
    )
    power_left = jnp.dot(
        new_stat_left, left_q_all, precision=highest, preferred_element_type=jnp.float32
    )
    local_left = jnp.sum(power_left * power_left)
    local_right = jnp.sum(power_right * power_right)
    total_left = lax.psum(local_left, "shard")
    total_right = lax.psum(local_right, ("shard", "tensor"))
    iterate_left = power_left * (math.sqrt(D) / (4.0 * jnp.sqrt(total_left)))
    for iteration in range(NS_STEPS):
        partial_gram = jnp.dot(
            iterate_left.T, iterate_left, precision=highest, preferred_element_type=jnp.float32
        )
        gram_left = lax.psum(partial_gram.astype(jnp.bfloat16), "shard").astype(jnp.float32)
        iterate_left = 1.5 * iterate_left - 0.5 * jnp.dot(
            iterate_left, gram_left, precision=highest, preferred_element_type=jnp.float32
        )
    iterate_right = power_right * (math.sqrt(FF) / (4.0 * jnp.sqrt(total_right)))
    row_ids = shard_pos * rows_right + lax.broadcasted_iota(jnp.int32, (rows_right, cols_right), 0)
    col_ids = tensor_pos * cols_right + lax.broadcasted_iota(jnp.int32, (rows_right, cols_right), 1)
    identity_tile = (row_ids == col_ids).astype(jnp.float32)
    for iteration in range(NS_STEPS):
        rounded_iterate = iterate_right.astype(jnp.bfloat16)
        iterate_rows = lax.all_gather(rounded_iterate, "tensor", axis=1, tiled=True)
        gram_right = lax.psum_scatter(
            jnp.dot(iterate_rows.T, rounded_iterate, preferred_element_type=jnp.float32).astype(
                jnp.bfloat16
            ),
            "shard",
            scatter_dimension=0,
            tiled=True,
        ).astype(jnp.float32)
        mixing = (1.5 * identity_tile - 0.5 * gram_right).astype(jnp.bfloat16)
        iterate_right = jnp.dot(
            iterate_rows,
            lax.all_gather(mixing, "shard", axis=0, tiled=True),
            preferred_element_type=jnp.float32,
        )
    return (
        update,
        new_moment_one,
        new_moment_two,
        new_stat_left,
        new_stat_right,
        iterate_left * math.sqrt(D),
        iterate_right * math.sqrt(FF),
    )


BF = jnp.bfloat16
F32 = jnp.float32
AXES = ("shard", "tensor")
PATTERN = (4, 2, 2, 2)


def dot_nn(a, b):
    return jnp.dot(a, b, preferred_element_type=F32)


def dot_nt(a, b):
    return lax.dot_general(a, b, (((1,), (1,)), ((), ())), preferred_element_type=F32)


def dot_tn(a, b):
    return lax.dot_general(a, b, (((0,), (0,)), ((), ())), preferred_element_type=F32)


def pairs(move):
    nz, nx, ny, nc = PATTERN
    out = []
    for z in range(nz):
        for x in range(nx):
            for y in range(ny):
                for c in range(nc):
                    to = move(z, x, y, c)
                    if 0 <= to[0] < nz:
                        source = ((z * nx + x) * ny + y) * nc + c
                        target = ((to[0] * nx + to[1]) * ny + to[2]) * nc + to[3]
                        out.append((source, target))
    return out


def swap_x(a):
    return lax.ppermute(a, AXES, pairs(lambda z, x, y, c: (z, 1 - x, y, c)))


def swap_y(a):
    return lax.ppermute(a, AXES, pairs(lambda z, x, y, c: (z, x, 1 - y, c)))


def swap_core(a):
    return lax.ppermute(a, AXES, pairs(lambda z, x, y, c: (z, x, y, 1 - c)))


def send_up(a):
    return lax.ppermute(a, AXES, pairs(lambda z, x, y, c: (z + 1, x, y, c)))


def send_down(a):
    return lax.ppermute(a, AXES, pairs(lambda z, x, y, c: (z - 1, x, y, c)))


def turn_over(a, straight):
    crossed = pairs(lambda z, x, y, c: (z if x != c else -1, 1 - x, y, 1 - c))
    return jnp.where(straight, a, lax.ppermute(a, AXES, crossed))


def stage(*parts):
    return lax.optimization_barrier(parts)


def near_of(z, up, down):
    return jnp.where(z % 2 == 0, down, up)


def mid_of(z, up1, down1, up2, down2):
    return jnp.where(z == 0, down2, jnp.where(z == 1, down1, jnp.where(z == 2, up1, up2)))


def far_of(z, up2, down2, up3, down3):
    return jnp.where(z == 0, down3, jnp.where(z == 1, down2, jnp.where(z == 2, up2, up3)))


def in_order(z, own, near, mid, far):
    places = (z, z + 1 - 2 * (z % 2), jnp.where(z < 2, 2, 1), jnp.where(z < 2, 3, 0))
    whole = jnp.zeros((4,) + own.shape, own.dtype)
    for block, place in zip((own, near, mid, far), places):
        whole = lax.dynamic_update_slice(whole, block[None], (place,) + (0,) * own.ndim)
    return whole


def along_z(z, own, steps):
    (up1, down1), (up2, down2), (up3, down3) = steps
    return in_order(
        z,
        own,
        near_of(z, up1, down1),
        mid_of(z, up1, down1, up2, down2),
        far_of(z, up2, down2, up3, down3),
    )


def put(whole, part, *start):
    return lax.dynamic_update_slice(whole, part, start)


def interleave(core, mine, theirs):
    rows, cols = mine.shape[1:]
    whole = jnp.zeros((4, 2, rows, cols), mine.dtype)
    whole = put(whole, mine[:, None], 0, core, 0, 0)
    whole = put(whole, theirs[:, None], 0, 1 - core, 0, 0)
    return whole.reshape(8 * rows, cols)


def pass_kernel(turn, scale_ref, *refs):
    slabs = refs[:8]
    if turn == 0:
        rows_ref, out_ref, square_ref, whole, inner, held, sums, sems = refs[8:]
    elif turn == 3:
        rows_ref, first_ref, out_ref, whole, inner, held, sems = refs[8:]
    else:
        rows_ref, out_ref, whole, inner, held, sems = refs[8:]
    size = whole.shape[0]
    tall = size // 4
    half = size // 8

    def copy(k):
        return pltpu.make_async_copy(
            slabs[k], whole.at[pl.ds(k * half, half), :], sems.at[k]
        )

    for k in range(8):
        copy(k).start()
    held[...] = rows_ref[...].astype(BF)
    if turn == 0:
        sums[...] = jnp.zeros_like(sums)

    def towards(j, carry):
        for k in range(4):

            @pl.when(j == k)
            def _():
                copy(2 * k).wait()
                copy(2 * k + 1).wait()

        span = pl.ds(pl.multiple_of(j * tall, tall), tall)
        inner[:, span] = dot_nt(held[...], whole[span, :]).astype(BF)
        if turn == 0:
            for part in range(4):
                cols = slice(part * tall, (part + 1) * tall)

                def add(i, total):
                    start = pl.multiple_of(j * tall + i * 16, 16)
                    block = whole[pl.ds(start, 16), cols].astype(F32)
                    return total + block * block

                zero = jnp.zeros((16, tall), F32)
                sums[...] += lax.fori_loop(0, tall // 16, add, zero)
        return carry

    lax.fori_loop(0, 4, towards, 0)
    if turn == 0:
        square = scale_ref[0] / jnp.sum(sums[...])
        square_ref[0] = square
    else:
        square = scale_ref[0]

    def back(j, carry):
        span = pl.ds(pl.multiple_of(j * tall, tall), tall)
        moved = square * dot_nn(inner[...], whole[:, span])
        if turn == 1:
            out_ref[:, span] = moved
        else:
            value = 1.5 * rows_ref[:, span].astype(F32) - 0.5 * moved
            if turn == 3:
                value = scale_ref[1] * (1.5 * first_ref[:, span] - 0.5 * value)
            out_ref[:, span] = value
        return carry

    lax.fori_loop(0, 2 if turn == 3 else 4, back, 0)


def refresh_pass(turn, scales, slabs, *rows):
    count, size = rows[0].shape
    in_vmem = pl.BlockSpec(memory_space=pltpu.VMEM)
    in_smem = pl.BlockSpec(memory_space=pltpu.SMEM)
    shapes = [jax.ShapeDtypeStruct((count, size // 2 if turn == 3 else size), F32)]
    scratch = [
        pltpu.VMEM((size, size), BF),
        pltpu.VMEM((count, size), BF),
        pltpu.VMEM((count, size), BF),
    ]
    if turn == 0:
        shapes.append(jax.ShapeDtypeStruct((1,), F32))
        scratch.append(pltpu.VMEM((16, size // 4), F32))
    return pl.pallas_call(
        functools.partial(pass_kernel, turn),
        out_shape=shapes,
        in_specs=[in_smem] + [pl.BlockSpec(memory_space=pl.ANY)] * 8 + [in_vmem] * len(rows),
        out_specs=[in_vmem, in_smem][: len(shapes)],
        scratch_shapes=scratch + [pltpu.SemaphoreType.DMA((8,))],
        compiler_params=pltpu.CompilerParams(vmem_limit_bytes=40 * 2**20),
        cost_estimate=pl.CostEstimate(
            flops=4 * count * size * size, bytes_accessed=2 * size * size, transcendentals=0
        ),
    )(scales, *slabs, *rows)


def local_pattern(gradient, moment_one, moment_two, stat_left, stat_right, basis_left, basis_right):
    rows_left = gradient.shape[0]
    rows_right = stat_right.shape[0]
    cols_right = stat_right.shape[1]
    shard_pos = lax.axis_index("shard")
    tensor_pos = lax.axis_index("tensor")
    z, x = shard_pos // 2, shard_pos % 2
    y, core = tensor_pos // 2, tensor_pos % 2
    straight = x == core
    half = rows_right // 2

    left_b = (basis_left / math.sqrt(D)).astype(BF)
    right_b = (basis_right / math.sqrt(FF)).astype(BF)
    stat_b = stat_right.astype(BF)
    part_left = rows_left // 2
    small = jnp.concatenate(
        [gradient, lax.dynamic_slice_in_dim(left_b, y * part_left, part_left, 0)]
    )
    rows_small = small.shape[0]

    turned, small_u1, small_d1 = stage(
        turn_over(right_b, straight), send_up(small), send_down(small)
    )
    both_u, both_d, stat_x, stat_y = stage(
        send_up(jnp.concatenate([turned, small_u1])),
        send_down(jnp.concatenate([turned, small_d1])),
        swap_x(stat_b),
        swap_y(stat_b),
    )
    turned_u1, small_u2 = both_u[:rows_right], both_u[rows_right:]
    turned_d1, small_d2 = both_d[:rows_right], both_d[rows_right:]
    both_u, both_d, stat_hi, stat_lo = stage(
        send_up(both_u), send_down(both_d), swap_x(stat_y[half:]), swap_y(stat_x[:half])
    )
    turned_u2, small_u3 = both_u[:rows_right], both_u[rows_right:]
    turned_d2, small_d3 = both_d[:rows_right], both_d[rows_right:]
    small_z = along_z(
        z, small, [(small_u1, small_d1), (small_u2, small_d2), (small_u3, small_d3)]
    ).reshape(4 * rows_small, cols_right)
    stat_xy = jnp.concatenate([stat_lo, stat_hi])
    stat_keep = [jnp.where(straight, stat_b, stat_x), jnp.where(straight, stat_y, stat_xy)]
    stat_send = [jnp.where(straight, stat_x, stat_b), jnp.where(straight, stat_xy, stat_y)]
    turned_u3, turned_d3, small_x, small_y, stat_got = stage(
        send_up(turned_u2),
        send_down(turned_d2),
        swap_x(small_z),
        swap_y(small_z),
        swap_core(jnp.concatenate(stat_send)),
    )
    turned_z = along_z(
        z,
        turned,
        [(turned_u1, turned_d1), (turned_u2, turned_d2), (turned_u3, turned_d3)],
    )
    stat_rows = jnp.zeros((rows_right, 4 * cols_right), BF)
    stat_rows = put(stat_rows, stat_keep[0], 0, (2 * y + core) * cols_right)
    stat_rows = put(stat_rows, stat_keep[1], 0, (2 - 2 * y + core) * cols_right)
    stat_rows = put(stat_rows, stat_got[:rows_right], 0, (2 * y + 1 - core) * cols_right)
    stat_rows = put(stat_rows, stat_got[rows_right:], 0, (3 - 2 * y - core) * cols_right)
    some = 2 * rows_small
    small_hi, small_lo, turned_got = stage(
        swap_x(small_y[some:]), swap_y(small_x[:some]), swap_core(turned_z)
    )
    right_cols = interleave(core, turned_z, turned_got)
    grad_core = jnp.zeros((4, 2, rows_left, 2 * cols_right), BF)
    left_all = jnp.zeros((4, 2, 2, part_left, cols_right), BF)
    small_xy = jnp.concatenate([small_lo, small_hi])
    for block, at_x, at_y in (
        (small_z, x, y),
        (small_x, 1 - x, y),
        (small_y, x, 1 - y),
        (small_xy, 1 - x, 1 - y),
    ):
        block = block.reshape(4, 1, rows_small, cols_right)
        grad_core = put(grad_core, block[:, :, :rows_left], 0, at_x, 0, at_y * cols_right)
        left_all = put(left_all, block[:, :, None, rows_left:], 0, at_x, at_y, 0, 0)
    grad_core = grad_core.reshape(8 * rows_left, 2 * cols_right)
    left_all = left_all.reshape(8 * rows_left, cols_right)
    (grad_other,) = stage(swap_core(grad_core))
    grad_whole = jnp.zeros((8 * rows_left, 4 * cols_right), BF)
    for k in range(2):
        cols = slice(k * cols_right, (k + 1) * cols_right)
        grad_whole = put(grad_whole, grad_core[:, cols], 0, (2 * k + core) * cols_right)
        grad_whole = put(grad_whole, grad_other[:, cols], 0, (2 * k + 1 - core) * cols_right)

    share = (1.0 - beta_stat) / D
    picked = lax.dynamic_slice_in_dim(grad_whole, (2 * z + core) * rows_right, rows_right, 1)
    carried = dot_nn(grad_whole, right_cols).astype(BF)
    power = beta_stat * dot_nn(stat_rows, right_cols) + share * dot_tn(picked, carried)
    power = power.astype(BF)

    own_cols = lax.dynamic_slice_in_dim(grad_whole, shard_pos * rows_right, rows_right, 1)
    own_grad = lax.dynamic_slice_in_dim(grad_whole, tensor_pos * cols_right, cols_right, 1)
    new_stat_right = blend_stat(stat_right, dot_tn(own_cols, own_grad), D)
    left_cols = lax.dynamic_slice_in_dim(left_all, (2 * z + core) * rows_left, rows_left, 1)
    rotated = dot_tn(left_cols, carried).astype(BF)
    grad_rows = lax.dynamic_slice_in_dim(grad_whole, shard_pos * rows_left, rows_left, 0)
    new_stat_left = blend_stat(stat_left, dot_nt(grad_rows, grad_whole), FF)
    power_left = dot_nn(new_stat_left.astype(BF), left_all)
    power_left_b = power_left.astype(BF)

    power_x, power_y, power_u1, power_d1, extra = stage(
        swap_x(power),
        swap_y(power),
        send_up(power),
        send_down(power),
        turn_over(jnp.concatenate([rotated, power_left_b]), straight),
    )
    near = near_of(z, power_u1, power_d1)
    rotated, left_t = extra[:rows_left], extra[rows_left:]
    new_moment_one, new_moment_two, direction = adam_moments(
        rotated.astype(F32), moment_one, moment_two
    )
    got_x, got_y, got_u, got_d, direction_t = stage(
        swap_x(jnp.concatenate([power_y[half:], near])),
        swap_y(jnp.concatenate([power_x[:half], near])),
        send_up(jnp.concatenate([power_u1, left_t])),
        send_down(jnp.concatenate([power_d1, left_t])),
        turn_over(direction, straight),
    )
    slab0 = jnp.concatenate(
        [power, power_x, power_y, jnp.concatenate([got_y[:half], got_x[:half]])], axis=1
    )
    near_x, near_y = got_x[half:], got_y[half:]
    power_u2, left_u1 = got_u[:rows_right], got_u[rows_right:]
    power_d2, left_d1 = got_d[:rows_right], got_d[rows_right:]
    mid = mid_of(z, power_u1, power_d1, power_u2, power_d2)
    got_x, got_y, got_u, got_d, slab0_other = stage(
        swap_x(jnp.concatenate([near_y[half:], mid])),
        swap_y(jnp.concatenate([near_x[:half], mid])),
        send_up(jnp.concatenate([power_u2, left_u1, direction_t])),
        send_down(jnp.concatenate([power_d2, left_d1, direction_t])),
        swap_core(slab0),
    )
    slab1 = jnp.concatenate(
        [near, near_x, near_y, jnp.concatenate([got_y[:half], got_x[:half]])], axis=1
    )
    mid_x, mid_y = got_x[half:], got_y[half:]
    power_u3, rest_u = got_u[:rows_right], got_u[rows_right:]
    power_d3, rest_d = got_d[:rows_right], got_d[rows_right:]
    left_u2, direction_u1 = rest_u[:rows_left], rest_u[rows_left:]
    left_d2, direction_d1 = rest_d[:rows_left], rest_d[rows_left:]
    far = far_of(z, power_u2, power_d2, power_u3, power_d3)
    got_x, got_y, rest_u, rest_d, slab1_other = stage(
        swap_x(jnp.concatenate([mid_y[half:], far])),
        swap_y(jnp.concatenate([mid_x[:half], far])),
        send_up(rest_u),
        send_down(rest_d),
        swap_core(slab1),
    )
    slab2 = jnp.concatenate(
        [mid, mid_x, mid_y, jnp.concatenate([got_y[:half], got_x[:half]])], axis=1
    )
    far_x, far_y = got_x[half:], got_y[half:]
    left_u3, direction_u2 = rest_u[:rows_left], rest_u[rows_left:]
    left_d3, direction_d2 = rest_d[:rows_left], rest_d[rows_left:]
    left_z = along_z(z, left_t, [(left_u1, left_d1), (left_u2, left_d2), (left_u3, left_d3)])
    got_x, got_y, direction_u3, direction_d3, slab2_other, left_other = stage(
        swap_x(far_y[half:]),
        swap_y(far_x[:half]),
        send_up(direction_u2),
        send_down(direction_d2),
        swap_core(slab2),
        swap_core(left_z),
    )
    slab3 = jnp.concatenate([far, far_x, far_y, jnp.concatenate([got_y, got_x])], axis=1)
    direction_z = along_z(
        z,
        direction_t,
        [
            (direction_u1, direction_d1),
            (direction_u2, direction_d2),
            (direction_u3, direction_d3),
        ],
    )
    slab3_other, direction_other = stage(swap_core(slab3), swap_core(direction_z))

    slabs = (slab0, slab0_other, slab1, slab1_other, slab2, slab2_other, slab3, slab3_other)
    own = lax.dynamic_slice_in_dim(jnp.where(straight, slab0, slab0_other), core * half, half, 0)
    first, square_right = refresh_pass(0, jnp.full((1,), FF / 16.0, F32), slabs, own)
    (second,) = refresh_pass(1, square_right, slabs, first)
    (third,) = refresh_pass(2, square_right, slabs, second)
    scales = jnp.concatenate([square_right, math.sqrt(FF) * jnp.sqrt(square_right)])
    (fresh,) = refresh_pass(3, scales, slabs, third, first)
    ahead, behind = fresh[:, :cols_right], fresh[:, cols_right:]
    mine = jnp.where(straight, ahead, behind)
    theirs = swap_core(jnp.where(straight, behind, ahead))
    new_basis_right = jnp.where(
        core == 0, jnp.concatenate([mine, theirs]), jnp.concatenate([theirs, mine])
    )

    direction_cols = interleave(core, direction_z, direction_other)
    left_rows = lax.dynamic_slice_in_dim(left_all, (2 * z + core) * rows_left, rows_left, 0)
    back_half = dot_nn(left_rows, direction_cols).astype(BF)
    back_terms = dot_nt(back_half, right_cols)
    width = 2 * cols_right
    away = lax.dynamic_slice_in_dim(back_terms, (1 - y) * width, width, 1).astype(BF)
    kept = lax.dynamic_slice_in_dim(back_terms, y * width, width, 1)
    kept = kept + swap_y(away).astype(F32)
    away = lax.dynamic_slice_in_dim(kept, (1 - x) * cols_right, cols_right, 1).astype(BF)
    kept = lax.dynamic_slice_in_dim(kept, x * cols_right, cols_right, 1)
    update = turn_over((kept + swap_x(away).astype(F32)).astype(BF), straight)

    power_all = interleave(core, left_z, left_other)
    square_left = D / (16.0 * jnp.sum(jnp.square(power_all.astype(F32))))
    keep = power_left
    value = power_left
    for turn in range(4):
        across = dot_nt(value.astype(BF), power_all).astype(BF)
        moved = square_left * dot_nn(across, power_all)
        value = moved if turn == 1 else 1.5 * value - 0.5 * moved
        if turn == 0:
            keep = value
    value = 1.5 * keep - 0.5 * value
    new_basis_left = value * (math.sqrt(D) * jnp.sqrt(square_left))
    return (
        update,
        new_moment_one,
        new_moment_two,
        new_stat_left,
        new_stat_right,
        new_basis_left,
        new_basis_right,
    )


def solution(mesh):
    nz, nx, ny, nc = PATTERN
    fits = (mesh.shape["shard"], mesh.shape["tensor"]) == (nz * nx, ny * nc)
    local = local_pattern if fits else local_general
    placed = (
        P("shard", "tensor"),
        P("shard", "tensor"),
        P("shard", "tensor"),
        P("shard", None),
        P("shard", "tensor"),
        P("shard", None),
        P("shard", "tensor"),
    )
    return jax.shard_map(
        local,
        mesh=mesh,
        in_specs=placed,
        out_specs=(
            P("shard", "tensor"),
            P("shard", "tensor"),
            P("shard", "tensor"),
            P("shard", None),
            P("shard", "tensor"),
            P("shard", None),
            P("shard", "tensor"),
        ),
        check_vma=False,
    )
```

```python
import functools
import math

import jax
import jax.numpy as jnp
from jax import lax
from jax.experimental import pallas as pl
from jax.experimental.pallas import tpu as pltpu
from jax.sharding import PartitionSpec as P

D = 768
FF = 3072
NS_STEPS = 2


beta_one = 0.95
beta_two = 0.95
beta_stat = 0.95
correction = 1.0 - 0.95**10
adam_eps = 1e-08
highest = lax.Precision.HIGHEST


def blend_stat(previous, product, divisor):
    return beta_stat * previous + (1.0 - beta_stat) * (product / divisor)


def adam_moments(rotated, moment_one, moment_two):
    first_moment = beta_one * moment_one + (1.0 - beta_one) * rotated
    second_moment = beta_two * moment_two + (1.0 - beta_two) * (rotated * rotated)
    direction = (
        first_moment / correction / (jnp.sqrt(second_moment / correction) + adam_eps)
    ).astype(jnp.bfloat16)
    return (first_moment, second_moment, direction)


def local_general(gradient, moment_one, moment_two, stat_left, stat_right, basis_left, basis_right):
    rows_left = gradient.shape[0]
    rows_right = stat_right.shape[0]
    cols_right = stat_right.shape[1]
    shard_pos = lax.axis_index("shard")
    tensor_pos = lax.axis_index("tensor")
    row_start = shard_pos * rows_left
    grad_cols = lax.all_gather(gradient, "shard", axis=0, tiled=True)
    left_terms = jnp.dot(gradient, grad_cols.T, preferred_element_type=jnp.float32)
    gram_rows = lax.psum(left_terms.astype(jnp.bfloat16), "tensor").astype(jnp.float32)
    new_stat_left = blend_stat(stat_left, gram_rows, FF)
    grad_whole = lax.all_gather(grad_cols, "tensor", axis=1, tiled=True)
    picked = lax.dynamic_slice_in_dim(grad_whole, shard_pos * rows_right, rows_right, 1)
    gram_block = jnp.dot(picked.T, grad_cols, preferred_element_type=jnp.float32)
    new_stat_right = blend_stat(stat_right, gram_block, D)
    basis_all = lax.all_gather(basis_left, "shard", axis=0, tiled=True)
    left_q_all = basis_all / math.sqrt(D)
    left_qb_all = left_q_all.astype(jnp.bfloat16)
    left_qb_own = lax.dynamic_slice_in_dim(left_qb_all, row_start, rows_left, 0)
    left_cols_own = lax.dynamic_slice_in_dim(left_qb_all, row_start, rows_left, 1)
    half_rotated = jnp.dot(left_cols_own.T, grad_cols, preferred_element_type=jnp.float32).astype(
        jnp.bfloat16
    )
    right_q = basis_right / math.sqrt(FF)
    right_qb = right_q.astype(jnp.bfloat16)
    right_cols_b = lax.all_gather(right_qb, "shard", axis=0, tiled=True)
    half_full = lax.all_gather(half_rotated, "tensor", axis=1, tiled=True)
    rotated = jnp.dot(half_full, right_cols_b, preferred_element_type=jnp.float32)
    new_moment_one, new_moment_two, direction = adam_moments(rotated, moment_one, moment_two)
    back_half = jnp.dot(
        left_qb_own,
        lax.all_gather(direction, "shard", axis=0, tiled=True),
        preferred_element_type=jnp.float32,
    ).astype(jnp.bfloat16)
    back_terms = jnp.dot(back_half, right_cols_b.T, preferred_element_type=jnp.float32)
    update = lax.psum_scatter(back_terms, "tensor", scatter_dimension=1, tiled=True).astype(
        jnp.bfloat16
    )
    stat_rows = lax.all_gather(new_stat_right, "tensor", axis=1, tiled=True)
    power_right = jnp.dot(
        stat_rows,
        lax.all_gather(right_q, "shard", axis=0, tiled=True),
        precision=highest,
        preferred_element_type=jnp.float32,
    )
    power_left = jnp.dot(
        new_stat_left, left_q_all, precision=highest, preferred_element_type=jnp.float32
    )
    local_left = jnp.sum(power_left * power_left)
    local_right = jnp.sum(power_right * power_right)
    total_left = lax.psum(local_left, "shard")
    total_right = lax.psum(local_right, ("shard", "tensor"))
    iterate_left = power_left * (math.sqrt(D) / (4.0 * jnp.sqrt(total_left)))
    for iteration in range(NS_STEPS):
        partial_gram = jnp.dot(
            iterate_left.T, iterate_left, precision=highest, preferred_element_type=jnp.float32
        )
        gram_left = lax.psum(partial_gram.astype(jnp.bfloat16), "shard").astype(jnp.float32)
        iterate_left = 1.5 * iterate_left - 0.5 * jnp.dot(
            iterate_left, gram_left, precision=highest, preferred_element_type=jnp.float32
        )
    iterate_right = power_right * (math.sqrt(FF) / (4.0 * jnp.sqrt(total_right)))
    row_ids = shard_pos * rows_right + lax.broadcasted_iota(jnp.int32, (rows_right, cols_right), 0)
    col_ids = tensor_pos * cols_right + lax.broadcasted_iota(jnp.int32, (rows_right, cols_right), 1)
    identity_tile = (row_ids == col_ids).astype(jnp.float32)
    for iteration in range(NS_STEPS):
        rounded_iterate = iterate_right.astype(jnp.bfloat16)
        iterate_rows = lax.all_gather(rounded_iterate, "tensor", axis=1, tiled=True)
        gram_right = lax.psum_scatter(
            jnp.dot(iterate_rows.T, rounded_iterate, preferred_element_type=jnp.float32).astype(
                jnp.bfloat16
            ),
            "shard",
            scatter_dimension=0,
            tiled=True,
        ).astype(jnp.float32)
        mixing = (1.5 * identity_tile - 0.5 * gram_right).astype(jnp.bfloat16)
        iterate_right = jnp.dot(
            iterate_rows,
            lax.all_gather(mixing, "shard", axis=0, tiled=True),
            preferred_element_type=jnp.float32,
        )
    return (
        update,
        new_moment_one,
        new_moment_two,
        new_stat_left,
        new_stat_right,
        iterate_left * math.sqrt(D),
        iterate_right * math.sqrt(FF),
    )


BF = jnp.bfloat16
F32 = jnp.float32
AXES = ("shard", "tensor")
PATTERN = (4, 2, 2, 2)


def dot_nn(a, b):
    return jnp.dot(a, b, preferred_element_type=F32)


def dot_nt(a, b):
    return lax.dot_general(a, b, (((1,), (1,)), ((), ())), preferred_element_type=F32)


def dot_tn(a, b):
    return lax.dot_general(a, b, (((0,), (0,)), ((), ())), preferred_element_type=F32)


def pairs(move):
    nz, nx, ny, nc = PATTERN
    out = []
    for z in range(nz):
        for x in range(nx):
            for y in range(ny):
                for c in range(nc):
                    to = move(z, x, y, c)
                    if 0 <= to[0] < nz:
                        source = ((z * nx + x) * ny + y) * nc + c
                        target = ((to[0] * nx + to[1]) * ny + to[2]) * nc + to[3]
                        out.append((source, target))
    return out


def swap_x(a):
    return lax.ppermute(a, AXES, pairs(lambda z, x, y, c: (z, 1 - x, y, c)))


def swap_y(a):
    return lax.ppermute(a, AXES, pairs(lambda z, x, y, c: (z, x, 1 - y, c)))


def swap_core(a):
    return lax.ppermute(a, AXES, pairs(lambda z, x, y, c: (z, x, y, 1 - c)))


def swap_outer(a):
    return lax.ppermute(a, AXES, pairs(lambda z, x, y, c: (z + 1 - 2 * (z % 2), x, y, c)))


def swap_inner(a):
    return lax.ppermute(a, AXES, pairs(lambda z, x, y, c: (3 - z if 0 < z < 3 else -1, x, y, c)))


def turn_over(a, straight):
    crossed = pairs(lambda z, x, y, c: (z if x != c else -1, 1 - x, y, 1 - c))
    return jnp.where(straight, a, lax.ppermute(a, AXES, crossed))


def stage(*parts):
    return lax.optimization_barrier(parts)


def places_z(z):
    return z + 1 - 2 * (z % 2), jnp.where(z < 2, 2, 1), jnp.where(z < 2, 3, 0)


def in_order(z, own, near, mid, far):
    whole = jnp.zeros((4,) + own.shape, own.dtype)
    for block, place in zip((own, near, mid, far), (z,) + places_z(z)):
        whole = lax.dynamic_update_slice(whole, block[None], (place,) + (0,) * own.ndim)
    return whole


def ordered_pair(ahead, first, second):
    both = jnp.concatenate([first[None], second[None]])
    return jnp.where(ahead, both, jnp.concatenate([second[None], first[None]]))


def put(whole, part, *start):
    return lax.dynamic_update_slice(whole, part, start)


def interleave(core, mine, theirs):
    rows, cols = mine.shape[1:]
    whole = jnp.zeros((4, 2, rows, cols), mine.dtype)
    whole = put(whole, mine[:, None], 0, core, 0, 0)
    whole = put(whole, theirs[:, None], 0, 1 - core, 0, 0)
    return whole.reshape(8 * rows, cols)


def refresh_kernel(part, scale_ref, place_ref, *refs):
    slabs = refs[:8]
    if part == 0:
        first_ref, second_ref, whole, inner, held, sems = refs[8:]
    else:
        second_ref, first_ref, out_ref, whole, inner, held, third, sems = refs[8:]
    size = whole.shape[0]
    count = held.shape[0]
    tall = size // 4
    half = size // 8
    square = scale_ref[0]

    def copy(k, i):
        return pltpu.make_async_copy(
            slabs[k].at[pl.ds(i * half, half), :],
            whole.at[pl.ds(k * half, half), pl.ds(i * tall, tall)],
            sems.at[k, i],
        )

    def arrived(j):
        for k in (2 * j, 2 * j + 1):
            for i in range(4):
                copy(k, i).wait()

    def span_of(j):
        return pl.ds(pl.multiple_of(j * tall, tall), tall)

    def towards(fresh):
        def step(j, carry):
            if fresh:
                for k in range(1 - part, 4):
                    pl.when(j == k)(functools.partial(arrived, k))
            span = span_of(j)
            inner[:, span] = dot_nt(held[...], whole[span, :]).astype(BF)
            return carry

        lax.fori_loop(0, 4, step, 0)

    def back(chunks, use):
        def step(j, carry):
            use(j, span_of(j), square * dot_nn(inner[...], whole[:, span_of(j)]))
            return carry

        lax.fori_loop(0, chunks, step, 0)

    for k in range(8):
        for i in range(4):
            copy(k, i).start()
    if part == 0:
        arrived(0)
        held[...] = whole[pl.ds(pl.multiple_of(place_ref[0], 16), count), :]
        towards(True)

        def use_first(j, span, moved):
            value = 1.5 * held[:, span].astype(F32) - 0.5 * moved
            first_ref[:, span] = value
            held[:, span] = value.astype(BF)

        back(4, use_first)
        towards(False)

        def use_second(j, span, moved):
            second_ref[:, span] = moved

        back(4, use_second)
    else:
        held[...] = second_ref[...].astype(BF)
        towards(True)

        def use_third(j, span, moved):
            value = 1.5 * second_ref[:, span] - 0.5 * moved
            third[:, span] = value
            held[:, span] = value.astype(BF)

        back(4, use_third)
        towards(False)

        def use_last(j, span, moved):
            value = 1.5 * third[:, span] - 0.5 * moved
            value = scale_ref[1] * (1.5 * first_ref[:, span] - 0.5 * value)
            out_ref[jnp.where(place_ref[1] == 1, j, 1 - j)] = value

        back(2, use_last)


def refresh_part(part, scales, places, slabs, *rows):
    size = slabs[0].shape[0] * 2
    count = size // 16
    in_vmem = pl.BlockSpec(memory_space=pltpu.VMEM)
    in_smem = pl.BlockSpec(memory_space=pltpu.SMEM)
    state = jax.ShapeDtypeStruct((count, size), F32)
    scratch = [
        pltpu.VMEM((size, size), BF),
        pltpu.VMEM((count, size), BF),
        pltpu.VMEM((count, size), BF),
    ]
    if part == 0:
        shapes = [state, state]
    else:
        shapes = [jax.ShapeDtypeStruct((2, count, size // 4), F32)]
        scratch.append(pltpu.VMEM((count, size), F32))
    return pl.pallas_call(
        functools.partial(refresh_kernel, part),
        out_shape=shapes,
        in_specs=[in_smem] * 2 + [pl.BlockSpec(memory_space=pl.ANY)] * 8 + [in_vmem] * len(rows),
        out_specs=[in_vmem] * len(shapes),
        scratch_shapes=scratch + [pltpu.SemaphoreType.DMA((8, 4))],
        compiler_params=pltpu.CompilerParams(vmem_limit_bytes=36 * 2**20),
        cost_estimate=pl.CostEstimate(
            flops=8 * count * size * size, bytes_accessed=2 * size * size, transcendentals=0
        ),
    )(scales, places, *slabs, *rows)


def squares(tiles):
    return jnp.sum(jnp.square(tiles.astype(F32)))


def local_pattern(gradient, moment_one, moment_two, stat_left, stat_right, basis_left, basis_right):
    rows_left = gradient.shape[0]
    rows_right = stat_right.shape[0]
    cols_right = stat_right.shape[1]
    shard_pos = lax.axis_index("shard")
    tensor_pos = lax.axis_index("tensor")
    z, x = shard_pos // 2, shard_pos % 2
    y, core = tensor_pos // 2, tensor_pos % 2
    straight = x == core
    inner = (z == 1) | (z == 2)
    half = rows_right // 2

    left_b = (basis_left / math.sqrt(D)).astype(BF)
    right_b = (basis_right / math.sqrt(FF)).astype(BF)
    stat_b = stat_right.astype(BF)
    part_left = rows_left // 2
    small = jnp.concatenate(
        [gradient, lax.dynamic_slice_in_dim(left_b, y * part_left, part_left, 0)]
    )
    rows_small = small.shape[0]

    turned, small_o1, small_i1 = stage(
        turn_over(right_b, straight), swap_outer(small), swap_inner(small)
    )
    got_o, got_i, stat_x, stat_y = stage(
        swap_outer(jnp.concatenate([turned, small_i1])),
        swap_inner(jnp.concatenate([turned, small_o1])),
        swap_x(stat_b),
        swap_y(stat_b),
    )
    turned_o1, small_o2 = got_o[:rows_right], got_o[rows_right:]
    turned_i1, small_i2 = got_i[:rows_right], got_i[rows_right:]
    small_1 = ordered_pair(z % 2 == 0, small, small_o1).reshape(2 * rows_small, cols_right)
    got_o, turned_i2, got_x, got_y = stage(
        swap_outer(jnp.concatenate([turned_i1, small_i2])),
        swap_inner(turned_o1),
        swap_x(jnp.concatenate([stat_y[half:], small_1])),
        swap_y(jnp.concatenate([stat_x[:half], small_1])),
    )
    turned_o2, small_o3 = got_o[:rows_right], got_o[rows_right:]
    small_2 = ordered_pair(
        z < 2, jnp.where(inner, small_i1, small_o2), jnp.where(inner, small_i2, small_o3)
    ).reshape(2 * rows_small, cols_right)
    stat_xy = jnp.concatenate([got_y[:half], got_x[:half]])
    small_1x, small_1y = got_x[half:], got_y[half:]
    stat_keep = [jnp.where(straight, stat_b, stat_x), jnp.where(straight, stat_y, stat_xy)]
    stat_send = [jnp.where(straight, stat_x, stat_b), jnp.where(straight, stat_xy, stat_y)]
    turned_o3, got_x, got_y, stat_got = stage(
        swap_outer(turned_i2),
        swap_x(jnp.concatenate([small_1y[rows_small:], small_2])),
        swap_y(jnp.concatenate([small_1x[:rows_small], small_2])),
        swap_core(jnp.concatenate(stat_send)),
    )
    small_1xy = jnp.concatenate([got_y[:rows_small], got_x[:rows_small]])
    small_2x, small_2y = got_x[rows_small:], got_y[rows_small:]
    turned_z = in_order(
        z,
        turned,
        turned_o1,
        jnp.where(inner, turned_i1, turned_o2),
        jnp.where(inner, turned_i2, turned_o3),
    )
    stat_rows = jnp.zeros((rows_right, 4 * cols_right), BF)
    stat_rows = put(stat_rows, stat_keep[0], 0, (2 * y + core) * cols_right)
    stat_rows = put(stat_rows, stat_keep[1], 0, (2 - 2 * y + core) * cols_right)
    stat_rows = put(stat_rows, stat_got[:rows_right], 0, (2 * y + 1 - core) * cols_right)
    stat_rows = put(stat_rows, stat_got[rows_right:], 0, (3 - 2 * y - core) * cols_right)
    small_2hi, small_2lo, turned_got = stage(
        swap_x(small_2y[rows_small:]), swap_y(small_2x[:rows_small]), swap_core(turned_z)
    )
    right_cols = interleave(core, turned_z, turned_got)
    grad_core = jnp.zeros((4, 2, rows_left, 2 * cols_right), BF)
    left_all = jnp.zeros((4, 2, 2, part_left, cols_right), BF)
    small_2xy = jnp.concatenate([small_2lo, small_2hi])
    low = 2 * (z // 2)
    for block, at_z, at_x, at_y in (
        (small_1, low, x, y),
        (small_1x, low, 1 - x, y),
        (small_1y, low, x, 1 - y),
        (small_1xy, low, 1 - x, 1 - y),
        (small_2, 2 - low, x, y),
        (small_2x, 2 - low, 1 - x, y),
        (small_2y, 2 - low, x, 1 - y),
        (small_2xy, 2 - low, 1 - x, 1 - y),
    ):
        block = block.reshape(2, 1, rows_small, cols_right)
        grad_core = put(grad_core, block[:, :, :rows_left], at_z, at_x, 0, at_y * cols_right)
        left_all = put(left_all, block[:, :, None, rows_left:], at_z, at_x, at_y, 0, 0)
    grad_core = grad_core.reshape(8 * rows_left, 2 * cols_right)
    left_all = left_all.reshape(8 * rows_left, cols_right)

    grad_other = swap_core(grad_core)
    rows_core = lax.dynamic_slice_in_dim(
        right_cols.reshape(2, 2, cols_right, cols_right), core, 1, 1
    ).reshape(2 * cols_right, cols_right)
    carried = dot_nn(grad_core, rows_core)
    carried = (carried + swap_core(carried.astype(BF)).astype(F32)).astype(BF)
    grad_whole = jnp.zeros((8 * rows_left, 4 * cols_right), BF)
    for k in range(2):
        cols = slice(k * cols_right, (k + 1) * cols_right)
        grad_whole = put(grad_whole, grad_core[:, cols], 0, (2 * k + core) * cols_right)
        grad_whole = put(grad_whole, grad_other[:, cols], 0, (2 * k + 1 - core) * cols_right)
    share = (1.0 - beta_stat) / D
    picked = lax.dynamic_slice_in_dim(grad_whole, (2 * z + core) * rows_right, rows_right, 1)
    power = beta_stat * dot_nn(stat_rows, right_cols) + share * dot_tn(picked, carried)
    power = power.astype(BF)

    own_cols = lax.dynamic_slice_in_dim(grad_whole, shard_pos * rows_right, rows_right, 1)
    own_grad = lax.dynamic_slice_in_dim(grad_whole, tensor_pos * cols_right, cols_right, 1)
    new_stat_right = blend_stat(stat_right, dot_tn(own_cols, own_grad), D)
    left_cols = lax.dynamic_slice_in_dim(left_all, (2 * z + core) * rows_left, rows_left, 1)
    rotated = dot_tn(left_cols, carried).astype(BF)
    grad_rows = lax.dynamic_slice_in_dim(grad_whole, shard_pos * rows_left, rows_left, 0)
    new_stat_left = blend_stat(stat_left, dot_nt(grad_rows, grad_whole), FF)
    power_left = dot_nn(new_stat_left.astype(BF), left_all)
    power_left_b = power_left.astype(BF)

    power_x, power_y, near, power_i1, extra = stage(
        swap_x(power),
        swap_y(power),
        swap_outer(power),
        swap_inner(power),
        turn_over(jnp.concatenate([rotated, power_left_b]), straight),
    )
    rotated, left_t = extra[:rows_left], extra[rows_left:]
    new_moment_one, new_moment_two, direction = adam_moments(
        rotated.astype(F32), moment_one, moment_two
    )
    got_x, got_y, got_o, got_i, direction_t = stage(
        swap_x(jnp.concatenate([power_y[half:], near])),
        swap_y(jnp.concatenate([power_x[:half], near])),
        swap_outer(jnp.concatenate([power_i1, left_t])),
        swap_inner(jnp.concatenate([near, left_t])),
        turn_over(direction, straight),
    )
    slab0 = jnp.concatenate([power, power_x, power_y, got_y[:half], got_x[:half]])
    near_x, near_y = got_x[half:], got_y[half:]
    power_o2, left_o1 = got_o[:rows_right], got_o[rows_right:]
    power_i2, left_i1 = got_i[:rows_right], got_i[rows_right:]
    mid = jnp.where(inner, power_i1, power_o2)
    got_x, got_y, got_o, got_i, slab0_other = stage(
        swap_x(jnp.concatenate([near_y[half:], mid])),
        swap_y(jnp.concatenate([near_x[:half], mid])),
        swap_outer(jnp.concatenate([power_i2, left_i1, direction_t])),
        swap_inner(jnp.concatenate([left_o1, direction_t])),
        swap_core(slab0),
    )
    slab1 = jnp.concatenate([near, near_x, near_y, got_y[:half], got_x[:half]])
    mid_x, mid_y = got_x[half:], got_y[half:]
    power_o3, left_o2, direction_o1 = (
        got_o[:rows_right],
        got_o[rows_right:-rows_left],
        got_o[-rows_left:],
    )
    left_i2, direction_i1 = got_i[:rows_left], got_i[rows_left:]
    far = jnp.where(inner, power_i2, power_o3)
    got_x, got_y, got_o, direction_i2, slab1_other = stage(
        swap_x(jnp.concatenate([mid_y[half:], far])),
        swap_y(jnp.concatenate([mid_x[:half], far])),
        swap_outer(jnp.concatenate([left_i2, direction_i1])),
        swap_inner(direction_o1),
        swap_core(slab1),
    )
    slab2 = jnp.concatenate([mid, mid_x, mid_y, got_y[:half], got_x[:half]])
    far_x, far_y = got_x[half:], got_y[half:]
    left_o3, direction_o2 = got_o[:rows_left], got_o[rows_left:]
    left_z = in_order(
        z,
        left_t,
        left_o1,
        jnp.where(inner, left_i1, left_o2),
        jnp.where(inner, left_i2, left_o3),
    )
    got_x, got_y, direction_o3, slab2_other, left_other = stage(
        swap_x(far_y[half:]),
        swap_y(far_x[:half]),
        swap_outer(direction_i2),
        swap_core(slab2),
        swap_core(left_z),
    )
    slab3 = jnp.concatenate([far, far_x, far_y, got_y, got_x])
    direction_z = in_order(
        z,
        direction_t,
        direction_o1,
        jnp.where(inner, direction_i1, direction_o2),
        jnp.where(inner, direction_i2, direction_o3),
    )
    sum_core = squares(slab0) + squares(slab1) + squares(slab2) + squares(slab3)
    sum_core = jnp.full((8, 128), sum_core)
    slab3_other, direction_other, sum_other = stage(
        swap_core(slab3), swap_core(direction_z), swap_core(sum_core)
    )
    square_right = FF / (16.0 * (sum_core[0, 0] + sum_other[0, 0]))

    slabs = (slab0, slab0_other, slab1, slab1_other, slab2, slab2_other, slab3, slab3_other)
    scales = jnp.stack([square_right, math.sqrt(FF) * jnp.sqrt(square_right)])
    places = jnp.stack(
        [jnp.where(straight, 0, rows_right) + core * half, straight.astype(jnp.int32)]
    )
    first, second = refresh_part(0, scales, places, slabs)
    (fresh,) = refresh_part(1, scales, places, slabs, second, first)
    theirs = swap_core(fresh[1])
    new_basis_right = jnp.zeros((rows_right, cols_right), F32)
    new_basis_right = put(new_basis_right, fresh[0], core * half, 0)
    new_basis_right = put(new_basis_right, theirs, (1 - core) * half, 0)

    direction_cols = interleave(core, direction_z, direction_other)
    left_rows = lax.dynamic_slice_in_dim(left_all, (2 * z + core) * rows_left, rows_left, 0)
    back_half = dot_nn(left_rows, direction_cols).astype(BF)
    back_terms = dot_nt(back_half, right_cols)
    width = 2 * cols_right
    away = lax.dynamic_slice_in_dim(back_terms, (1 - y) * width, width, 1).astype(BF)
    kept = lax.dynamic_slice_in_dim(back_terms, y * width, width, 1)
    kept = kept + swap_y(away).astype(F32)
    away = lax.dynamic_slice_in_dim(kept, (1 - x) * cols_right, cols_right, 1).astype(BF)
    kept = lax.dynamic_slice_in_dim(kept, x * cols_right, cols_right, 1)
    update = turn_over((kept + swap_x(away).astype(F32)).astype(BF), straight)

    power_all = interleave(core, left_z, left_other)
    square_left = D / (16.0 * squares(power_all))
    keep = power_left
    value = power_left
    for turn in range(4):
        across = dot_nt(value.astype(BF), power_all).astype(BF)
        moved = square_left * dot_nn(across, power_all)
        value = moved if turn == 1 else 1.5 * value - 0.5 * moved
        if turn == 0:
            keep = value
    value = 1.5 * keep - 0.5 * value
    new_basis_left = value * (math.sqrt(D) * jnp.sqrt(square_left))
    return (
        update,
        new_moment_one,
        new_moment_two,
        new_stat_left,
        new_stat_right,
        new_basis_left,
        new_basis_right,
    )


def solution(mesh):
    nz, nx, ny, nc = PATTERN
    fits = (mesh.shape["shard"], mesh.shape["tensor"]) == (nz * nx, ny * nc)
    local = local_pattern if fits else local_general
    placed = (
        P("shard", "tensor"),
        P("shard", "tensor"),
        P("shard", "tensor"),
        P("shard", None),
        P("shard", "tensor"),
        P("shard", None),
        P("shard", "tensor"),
    )
    return jax.shard_map(
        local,
        mesh=mesh,
        in_specs=placed,
        out_specs=(
            P("shard", "tensor"),
            P("shard", "tensor"),
            P("shard", "tensor"),
            P("shard", None),
            P("shard", "tensor"),
            P("shard", None),
            P("shard", "tensor"),
        ),
        check_vma=False,
    )
```

```python
import functools
import math

import jax
import jax.numpy as jnp
from jax import lax
from jax.experimental import pallas as pl
from jax.experimental.pallas import tpu as pltpu
from jax.sharding import PartitionSpec as P

D = 768
FF = 3072
NS_STEPS = 2


beta_one = 0.95
beta_two = 0.95
beta_stat = 0.95
correction = 1.0 - 0.95**10
adam_eps = 1e-08
highest = lax.Precision.HIGHEST


def blend_stat(previous, product, divisor):
    return beta_stat * previous + (1.0 - beta_stat) * (product / divisor)


def adam_moments(rotated, moment_one, moment_two):
    first_moment = beta_one * moment_one + (1.0 - beta_one) * rotated
    second_moment = beta_two * moment_two + (1.0 - beta_two) * (rotated * rotated)
    direction = (
        first_moment / correction / (jnp.sqrt(second_moment / correction) + adam_eps)
    ).astype(jnp.bfloat16)
    return (first_moment, second_moment, direction)


def local_general(gradient, moment_one, moment_two, stat_left, stat_right, basis_left, basis_right):
    rows_left = gradient.shape[0]
    rows_right = stat_right.shape[0]
    cols_right = stat_right.shape[1]
    shard_pos = lax.axis_index("shard")
    tensor_pos = lax.axis_index("tensor")
    row_start = shard_pos * rows_left
    grad_cols = lax.all_gather(gradient, "shard", axis=0, tiled=True)
    left_terms = jnp.dot(gradient, grad_cols.T, preferred_element_type=jnp.float32)
    gram_rows = lax.psum(left_terms.astype(jnp.bfloat16), "tensor").astype(jnp.float32)
    new_stat_left = blend_stat(stat_left, gram_rows, FF)
    grad_whole = lax.all_gather(grad_cols, "tensor", axis=1, tiled=True)
    picked = lax.dynamic_slice_in_dim(grad_whole, shard_pos * rows_right, rows_right, 1)
    gram_block = jnp.dot(picked.T, grad_cols, preferred_element_type=jnp.float32)
    new_stat_right = blend_stat(stat_right, gram_block, D)
    basis_all = lax.all_gather(basis_left, "shard", axis=0, tiled=True)
    left_q_all = basis_all / math.sqrt(D)
    left_qb_all = left_q_all.astype(jnp.bfloat16)
    left_qb_own = lax.dynamic_slice_in_dim(left_qb_all, row_start, rows_left, 0)
    left_cols_own = lax.dynamic_slice_in_dim(left_qb_all, row_start, rows_left, 1)
    half_rotated = jnp.dot(left_cols_own.T, grad_cols, preferred_element_type=jnp.float32).astype(
        jnp.bfloat16
    )
    right_q = basis_right / math.sqrt(FF)
    right_qb = right_q.astype(jnp.bfloat16)
    right_cols_b = lax.all_gather(right_qb, "shard", axis=0, tiled=True)
    half_full = lax.all_gather(half_rotated, "tensor", axis=1, tiled=True)
    rotated = jnp.dot(half_full, right_cols_b, preferred_element_type=jnp.float32)
    new_moment_one, new_moment_two, direction = adam_moments(rotated, moment_one, moment_two)
    back_half = jnp.dot(
        left_qb_own,
        lax.all_gather(direction, "shard", axis=0, tiled=True),
        preferred_element_type=jnp.float32,
    ).astype(jnp.bfloat16)
    back_terms = jnp.dot(back_half, right_cols_b.T, preferred_element_type=jnp.float32)
    update = lax.psum_scatter(back_terms, "tensor", scatter_dimension=1, tiled=True).astype(
        jnp.bfloat16
    )
    stat_rows = lax.all_gather(new_stat_right, "tensor", axis=1, tiled=True)
    power_right = jnp.dot(
        stat_rows,
        lax.all_gather(right_q, "shard", axis=0, tiled=True),
        precision=highest,
        preferred_element_type=jnp.float32,
    )
    power_left = jnp.dot(
        new_stat_left, left_q_all, precision=highest, preferred_element_type=jnp.float32
    )
    local_left = jnp.sum(power_left * power_left)
    local_right = jnp.sum(power_right * power_right)
    total_left = lax.psum(local_left, "shard")
    total_right = lax.psum(local_right, ("shard", "tensor"))
    iterate_left = power_left * (math.sqrt(D) / (4.0 * jnp.sqrt(total_left)))
    for iteration in range(NS_STEPS):
        partial_gram = jnp.dot(
            iterate_left.T, iterate_left, precision=highest, preferred_element_type=jnp.float32
        )
        gram_left = lax.psum(partial_gram.astype(jnp.bfloat16), "shard").astype(jnp.float32)
        iterate_left = 1.5 * iterate_left - 0.5 * jnp.dot(
            iterate_left, gram_left, precision=highest, preferred_element_type=jnp.float32
        )
    iterate_right = power_right * (math.sqrt(FF) / (4.0 * jnp.sqrt(total_right)))
    row_ids = shard_pos * rows_right + lax.broadcasted_iota(jnp.int32, (rows_right, cols_right), 0)
    col_ids = tensor_pos * cols_right + lax.broadcasted_iota(jnp.int32, (rows_right, cols_right), 1)
    identity_tile = (row_ids == col_ids).astype(jnp.float32)
    for iteration in range(NS_STEPS):
        rounded_iterate = iterate_right.astype(jnp.bfloat16)
        iterate_rows = lax.all_gather(rounded_iterate, "tensor", axis=1, tiled=True)
        gram_right = lax.psum_scatter(
            jnp.dot(iterate_rows.T, rounded_iterate, preferred_element_type=jnp.float32).astype(
                jnp.bfloat16
            ),
            "shard",
            scatter_dimension=0,
            tiled=True,
        ).astype(jnp.float32)
        mixing = (1.5 * identity_tile - 0.5 * gram_right).astype(jnp.bfloat16)
        iterate_right = jnp.dot(
            iterate_rows,
            lax.all_gather(mixing, "shard", axis=0, tiled=True),
            preferred_element_type=jnp.float32,
        )
    return (
        update,
        new_moment_one,
        new_moment_two,
        new_stat_left,
        new_stat_right,
        iterate_left * math.sqrt(D),
        iterate_right * math.sqrt(FF),
    )


BF = jnp.bfloat16
F32 = jnp.float32
AXES = ("shard", "tensor")
PATTERN = (4, 2, 2, 2)


def dot_nn(a, b):
    return jnp.dot(a, b, preferred_element_type=F32)


def dot_nt(a, b):
    return lax.dot_general(a, b, (((1,), (1,)), ((), ())), preferred_element_type=F32)


def dot_tn(a, b):
    return lax.dot_general(a, b, (((0,), (0,)), ((), ())), preferred_element_type=F32)


def pairs(move):
    nz, nx, ny, nc = PATTERN
    out = []
    for z in range(nz):
        for x in range(nx):
            for y in range(ny):
                for c in range(nc):
                    to = move(z, x, y, c)
                    if 0 <= to[0] < nz:
                        source = ((z * nx + x) * ny + y) * nc + c
                        target = ((to[0] * nx + to[1]) * ny + to[2]) * nc + to[3]
                        out.append((source, target))
    return out


def swap_x(a):
    return lax.ppermute(a, AXES, pairs(lambda z, x, y, c: (z, 1 - x, y, c)))


def swap_y(a):
    return lax.ppermute(a, AXES, pairs(lambda z, x, y, c: (z, x, 1 - y, c)))


def swap_core(a):
    return lax.ppermute(a, AXES, pairs(lambda z, x, y, c: (z, x, y, 1 - c)))


def swap_outer(a):
    return lax.ppermute(a, AXES, pairs(lambda z, x, y, c: (z + 1 - 2 * (z % 2), x, y, c)))


def swap_inner(a):
    return lax.ppermute(a, AXES, pairs(lambda z, x, y, c: (3 - z if 0 < z < 3 else -1, x, y, c)))


def turn_over(a, straight):
    crossed = pairs(lambda z, x, y, c: (z if x != c else -1, 1 - x, y, 1 - c))
    return jnp.where(straight, a, lax.ppermute(a, AXES, crossed))


def stage(*parts):
    return lax.optimization_barrier(parts)


def swap_to(across, along):
    return lambda a: lax.ppermute(
        a, AXES, pairs(lambda z, x, y, c: (z, c, (y + along) % 2, (x + across) % 2))
    )


def places_z(z):
    return z + 1 - 2 * (z % 2), jnp.where(z < 2, 2, 1), jnp.where(z < 2, 3, 0)


def in_order(z, own, near, mid, far):
    whole = jnp.zeros((4,) + own.shape, own.dtype)
    for block, place in zip((own, near, mid, far), (z,) + places_z(z)):
        whole = lax.dynamic_update_slice(whole, block[None], (place,) + (0,) * own.ndim)
    return whole


def ordered_pair(ahead, first, second):
    both = jnp.concatenate([first[None], second[None]])
    return jnp.where(ahead, both, jnp.concatenate([second[None], first[None]]))


def put(whole, part, *start):
    return lax.dynamic_update_slice(whole, part, start)


def interleave(core, mine, theirs):
    rows, cols = mine.shape[1:]
    whole = jnp.zeros((4, 2, rows, cols), mine.dtype)
    whole = put(whole, mine[:, None], 0, core, 0, 0)
    whole = put(whole, theirs[:, None], 0, 1 - core, 0, 0)
    return whole.reshape(8 * rows, cols)


def refresh_kernel(place_ref, sum_ref, more_ref, *refs):
    slabs = refs[:8]
    out_ref, whole, inner, held, total, first, sems = refs[8:]
    count, size = held.shape
    tall = size // 4
    half = size // 8

    def copy(k, i):
        source = slabs[k].at[pl.ds(i * half, half), :]
        target = whole.at[pl.ds(k * half, half), pl.ds(i * tall, tall)]
        return pltpu.make_async_copy(source, target, sems.at[k, i])

    def arrived(j):
        for k in (2 * j, 2 * j + 1):
            for i in range(4):
                copy(k, i).wait()

    def span_of(j):
        return pl.ds(pl.multiple_of(j * tall, tall), tall)

    for k in range(8):
        for i in range(4):
            copy(k, i).start()
    squares = size / (16.0 * (sum_ref[...] + more_ref[...]))
    square = squares[0, 0]
    last = (math.sqrt(size) * jnp.sqrt(squares))[0, 0]
    arrived(0)
    held[...] = whole[pl.ds(pl.multiple_of(place_ref[0], 16), count), :]
    total[...] = held[...].astype(F32)

    def one_pass(i, carry):
        def towards(j, carry):
            @pl.when(i == 0)
            def _():
                for k in range(1, 4):
                    pl.when(j == k)(functools.partial(arrived, k))

            inner[:, span_of(j)] = dot_nt(held[...], whole[span_of(j), :]).astype(BF)
            return carry

        lax.fori_loop(0, 4, towards, 0)
        keep = jnp.where(i == 1, 0.0, 1.5)
        take = jnp.where(i == 1, square, -0.5 * square)

        def back(j, carry):
            span = span_of(j)
            value = keep * total[:, span] + take * dot_nn(inner[...], whole[:, span])
            total[:, span] = value
            held[:, span] = value.astype(BF)

            @pl.when(i == 0)
            def _():
                first[:, span] = value

            return carry

        lax.fori_loop(0, jnp.where(i == 3, 2, 4), back, 0)
        return carry

    lax.fori_loop(0, 4, one_pass, 0)
    for k in range(2):
        span = slice(k * tall, (k + 1) * tall)
        place = jnp.where(place_ref[1] == 1, k, 1 - k)
        out_ref[place] = last * (1.5 * first[:, span] - 0.5 * total[:, span])


def refresh(places, sums, slabs):
    size, tall = 2 * slabs[0].shape[0], slabs[0].shape[1]
    count = size // 16
    in_vmem = pl.BlockSpec(memory_space=pltpu.VMEM)
    in_smem = pl.BlockSpec(memory_space=pltpu.SMEM)
    mine = pl.BlockSpec(memory_space=pl.ANY)
    theirs = pl.BlockSpec(memory_space=pltpu.HBM)
    return pl.pallas_call(
        refresh_kernel,
        out_shape=jax.ShapeDtypeStruct((2, count, tall), F32),
        in_specs=[in_smem] + [in_vmem] * 2 + [mine, theirs] * 4,
        out_specs=in_vmem,
        scratch_shapes=[
            pltpu.VMEM((size, size), BF),
            pltpu.VMEM((count, size), BF),
            pltpu.VMEM((count, size), BF),
            pltpu.VMEM((count, size), F32),
            pltpu.VMEM((count, size), F32),
            pltpu.SemaphoreType.DMA((8, 4)),
        ],
        compiler_params=pltpu.CompilerParams(vmem_limit_bytes=34 * 2**20),
        cost_estimate=pl.CostEstimate(
            flops=15 * count * size * size, bytes_accessed=2 * size * size, transcendentals=0
        ),
    )(places, *sums, *slabs)


def side_kernel(place_ref, core_ref, other_ref, cols_ref, rows_ref, power_ref, *refs):
    basis_ref, terms, power, direction = refs[0], refs[1:5], refs[5], refs[6]
    rows = power_ref.shape[0]
    size = power.shape[0]
    for k in range(8):
        source = (core_ref, other_ref)[k // 4]
        start = (k % 4) * 2 * rows
        place = pl.ds(pl.multiple_of(place_ref[k], 16), rows)
        direction[place, :] = source[start : start + rows, :]
        power[k * rows : (k + 1) * rows, :] = source[start + rows : start + 2 * rows, :]
    back_half = dot_nn(rows_ref[...], direction[...]).astype(BF)
    for k in range(4):
        block = pl.ds(pl.multiple_of(place_ref[8 + k], 16), size)
        terms[k][...] = dot_nt(back_half, cols_ref[block, :]).astype(BF)
    total = jnp.zeros((rows, size), F32)
    for k in range(8):
        total += jnp.square(power[k * rows : (k + 1) * rows, :].astype(F32))
    square = size / (16.0 * jnp.sum(total))
    keep = power_ref[...]
    value = keep
    for turn in range(4):
        across = dot_nt(value.astype(BF), power[...]).astype(BF)
        moved = square * dot_nn(across, power[...])
        value = moved if turn == 1 else 1.5 * value - 0.5 * moved
        if turn == 0:
            keep = value
    scale = math.sqrt(size) * jnp.sqrt(jnp.full((rows, size), square))
    basis_ref[...] = scale * (1.5 * keep - 0.5 * value)


def side(places, extra_core, extra_other, right_cols, left_rows, power_left):
    rows, size = power_left.shape
    in_vmem = pl.BlockSpec(memory_space=pltpu.VMEM)
    term = jax.ShapeDtypeStruct((rows, size), BF)
    return pl.pallas_call(
        side_kernel,
        out_shape=[jax.ShapeDtypeStruct((rows, size), F32)] + [term] * 4,
        in_specs=[pl.BlockSpec(memory_space=pltpu.SMEM)] + [in_vmem] * 5,
        out_specs=[in_vmem] * 5,
        scratch_shapes=[pltpu.VMEM((size, size), BF), pltpu.VMEM((size, size), BF)],
        compiler_params=pltpu.CompilerParams(vmem_limit_bytes=12 * 2**20),
        cost_estimate=pl.CostEstimate(
            flops=26 * rows * size * size, bytes_accessed=12 * size * size, transcendentals=0
        ),
    )(places, extra_core, extra_other, right_cols, left_rows, power_left)


def squares(tiles):
    return jnp.sum(jnp.square(tiles.astype(F32)))


def local_pattern(gradient, moment_one, moment_two, stat_left, stat_right, basis_left, basis_right):
    rows_left = gradient.shape[0]
    rows_right = stat_right.shape[0]
    cols_right = stat_right.shape[1]
    shard_pos = lax.axis_index("shard")
    tensor_pos = lax.axis_index("tensor")
    z, x = shard_pos // 2, shard_pos % 2
    y, core = tensor_pos // 2, tensor_pos % 2
    straight = x == core
    inner = (z == 1) | (z == 2)
    half = rows_right // 2

    left_b = (basis_left / math.sqrt(D)).astype(BF)
    right_b = (basis_right / math.sqrt(FF)).astype(BF)
    stat_b = stat_right.astype(BF)
    part_left = rows_left // 2
    small = jnp.concatenate(
        [gradient, lax.dynamic_slice_in_dim(left_b, y * part_left, part_left, 0)]
    )
    rows_small = small.shape[0]

    turned, small_o1, small_i1 = stage(
        turn_over(right_b, straight), swap_outer(small), swap_inner(small)
    )
    got_i, got_o, stat_y, stat_x = stage(
        swap_inner(jnp.concatenate([turned, small_o1])),
        swap_outer(jnp.concatenate([turned, small_i1])),
        swap_y(stat_b),
        swap_x(stat_b),
    )
    turned_o1, small_o2 = got_o[:rows_right], got_o[rows_right:]
    turned_i1, small_i2 = got_i[:rows_right], got_i[rows_right:]
    small_1 = ordered_pair(z % 2 == 0, small, small_o1).reshape(2 * rows_small, cols_right)
    turned_i2, got_o, got_y, got_x = stage(
        swap_inner(turned_o1),
        swap_outer(jnp.concatenate([turned_i1, small_i2])),
        swap_y(jnp.concatenate([stat_x[:half], small_1])),
        swap_x(jnp.concatenate([stat_y[half:], small_1])),
    )
    turned_o2, small_o3 = got_o[:rows_right], got_o[rows_right:]
    small_2 = ordered_pair(
        z < 2, jnp.where(inner, small_i1, small_o2), jnp.where(inner, small_i2, small_o3)
    ).reshape(2 * rows_small, cols_right)
    stat_xy = jnp.concatenate([got_y[:half], got_x[:half]])
    small_1x, small_1y = got_x[half:], got_y[half:]
    stat_keep = [jnp.where(straight, stat_b, stat_x), jnp.where(straight, stat_y, stat_xy)]
    stat_send = [jnp.where(straight, stat_x, stat_b), jnp.where(straight, stat_xy, stat_y)]
    turned_o3, got_x, got_y, stat_got = stage(
        swap_outer(turned_i2),
        swap_x(jnp.concatenate([small_1y[rows_small:], small_2])),
        swap_y(jnp.concatenate([small_1x[:rows_small], small_2])),
        swap_core(jnp.concatenate(stat_send)),
    )
    small_1xy = jnp.concatenate([got_y[:rows_small], got_x[:rows_small]])
    small_2x, small_2y = got_x[rows_small:], got_y[rows_small:]
    turned_z = in_order(
        z,
        turned,
        turned_o1,
        jnp.where(inner, turned_i1, turned_o2),
        jnp.where(inner, turned_i2, turned_o3),
    )
    stat_rows = jnp.zeros((rows_right, 4 * cols_right), BF)
    stat_rows = put(stat_rows, stat_keep[0], 0, (2 * y + core) * cols_right)
    stat_rows = put(stat_rows, stat_keep[1], 0, (2 - 2 * y + core) * cols_right)
    stat_rows = put(stat_rows, stat_got[:rows_right], 0, (2 * y + 1 - core) * cols_right)
    stat_rows = put(stat_rows, stat_got[rows_right:], 0, (3 - 2 * y - core) * cols_right)
    small_2hi, small_2lo, turned_got = stage(
        swap_x(small_2y[rows_small:]), swap_y(small_2x[:rows_small]), swap_core(turned_z)
    )
    right_cols = interleave(core, turned_z, turned_got)
    grad_core = jnp.zeros((4, 2, rows_left, 2 * cols_right), BF)
    left_all = jnp.zeros((4, 2, 2, part_left, cols_right), BF)
    small_2xy = jnp.concatenate([small_2lo, small_2hi])
    low = 2 * (z // 2)
    for block, at_z, at_x, at_y in (
        (small_1, low, x, y),
        (small_1x, low, 1 - x, y),
        (small_1y, low, x, 1 - y),
        (small_1xy, low, 1 - x, 1 - y),
        (small_2, 2 - low, x, y),
        (small_2x, 2 - low, 1 - x, y),
        (small_2y, 2 - low, x, 1 - y),
        (small_2xy, 2 - low, 1 - x, 1 - y),
    ):
        block = block.reshape(2, 1, rows_small, cols_right)
        grad_core = put(grad_core, block[:, :, :rows_left], at_z, at_x, 0, at_y * cols_right)
        left_all = put(left_all, block[:, :, None, rows_left:], at_z, at_x, at_y, 0, 0)
    grad_core = grad_core.reshape(8 * rows_left, 2 * cols_right)
    left_all = left_all.reshape(8 * rows_left, cols_right)

    grad_other = swap_core(grad_core)
    rows_core = lax.dynamic_slice_in_dim(
        right_cols.reshape(2, 2, cols_right, cols_right), core, 1, 1
    ).reshape(2 * cols_right, cols_right)
    carried = dot_nn(grad_core, rows_core)
    carried = (carried + swap_core(carried.astype(BF)).astype(F32)).astype(BF)
    grad_whole = jnp.zeros((8 * rows_left, 4 * cols_right), BF)
    for k in range(2):
        cols = slice(k * cols_right, (k + 1) * cols_right)
        grad_whole = put(grad_whole, grad_core[:, cols], 0, (2 * k + core) * cols_right)
        grad_whole = put(grad_whole, grad_other[:, cols], 0, (2 * k + 1 - core) * cols_right)
    share = (1.0 - beta_stat) / D
    picked = lax.dynamic_slice_in_dim(grad_whole, (2 * z + core) * rows_right, rows_right, 1)
    power = beta_stat * dot_nn(stat_rows, right_cols) + share * dot_tn(picked, carried)
    power = power.astype(BF)

    own_cols = lax.dynamic_slice_in_dim(grad_whole, shard_pos * rows_right, rows_right, 1)
    own_grad = lax.dynamic_slice_in_dim(grad_whole, tensor_pos * cols_right, cols_right, 1)
    new_stat_right = blend_stat(stat_right, dot_tn(own_cols, own_grad), D)
    left_cols = lax.dynamic_slice_in_dim(left_all, (2 * z + core) * rows_left, rows_left, 1)
    rotated = dot_tn(left_cols, carried).astype(BF)
    grad_rows = lax.dynamic_slice_in_dim(grad_whole, shard_pos * rows_left, rows_left, 0)
    new_stat_left = blend_stat(stat_left, dot_nt(grad_rows, grad_whole), FF)
    power_left = dot_nn(new_stat_left.astype(BF), left_all)
    power_left_b = power_left.astype(BF)

    rotated = turn_over(rotated, straight)
    new_moment_one, new_moment_two, direction = adam_moments(
        rotated.astype(F32), moment_one, moment_two
    )
    extra = turn_over(jnp.concatenate([direction, power_left_b]), straight)
    power_i1, near, power_y, power_x, extra, new_stat_right = stage(
        swap_inner(power),
        swap_outer(power),
        swap_y(power),
        swap_x(power),
        extra,
        new_stat_right,
    )
    got_i, got_o, got_y, got_x = stage(
        swap_inner(jnp.concatenate([near, extra])),
        swap_outer(jnp.concatenate([power_i1, extra])),
        swap_y(jnp.concatenate([power_x[:half], near])),
        swap_x(jnp.concatenate([power_y[half:], near])),
    )
    slab0 = jnp.concatenate([power, power_x, power_y, got_y[:half], got_x[:half]])
    near_x, near_y = got_x[half:], got_y[half:]
    power_o2, extra_o1 = got_o[:rows_right], got_o[rows_right:]
    power_i2, extra_i1 = got_i[:rows_right], got_i[rows_right:]
    mid = jnp.where(inner, power_i1, power_o2)
    slab0_other = swap_core(slab0)
    extra_i2, got_o, got_y, got_x, slab0_other, sum0 = stage(
        swap_inner(extra_o1),
        swap_outer(jnp.concatenate([power_i2, extra_i1])),
        swap_y(jnp.concatenate([near_x[:half], mid])),
        swap_x(jnp.concatenate([near_y[half:], mid])),
        slab0_other,
        squares(slab0_other),
    )
    slab1 = jnp.concatenate([near, near_x, near_y, got_y[:half], got_x[:half]])
    mid_x, mid_y = got_x[half:], got_y[half:]
    power_o3, extra_o2 = got_o[:rows_right], got_o[rows_right:]
    far = jnp.where(inner, power_i2, power_o3)
    slab1_other = swap_core(slab1)
    extra_o3, got_y, got_x, slab1_other, sum1 = stage(
        swap_outer(extra_i2),
        swap_y(jnp.concatenate([mid_x[:half], far])),
        swap_x(jnp.concatenate([mid_y[half:], far])),
        slab1_other,
        squares(slab1_other),
    )
    slab2 = jnp.concatenate([mid, mid_x, mid_y, got_y[:half], got_x[:half]])
    far_x, far_y = got_x[half:], got_y[half:]
    extra_core = jnp.concatenate(
        [extra, extra_o1, jnp.where(inner, extra_i1, extra_o2), jnp.where(inner, extra_i2, extra_o3)]
    )
    slab2_other = swap_core(slab2)
    extra_other = swap_core(extra_core)
    near_place, mid_place, far_place = places_z(z)
    side_places = [
        (2 * at_z + at_x) * rows_left
        for at_x in (core, 1 - core)
        for at_z in (z, near_place, mid_place, far_place)
    ] + [
        ((y + along) % 2 * 2 + (x + across) % 2) * cols_right
        for along in range(2)
        for across in range(2)
    ]
    new_basis_left, *terms = side(
        jnp.stack(side_places),
        extra_core,
        extra_other,
        right_cols,
        lax.dynamic_slice_in_dim(left_all, (2 * z + core) * rows_left, rows_left, 0),
        power_left,
    )
    got_y, got_x, slab2_other, sum2, new_basis_left = stage(
        swap_y(far_x[:half]),
        swap_x(far_y[half:]),
        slab2_other,
        squares(slab2_other),
        new_basis_left,
    )
    slab3 = jnp.concatenate([far, far_x, far_y, got_y, got_x])
    slab3_other = swap_core(slab3)
    sum_core = jnp.full((8, 128), sum0 + sum1 + sum2 + squares(slab3))

    terms = [
        swap_to(across, along)(terms[2 * along + across])
        for along in range(2)
        for across in range(2)
    ]
    update = sum(term.astype(F32) for term in terms).astype(BF)

    places = jnp.stack(
        [jnp.where(straight, 0, rows_right) + core * half, straight.astype(jnp.int32)]
    )
    slabs = (slab0, slab0_other, slab1, slab1_other, slab2, slab2_other, slab3, slab3_other)
    fresh = refresh(places, (sum_core, swap_core(sum_core)), slabs)
    theirs = swap_core(fresh[1])
    new_basis_right = jnp.zeros((rows_right, cols_right), F32)
    new_basis_right = put(new_basis_right, fresh[0], core * half, 0)
    new_basis_right = put(new_basis_right, theirs, (1 - core) * half, 0)
    return (
        update,
        new_moment_one,
        new_moment_two,
        new_stat_left,
        new_stat_right,
        new_basis_left,
        new_basis_right,
    )


def solution(mesh):
    nz, nx, ny, nc = PATTERN
    fits = (mesh.shape["shard"], mesh.shape["tensor"]) == (nz * nx, ny * nc)
    local = local_pattern if fits else local_general
    placed = (
        P("shard", "tensor"),
        P("shard", "tensor"),
        P("shard", "tensor"),
        P("shard", None),
        P("shard", "tensor"),
        P("shard", None),
        P("shard", "tensor"),
    )
    return jax.shard_map(
        local,
        mesh=mesh,
        in_specs=placed,
        out_specs=(
            P("shard", "tensor"),
            P("shard", "tensor"),
            P("shard", "tensor"),
            P("shard", None),
            P("shard", "tensor"),
            P("shard", None),
            P("shard", "tensor"),
        ),
        check_vma=False,
    )
```

```python
import functools
import math

import jax
import jax.numpy as jnp
from jax import lax
from jax.experimental import pallas as pl
from jax.experimental.pallas import tpu as pltpu
from jax.sharding import PartitionSpec as P

D = 768
FF = 3072
NS_STEPS = 2


beta_one = 0.95
beta_two = 0.95
beta_stat = 0.95
correction = 1.0 - 0.95**10
adam_eps = 1e-08
highest = lax.Precision.HIGHEST


def blend_stat(previous, product, divisor):
    return beta_stat * previous + (1.0 - beta_stat) * (product / divisor)


def adam_moments(rotated, moment_one, moment_two):
    first_moment = beta_one * moment_one + (1.0 - beta_one) * rotated
    second_moment = beta_two * moment_two + (1.0 - beta_two) * (rotated * rotated)
    direction = (
        first_moment / correction / (jnp.sqrt(second_moment / correction) + adam_eps)
    ).astype(jnp.bfloat16)
    return (first_moment, second_moment, direction)


def local_general(gradient, moment_one, moment_two, stat_left, stat_right, basis_left, basis_right):
    rows_left = gradient.shape[0]
    rows_right = stat_right.shape[0]
    cols_right = stat_right.shape[1]
    shard_pos = lax.axis_index("shard")
    tensor_pos = lax.axis_index("tensor")
    row_start = shard_pos * rows_left
    grad_cols = lax.all_gather(gradient, "shard", axis=0, tiled=True)
    left_terms = jnp.dot(gradient, grad_cols.T, preferred_element_type=jnp.float32)
    gram_rows = lax.psum(left_terms.astype(jnp.bfloat16), "tensor").astype(jnp.float32)
    new_stat_left = blend_stat(stat_left, gram_rows, FF)
    grad_whole = lax.all_gather(grad_cols, "tensor", axis=1, tiled=True)
    picked = lax.dynamic_slice_in_dim(grad_whole, shard_pos * rows_right, rows_right, 1)
    gram_block = jnp.dot(picked.T, grad_cols, preferred_element_type=jnp.float32)
    new_stat_right = blend_stat(stat_right, gram_block, D)
    basis_all = lax.all_gather(basis_left, "shard", axis=0, tiled=True)
    left_q_all = basis_all / math.sqrt(D)
    left_qb_all = left_q_all.astype(jnp.bfloat16)
    left_qb_own = lax.dynamic_slice_in_dim(left_qb_all, row_start, rows_left, 0)
    left_cols_own = lax.dynamic_slice_in_dim(left_qb_all, row_start, rows_left, 1)
    half_rotated = jnp.dot(left_cols_own.T, grad_cols, preferred_element_type=jnp.float32).astype(
        jnp.bfloat16
    )
    right_q = basis_right / math.sqrt(FF)
    right_qb = right_q.astype(jnp.bfloat16)
    right_cols_b = lax.all_gather(right_qb, "shard", axis=0, tiled=True)
    half_full = lax.all_gather(half_rotated, "tensor", axis=1, tiled=True)
    rotated = jnp.dot(half_full, right_cols_b, preferred_element_type=jnp.float32)
    new_moment_one, new_moment_two, direction = adam_moments(rotated, moment_one, moment_two)
    back_half = jnp.dot(
        left_qb_own,
        lax.all_gather(direction, "shard", axis=0, tiled=True),
        preferred_element_type=jnp.float32,
    ).astype(jnp.bfloat16)
    back_terms = jnp.dot(back_half, right_cols_b.T, preferred_element_type=jnp.float32)
    update = lax.psum_scatter(back_terms, "tensor", scatter_dimension=1, tiled=True).astype(
        jnp.bfloat16
    )
    stat_rows = lax.all_gather(new_stat_right, "tensor", axis=1, tiled=True)
    power_right = jnp.dot(
        stat_rows,
        lax.all_gather(right_q, "shard", axis=0, tiled=True),
        precision=highest,
        preferred_element_type=jnp.float32,
    )
    power_left = jnp.dot(
        new_stat_left, left_q_all, precision=highest, preferred_element_type=jnp.float32
    )
    local_left = jnp.sum(power_left * power_left)
    local_right = jnp.sum(power_right * power_right)
    total_left = lax.psum(local_left, "shard")
    total_right = lax.psum(local_right, ("shard", "tensor"))
    iterate_left = power_left * (math.sqrt(D) / (4.0 * jnp.sqrt(total_left)))
    for iteration in range(NS_STEPS):
        partial_gram = jnp.dot(
            iterate_left.T, iterate_left, precision=highest, preferred_element_type=jnp.float32
        )
        gram_left = lax.psum(partial_gram.astype(jnp.bfloat16), "shard").astype(jnp.float32)
        iterate_left = 1.5 * iterate_left - 0.5 * jnp.dot(
            iterate_left, gram_left, precision=highest, preferred_element_type=jnp.float32
        )
    iterate_right = power_right * (math.sqrt(FF) / (4.0 * jnp.sqrt(total_right)))
    row_ids = shard_pos * rows_right + lax.broadcasted_iota(jnp.int32, (rows_right, cols_right), 0)
    col_ids = tensor_pos * cols_right + lax.broadcasted_iota(jnp.int32, (rows_right, cols_right), 1)
    identity_tile = (row_ids == col_ids).astype(jnp.float32)
    for iteration in range(NS_STEPS):
        rounded_iterate = iterate_right.astype(jnp.bfloat16)
        iterate_rows = lax.all_gather(rounded_iterate, "tensor", axis=1, tiled=True)
        gram_right = lax.psum_scatter(
            jnp.dot(iterate_rows.T, rounded_iterate, preferred_element_type=jnp.float32).astype(
                jnp.bfloat16
            ),
            "shard",
            scatter_dimension=0,
            tiled=True,
        ).astype(jnp.float32)
        mixing = (1.5 * identity_tile - 0.5 * gram_right).astype(jnp.bfloat16)
        iterate_right = jnp.dot(
            iterate_rows,
            lax.all_gather(mixing, "shard", axis=0, tiled=True),
            preferred_element_type=jnp.float32,
        )
    return (
        update,
        new_moment_one,
        new_moment_two,
        new_stat_left,
        new_stat_right,
        iterate_left * math.sqrt(D),
        iterate_right * math.sqrt(FF),
    )


BF = jnp.bfloat16
F32 = jnp.float32
AXES = ("shard", "tensor")
PATTERN = (4, 2, 2, 2)


def dot_nn(a, b):
    return jnp.dot(a, b, preferred_element_type=F32)


def dot_nt(a, b):
    return lax.dot_general(a, b, (((1,), (1,)), ((), ())), preferred_element_type=F32)


def dot_tn(a, b):
    return lax.dot_general(a, b, (((0,), (0,)), ((), ())), preferred_element_type=F32)


def pairs(move):
    nz, nx, ny, nc = PATTERN
    out = []
    for z in range(nz):
        for x in range(nx):
            for y in range(ny):
                for c in range(nc):
                    to = move(z, x, y, c)
                    if 0 <= to[0] < nz:
                        source = ((z * nx + x) * ny + y) * nc + c
                        target = ((to[0] * nx + to[1]) * ny + to[2]) * nc + to[3]
                        out.append((source, target))
    return out


def swap_x(a):
    return lax.ppermute(a, AXES, pairs(lambda z, x, y, c: (z, 1 - x, y, c)))


def swap_y(a):
    return lax.ppermute(a, AXES, pairs(lambda z, x, y, c: (z, x, 1 - y, c)))


def swap_core(a):
    return lax.ppermute(a, AXES, pairs(lambda z, x, y, c: (z, x, y, 1 - c)))


def swap_outer(a):
    return lax.ppermute(a, AXES, pairs(lambda z, x, y, c: (z + 1 - 2 * (z % 2), x, y, c)))


def swap_inner(a):
    return lax.ppermute(a, AXES, pairs(lambda z, x, y, c: (3 - z if 0 < z < 3 else -1, x, y, c)))


def turn_over(a, straight):
    crossed = pairs(lambda z, x, y, c: (z if x != c else -1, 1 - x, y, 1 - c))
    return jnp.where(straight, a, lax.ppermute(a, AXES, crossed))


def stage(*parts):
    return lax.optimization_barrier(parts)


def swap_diagonal(a):
    return lax.ppermute(a, AXES, pairs(lambda z, x, y, c: (z, 1 - x, 1 - y, c)))


def swap_to(across, along):
    return lambda a: lax.ppermute(
        a, AXES, pairs(lambda z, x, y, c: (z, c, (y + along) % 2, (x + across) % 2))
    )


def places_z(z):
    return z + 1 - 2 * (z % 2), jnp.where(z < 2, 2, 1), jnp.where(z < 2, 3, 0)


def in_order(z, own, near, mid, far):
    whole = jnp.zeros((4,) + own.shape, own.dtype)
    for block, place in zip((own, near, mid, far), (z,) + places_z(z)):
        whole = lax.dynamic_update_slice(whole, block[None], (place,) + (0,) * own.ndim)
    return whole


def ordered_pair(ahead, first, second):
    both = jnp.concatenate([first[None], second[None]])
    return jnp.where(ahead, both, jnp.concatenate([second[None], first[None]]))


def put(whole, part, *start):
    return lax.dynamic_update_slice(whole, part, start)


def interleave(core, mine, theirs):
    rows, cols = mine.shape[1:]
    whole = jnp.zeros((4, 2, rows, cols), mine.dtype)
    whole = put(whole, mine[:, None], 0, core, 0, 0)
    whole = put(whole, theirs[:, None], 0, 1 - core, 0, 0)
    return whole.reshape(8 * rows, cols)


def refresh_kernel(place_ref, sum_ref, *refs):
    slabs = refs[:8]
    out_ref, whole, inner, held, total, first, sems = refs[8:]
    count, size = held.shape
    tall = size // 4
    half = size // 8

    def copy(k, i):
        source = slabs[k].at[pl.ds(i * half, half), :]
        target = whole.at[pl.ds(k * half, half), pl.ds(i * tall, tall)]
        return pltpu.make_async_copy(source, target, sems.at[k, i])

    def arrived(j):
        for k in (2 * j, 2 * j + 1):
            for i in range(4):
                copy(k, i).wait()

    def span_of(j):
        return pl.ds(pl.multiple_of(j * tall, tall), tall)

    for k in range(8):
        for i in range(4):
            copy(k, i).start()
    squares = size / (16.0 * sum_ref[...])
    square = squares[0, 0]
    last = (math.sqrt(size) * jnp.sqrt(squares))[0, 0]
    arrived(0)
    held[...] = whole[pl.ds(pl.multiple_of(place_ref[0], 16), count), :]
    total[...] = held[...].astype(F32)

    def one_pass(i, carry):
        def towards(j, carry):
            @pl.when(i == 0)
            def _():
                for k in range(1, 4):
                    pl.when(j == k)(functools.partial(arrived, k))

            inner[:, span_of(j)] = dot_nt(held[...], whole[span_of(j), :]).astype(BF)
            return carry

        lax.fori_loop(0, 4, towards, 0)
        keep = jnp.where(i == 1, 0.0, 1.5)
        take = jnp.where(i == 1, square, -0.5 * square)

        def back(j, carry):
            span = span_of(j)
            value = keep * total[:, span] + take * dot_nn(inner[...], whole[:, span])
            total[:, span] = value
            held[:, span] = value.astype(BF)

            @pl.when(i == 0)
            def _():
                first[:, span] = value

            return carry

        lax.fori_loop(0, jnp.where(i == 3, 2, 4), back, 0)
        return carry

    lax.fori_loop(0, 4, one_pass, 0)
    for k in range(2):
        span = slice(k * tall, (k + 1) * tall)
        place = jnp.where(place_ref[1] == 1, k, 1 - k)
        out_ref[place] = last * (1.5 * first[:, span] - 0.5 * total[:, span])


def refresh(places, sums, slabs):
    size, tall = 2 * slabs[0].shape[0], slabs[0].shape[1]
    count = size // 16
    in_vmem = pl.BlockSpec(memory_space=pltpu.VMEM)
    in_smem = pl.BlockSpec(memory_space=pltpu.SMEM)
    mine = pl.BlockSpec(memory_space=pl.ANY)
    theirs = pl.BlockSpec(memory_space=pltpu.HBM)
    return pl.pallas_call(
        refresh_kernel,
        out_shape=jax.ShapeDtypeStruct((2, count, tall), F32),
        in_specs=[in_smem] + [in_vmem] + [mine, theirs] * 4,
        out_specs=in_vmem,
        scratch_shapes=[
            pltpu.VMEM((size, size), BF),
            pltpu.VMEM((count, size), BF),
            pltpu.VMEM((count, size), BF),
            pltpu.VMEM((count, size), F32),
            pltpu.VMEM((count, size), F32),
            pltpu.SemaphoreType.DMA((8, 4)),
        ],
        compiler_params=pltpu.CompilerParams(vmem_limit_bytes=56 * 2**20),
        cost_estimate=pl.CostEstimate(
            flops=15 * count * size * size, bytes_accessed=2 * size * size, transcendentals=0
        ),
    )(places, sums, *slabs)


def side_kernel(place_ref, core_ref, other_ref, cols_ref, rows_ref, power_ref, *refs):
    basis_ref, sum_ref, terms = refs[0], refs[1], refs[2:6]
    power, direction, cols, sems = refs[6:]
    rows, size = power_ref.shape
    step = core_ref.shape[0] // 4

    def copy(k):
        block = pl.ds(pl.multiple_of(place_ref[8 + k], 16), size)
        return pltpu.make_async_copy(cols_ref.at[block, :], cols.at[k], sems.at[k])

    for k in range(4):
        copy(k).start()
    total = jnp.zeros((8, 128), F32)
    for k in range(8):
        source = (core_ref, other_ref)[k // 4]
        start = (k % 4) * step
        place = pl.ds(pl.multiple_of(place_ref[k], 16), rows)
        direction[place, :] = source[start : start + rows, :]
        power[k * rows : (k + 1) * rows, :] = source[start + rows : start + 2 * rows, :]
        part = source[start + 2 * rows : start + step, :128].astype(F32)
        total += jnp.sum(part, axis=0, keepdims=True)
    sum_ref[...] = total
    squares = jnp.zeros((rows, size), F32)
    for k in range(8):
        squares += jnp.square(power[k * rows : (k + 1) * rows, :].astype(F32))
    square = size / (16.0 * jnp.sum(squares))
    keep = power_ref[...]
    value = keep
    for turn in range(4):
        across = dot_nt(value.astype(BF), power[...]).astype(BF)
        moved = square * dot_nn(across, power[...])
        value = moved if turn == 1 else 1.5 * value - 0.5 * moved
        if turn == 0:
            keep = value
    scale = math.sqrt(size) * jnp.sqrt(jnp.full((rows, size), square))
    basis_ref[...] = scale * (1.5 * keep - 0.5 * value)
    back_half = dot_nn(rows_ref[...], direction[...]).astype(BF)
    for k in range(4):
        copy(k).wait()
        terms[k][...] = dot_nt(back_half, cols[k]).astype(BF)


def side(places, extra_core, extra_other, right_cols, left_rows, power_left):
    rows, size = power_left.shape
    in_vmem = pl.BlockSpec(memory_space=pltpu.VMEM)
    term = jax.ShapeDtypeStruct((rows, size), BF)
    sums = jax.ShapeDtypeStruct((8, 128), F32)
    return pl.pallas_call(
        side_kernel,
        out_shape=[jax.ShapeDtypeStruct((rows, size), F32), sums] + [term] * 4,
        in_specs=[pl.BlockSpec(memory_space=pltpu.SMEM)]
        + [in_vmem] * 2
        + [pl.BlockSpec(memory_space=pl.ANY)]
        + [in_vmem] * 2,
        out_specs=[in_vmem] * 6,
        scratch_shapes=[
            pltpu.VMEM((size, size), BF),
            pltpu.VMEM((size, size), BF),
            pltpu.VMEM((4, size, size), BF),
            pltpu.SemaphoreType.DMA((4,)),
        ],
        compiler_params=pltpu.CompilerParams(vmem_limit_bytes=56 * 2**20),
        cost_estimate=pl.CostEstimate(
            flops=26 * rows * size * size, bytes_accessed=12 * size * size, transcendentals=0
        ),
    )(places, extra_core, extra_other, right_cols, left_rows, power_left)


def split_sum(total, cols):
    row = lax.broadcasted_iota(jnp.int32, (16, cols), 0)
    block = jnp.zeros((16, cols), F32)
    for k in range(3):
        head = lax.reduce_precision(total, 8, 7)
        block = jnp.where(row == k, head, block)
        total = total - head
    return block.astype(BF)


def local_pattern(gradient, moment_one, moment_two, stat_left, stat_right, basis_left, basis_right):
    rows_left = gradient.shape[0]
    rows_right = stat_right.shape[0]
    cols_right = stat_right.shape[1]
    shard_pos = lax.axis_index("shard")
    tensor_pos = lax.axis_index("tensor")
    z, x = shard_pos // 2, shard_pos % 2
    y, core = tensor_pos // 2, tensor_pos % 2
    straight = x == core
    inner = (z == 1) | (z == 2)
    half = rows_right // 2

    left_b = (basis_left / math.sqrt(D)).astype(BF)
    right_b = (basis_right / math.sqrt(FF)).astype(BF)
    stat_b = stat_right.astype(BF)
    part_left = rows_left // 2
    small = jnp.concatenate(
        [gradient, lax.dynamic_slice_in_dim(left_b, y * part_left, part_left, 0)]
    )
    rows_small = small.shape[0]

    turned, small_o1, small_i1, moment_one, moment_two, stat_left = stage(
        turn_over(right_b, straight),
        swap_outer(small),
        swap_inner(small),
        moment_one,
        moment_two,
        stat_left,
    )
    early = jnp.concatenate([moment_one, moment_two, stat_left]).astype(BF)
    got_i, got_o, stat_y, stat_x, early = stage(
        swap_inner(jnp.concatenate([turned, small_o1])),
        swap_outer(jnp.concatenate([turned, small_i1])),
        swap_y(stat_b),
        swap_x(stat_b),
        turn_over(early, straight),
    )
    turned_o1, small_o2 = got_o[:rows_right], got_o[rows_right:]
    turned_i1, small_i2 = got_i[:rows_right], got_i[rows_right:]
    small_1 = ordered_pair(z % 2 == 0, small, small_o1).reshape(2 * rows_small, cols_right)
    turned_i2, got_o, got_y, got_x = stage(
        swap_inner(turned_o1),
        swap_outer(jnp.concatenate([turned_i1, small_i2])),
        swap_y(jnp.concatenate([stat_x[:half], small_1])),
        swap_x(jnp.concatenate([stat_y[half:], small_1])),
    )
    turned_o2, small_o3 = got_o[:rows_right], got_o[rows_right:]
    small_2 = ordered_pair(
        z < 2, jnp.where(inner, small_i1, small_o2), jnp.where(inner, small_i2, small_o3)
    ).reshape(2 * rows_small, cols_right)
    stat_xy = jnp.concatenate([got_y[:half], got_x[:half]])
    small_1x, small_1y = got_x[half:], got_y[half:]
    stat_keep = [jnp.where(straight, stat_b, stat_x), jnp.where(straight, stat_y, stat_xy)]
    stat_send = [jnp.where(straight, stat_x, stat_b), jnp.where(straight, stat_xy, stat_y)]
    turned_o3, got_x, got_y, stat_got = stage(
        swap_outer(turned_i2),
        swap_x(jnp.concatenate([small_1y[rows_small:], small_2])),
        swap_y(jnp.concatenate([small_1x[:rows_small], small_2])),
        swap_core(jnp.concatenate(stat_send)),
    )
    small_1xy = jnp.concatenate([got_y[:rows_small], got_x[:rows_small]])
    small_2x, small_2y = got_x[rows_small:], got_y[rows_small:]
    turned_z = in_order(
        z,
        turned,
        turned_o1,
        jnp.where(inner, turned_i1, turned_o2),
        jnp.where(inner, turned_i2, turned_o3),
    )
    stat_rows = jnp.zeros((rows_right, 4 * cols_right), BF)
    stat_rows = put(stat_rows, stat_keep[0], 0, (2 * y + core) * cols_right)
    stat_rows = put(stat_rows, stat_keep[1], 0, (2 - 2 * y + core) * cols_right)
    stat_rows = put(stat_rows, stat_got[:rows_right], 0, (2 * y + 1 - core) * cols_right)
    stat_rows = put(stat_rows, stat_got[rows_right:], 0, (3 - 2 * y - core) * cols_right)
    small_2hi, small_2lo, turned_got = stage(
        swap_x(small_2y[rows_small:]), swap_y(small_2x[:rows_small]), swap_core(turned_z)
    )
    right_cols = interleave(core, turned_z, turned_got)
    grad_core = jnp.zeros((4, 2, rows_left, 2 * cols_right), BF)
    left_all = jnp.zeros((4, 2, 2, part_left, cols_right), BF)
    small_2xy = jnp.concatenate([small_2lo, small_2hi])
    low = 2 * (z // 2)
    for block, at_z, at_x, at_y in (
        (small_1, low, x, y),
        (small_1x, low, 1 - x, y),
        (small_1y, low, x, 1 - y),
        (small_1xy, low, 1 - x, 1 - y),
        (small_2, 2 - low, x, y),
        (small_2x, 2 - low, 1 - x, y),
        (small_2y, 2 - low, x, 1 - y),
        (small_2xy, 2 - low, 1 - x, 1 - y),
    ):
        block = block.reshape(2, 1, rows_small, cols_right)
        grad_core = put(grad_core, block[:, :, :rows_left], at_z, at_x, 0, at_y * cols_right)
        left_all = put(left_all, block[:, :, None, rows_left:], at_z, at_x, at_y, 0, 0)
    grad_core = grad_core.reshape(8 * rows_left, 2 * cols_right)
    left_all = left_all.reshape(8 * rows_left, cols_right)

    grad_other = swap_core(grad_core)
    rows_core = lax.dynamic_slice_in_dim(
        right_cols.reshape(2, 2, cols_right, cols_right), core, 1, 1
    ).reshape(2 * cols_right, cols_right)
    carried = dot_nn(grad_core, rows_core)
    carried = (carried + swap_core(carried.astype(BF)).astype(F32)).astype(BF)

    def grad_block(at_x):
        start = (z // 2) * cols_right + at_x * rows_right
        ours = lax.dynamic_slice_in_dim(grad_core, start, rows_right, 1)
        other = lax.dynamic_slice_in_dim(grad_other, start, rows_right, 1)
        return jnp.where(z % 2 == core, ours, other)

    def grad_gram(start):
        total = 0.0
        for part in (grad_core, grad_other):
            rows = lax.dynamic_slice_in_dim(part, start, rows_left, 0)
            total = total + dot_nt(rows, part)
        return total

    share = (1.0 - beta_stat) / D
    picked = grad_block(core)
    power = beta_stat * dot_nn(stat_rows, right_cols) + share * dot_tn(picked, carried)
    power, carried = stage(power.astype(BF), carried)

    here = (2 * z + core) * rows_left
    early = early.astype(F32)
    left_cols = lax.dynamic_slice_in_dim(left_all, here, rows_left, 1)
    rotated = dot_tn(left_cols, carried)
    _, _, direction = adam_moments(rotated, early[:rows_left], early[rows_left : 2 * rows_left])
    stat_t = blend_stat(early[2 * rows_left :], grad_gram(here), FF)
    left_t = dot_nn(stat_t.astype(BF), left_all).astype(BF)
    square = jnp.sum(jnp.square(power.astype(F32)), keepdims=True)
    extra = jnp.concatenate([direction, left_t, split_sum(square, cols_right)])

    own_grad = lax.dynamic_slice_in_dim(grad_core, y * cols_right, cols_right, 1)
    new_stat_right = blend_stat(stat_right, dot_tn(grad_block(x), own_grad), D)
    new_stat_left = blend_stat(stat_left, grad_gram(shard_pos * rows_left), FF)
    power_left = dot_nn(new_stat_left.astype(BF), left_all)

    power_i1, near, power_y, power_x, extra = stage(
        swap_inner(power),
        swap_outer(power),
        swap_y(power),
        swap_x(power),
        extra,
    )
    got_i, got_o, got_y, got_x, new_stat_right, new_stat_left, power_left = stage(
        swap_inner(jnp.concatenate([near, extra])),
        swap_outer(jnp.concatenate([power_i1, extra])),
        swap_y(jnp.concatenate([power_x[:half], near])),
        swap_x(jnp.concatenate([power_y[half:], near])),
        new_stat_right,
        new_stat_left,
        power_left,
    )
    slab0 = jnp.concatenate([power, power_x, power_y, got_y[:half], got_x[:half]])
    near_x, near_y = got_x[half:], got_y[half:]
    power_o2, extra_o1 = got_o[:rows_right], got_o[rows_right:]
    power_i2, extra_i1 = got_i[:rows_right], got_i[rows_right:]
    mid = jnp.where(inner, power_i1, power_o2)
    extra_i2, got_o, got_y, got_x, slab0_other = stage(
        swap_inner(extra_o1),
        swap_outer(jnp.concatenate([power_i2, extra_i1])),
        swap_y(jnp.concatenate([near_x[:half], mid])),
        swap_x(jnp.concatenate([near_y[half:], mid])),
        swap_core(slab0),
    )
    slab1 = jnp.concatenate([near, near_x, near_y, got_y[:half], got_x[:half]])
    mid_x, mid_y = got_x[half:], got_y[half:]
    power_o3, extra_o2 = got_o[:rows_right], got_o[rows_right:]
    far = jnp.where(inner, power_i2, power_o3)
    extra_o3, got_y, got_x, slab1_other = stage(
        swap_outer(extra_i2),
        swap_y(jnp.concatenate([mid_x[:half], far])),
        swap_x(jnp.concatenate([mid_y[half:], far])),
        swap_core(slab1),
    )
    slab2 = jnp.concatenate([mid, mid_x, mid_y, got_y[:half], got_x[:half]])
    far_x, far_y = got_x[half:], got_y[half:]
    extra_core = jnp.concatenate(
        [extra, extra_o1, jnp.where(inner, extra_i1, extra_o2), jnp.where(inner, extra_i2, extra_o3)]
    )
    extra_other = swap_core(extra_core)
    near_place, mid_place, far_place = places_z(z)
    side_places = [
        (2 * at_z + at_x) * rows_left
        for at_x in (core, 1 - core)
        for at_z in (z, near_place, mid_place, far_place)
    ] + [
        ((y + along) % 2 * 2 + (x + across) % 2) * cols_right
        for along in range(2)
        for across in range(2)
    ]
    new_basis_left, sums, *terms = side(
        jnp.stack(side_places),
        extra_core,
        extra_other,
        right_cols,
        lax.dynamic_slice_in_dim(left_all, (2 * z + core) * rows_left, rows_left, 0),
        power_left,
    )
    got_y, got_x, slab2_other, rotated, new_basis_left, sums = stage(
        swap_y(far_x[:half]),
        swap_x(far_y[half:]),
        swap_core(slab2),
        rotated.astype(BF),
        new_basis_left,
        sums,
    )
    slab3 = jnp.concatenate([far, far_x, far_y, got_y, got_x])
    rotated = turn_over(rotated, straight)
    new_moment_one, new_moment_two, _ = adam_moments(
        rotated.astype(F32), moment_one, moment_two
    )
    slab3_other = swap_core(slab3)
    sums = sums + swap_x(sums) + swap_y(sums) + swap_diagonal(sums)

    terms = [
        swap_to(across, along)(terms[2 * along + across])
        for along in range(2)
        for across in range(2)
    ]
    update = sum(term.astype(F32) for term in terms).astype(BF)

    places = jnp.stack(
        [jnp.where(straight, 0, rows_right) + core * half, straight.astype(jnp.int32)]
    )
    slabs = (slab0, slab0_other, slab1, slab1_other, slab2, slab2_other, slab3, slab3_other)
    fresh = refresh(places, sums, slabs)
    theirs = swap_core(fresh[1])
    new_basis_right = jnp.zeros((rows_right, cols_right), F32)
    new_basis_right = put(new_basis_right, fresh[0], core * half, 0)
    new_basis_right = put(new_basis_right, theirs, (1 - core) * half, 0)
    return (
        update,
        new_moment_one,
        new_moment_two,
        new_stat_left,
        new_stat_right,
        new_basis_left,
        new_basis_right,
    )


def solution(mesh):
    nz, nx, ny, nc = PATTERN
    fits = (mesh.shape["shard"], mesh.shape["tensor"]) == (nz * nx, ny * nc)
    local = local_pattern if fits else local_general
    placed = (
        P("shard", "tensor"),
        P("shard", "tensor"),
        P("shard", "tensor"),
        P("shard", None),
        P("shard", "tensor"),
        P("shard", None),
        P("shard", "tensor"),
    )
    return jax.shard_map(
        local,
        mesh=mesh,
        in_specs=placed,
        out_specs=(
            P("shard", "tensor"),
            P("shard", "tensor"),
            P("shard", "tensor"),
            P("shard", None),
            P("shard", "tensor"),
            P("shard", None),
            P("shard", "tensor"),
        ),
        check_vma=False,
    )
```

```python
import functools
import math

import jax
import jax.numpy as jnp
from jax import lax
from jax.experimental import pallas as pl
from jax.experimental.pallas import tpu as pltpu
from jax.sharding import PartitionSpec as P

D = 768
FF = 3072
NS_STEPS = 2


beta_one = 0.95
beta_two = 0.95
beta_stat = 0.95
correction = 1.0 - 0.95**10
adam_eps = 1e-08
highest = lax.Precision.HIGHEST


def blend_stat(previous, product, divisor):
    return beta_stat * previous + (1.0 - beta_stat) * (product / divisor)


def adam_moments(rotated, moment_one, moment_two):
    first_moment = beta_one * moment_one + (1.0 - beta_one) * rotated
    second_moment = beta_two * moment_two + (1.0 - beta_two) * (rotated * rotated)
    direction = (
        first_moment / correction / (jnp.sqrt(second_moment / correction) + adam_eps)
    ).astype(jnp.bfloat16)
    return (first_moment, second_moment, direction)


def local_general(gradient, moment_one, moment_two, stat_left, stat_right, basis_left, basis_right):
    rows_left = gradient.shape[0]
    rows_right = stat_right.shape[0]
    cols_right = stat_right.shape[1]
    shard_pos = lax.axis_index("shard")
    tensor_pos = lax.axis_index("tensor")
    row_start = shard_pos * rows_left
    grad_cols = lax.all_gather(gradient, "shard", axis=0, tiled=True)
    left_terms = jnp.dot(gradient, grad_cols.T, preferred_element_type=jnp.float32)
    gram_rows = lax.psum(left_terms.astype(jnp.bfloat16), "tensor").astype(jnp.float32)
    new_stat_left = blend_stat(stat_left, gram_rows, FF)
    grad_whole = lax.all_gather(grad_cols, "tensor", axis=1, tiled=True)
    picked = lax.dynamic_slice_in_dim(grad_whole, shard_pos * rows_right, rows_right, 1)
    gram_block = jnp.dot(picked.T, grad_cols, preferred_element_type=jnp.float32)
    new_stat_right = blend_stat(stat_right, gram_block, D)
    basis_all = lax.all_gather(basis_left, "shard", axis=0, tiled=True)
    left_q_all = basis_all / math.sqrt(D)
    left_qb_all = left_q_all.astype(jnp.bfloat16)
    left_qb_own = lax.dynamic_slice_in_dim(left_qb_all, row_start, rows_left, 0)
    left_cols_own = lax.dynamic_slice_in_dim(left_qb_all, row_start, rows_left, 1)
    half_rotated = jnp.dot(left_cols_own.T, grad_cols, preferred_element_type=jnp.float32).astype(
        jnp.bfloat16
    )
    right_q = basis_right / math.sqrt(FF)
    right_qb = right_q.astype(jnp.bfloat16)
    right_cols_b = lax.all_gather(right_qb, "shard", axis=0, tiled=True)
    half_full = lax.all_gather(half_rotated, "tensor", axis=1, tiled=True)
    rotated = jnp.dot(half_full, right_cols_b, preferred_element_type=jnp.float32)
    new_moment_one, new_moment_two, direction = adam_moments(rotated, moment_one, moment_two)
    back_half = jnp.dot(
        left_qb_own,
        lax.all_gather(direction, "shard", axis=0, tiled=True),
        preferred_element_type=jnp.float32,
    ).astype(jnp.bfloat16)
    back_terms = jnp.dot(back_half, right_cols_b.T, preferred_element_type=jnp.float32)
    update = lax.psum_scatter(back_terms, "tensor", scatter_dimension=1, tiled=True).astype(
        jnp.bfloat16
    )
    stat_rows = lax.all_gather(new_stat_right, "tensor", axis=1, tiled=True)
    power_right = jnp.dot(
        stat_rows,
        lax.all_gather(right_q, "shard", axis=0, tiled=True),
        precision=highest,
        preferred_element_type=jnp.float32,
    )
    power_left = jnp.dot(
        new_stat_left, left_q_all, precision=highest, preferred_element_type=jnp.float32
    )
    local_left = jnp.sum(power_left * power_left)
    local_right = jnp.sum(power_right * power_right)
    total_left = lax.psum(local_left, "shard")
    total_right = lax.psum(local_right, ("shard", "tensor"))
    iterate_left = power_left * (math.sqrt(D) / (4.0 * jnp.sqrt(total_left)))
    for iteration in range(NS_STEPS):
        partial_gram = jnp.dot(
            iterate_left.T, iterate_left, precision=highest, preferred_element_type=jnp.float32
        )
        gram_left = lax.psum(partial_gram.astype(jnp.bfloat16), "shard").astype(jnp.float32)
        iterate_left = 1.5 * iterate_left - 0.5 * jnp.dot(
            iterate_left, gram_left, precision=highest, preferred_element_type=jnp.float32
        )
    iterate_right = power_right * (math.sqrt(FF) / (4.0 * jnp.sqrt(total_right)))
    row_ids = shard_pos * rows_right + lax.broadcasted_iota(jnp.int32, (rows_right, cols_right), 0)
    col_ids = tensor_pos * cols_right + lax.broadcasted_iota(jnp.int32, (rows_right, cols_right), 1)
    identity_tile = (row_ids == col_ids).astype(jnp.float32)
    for iteration in range(NS_STEPS):
        rounded_iterate = iterate_right.astype(jnp.bfloat16)
        iterate_rows = lax.all_gather(rounded_iterate, "tensor", axis=1, tiled=True)
        gram_right = lax.psum_scatter(
            jnp.dot(iterate_rows.T, rounded_iterate, preferred_element_type=jnp.float32).astype(
                jnp.bfloat16
            ),
            "shard",
            scatter_dimension=0,
            tiled=True,
        ).astype(jnp.float32)
        mixing = (1.5 * identity_tile - 0.5 * gram_right).astype(jnp.bfloat16)
        iterate_right = jnp.dot(
            iterate_rows,
            lax.all_gather(mixing, "shard", axis=0, tiled=True),
            preferred_element_type=jnp.float32,
        )
    return (
        update,
        new_moment_one,
        new_moment_two,
        new_stat_left,
        new_stat_right,
        iterate_left * math.sqrt(D),
        iterate_right * math.sqrt(FF),
    )


BF = jnp.bfloat16
F32 = jnp.float32
AXES = ("shard", "tensor")
PATTERN = (4, 2, 2, 2)


def dot_nn(a, b):
    return jnp.dot(a, b, preferred_element_type=F32)


def dot_nt(a, b):
    return lax.dot_general(a, b, (((1,), (1,)), ((), ())), preferred_element_type=F32)


def dot_tn(a, b):
    return lax.dot_general(a, b, (((0,), (0,)), ((), ())), preferred_element_type=F32)


def pairs(move):
    nz, nx, ny, nc = PATTERN
    out = []
    for z in range(nz):
        for x in range(nx):
            for y in range(ny):
                for c in range(nc):
                    to = move(z, x, y, c)
                    if 0 <= to[0] < nz:
                        source = ((z * nx + x) * ny + y) * nc + c
                        target = ((to[0] * nx + to[1]) * ny + to[2]) * nc + to[3]
                        out.append((source, target))
    return out


def swap_x(a):
    return lax.ppermute(a, AXES, pairs(lambda z, x, y, c: (z, 1 - x, y, c)))


def swap_y(a):
    return lax.ppermute(a, AXES, pairs(lambda z, x, y, c: (z, x, 1 - y, c)))


def swap_core(a):
    return lax.ppermute(a, AXES, pairs(lambda z, x, y, c: (z, x, y, 1 - c)))


def swap_outer(a):
    return lax.ppermute(a, AXES, pairs(lambda z, x, y, c: (z + 1 - 2 * (z % 2), x, y, c)))


def swap_inner(a):
    return lax.ppermute(a, AXES, pairs(lambda z, x, y, c: (3 - z if 0 < z < 3 else -1, x, y, c)))


def turn_over(a, straight):
    crossed = pairs(lambda z, x, y, c: (z if x != c else -1, 1 - x, y, 1 - c))
    return jnp.where(straight, a, lax.ppermute(a, AXES, crossed))


def stage(*parts):
    return lax.optimization_barrier(parts)


def swap_diagonal(a):
    return lax.ppermute(a, AXES, pairs(lambda z, x, y, c: (z, 1 - x, 1 - y, c)))


def swap_to(across, along):
    return lambda a: lax.ppermute(
        a, AXES, pairs(lambda z, x, y, c: (z, c, (y + along) % 2, (x + across) % 2))
    )


def places_z(z):
    return z + 1 - 2 * (z % 2), jnp.where(z < 2, 2, 1), jnp.where(z < 2, 3, 0)


def in_order(z, own, near, mid, far):
    whole = jnp.zeros((4,) + own.shape, own.dtype)
    for block, place in zip((own, near, mid, far), (z,) + places_z(z)):
        whole = lax.dynamic_update_slice(whole, block[None], (place,) + (0,) * own.ndim)
    return whole


def ordered_pair(ahead, first, second):
    both = jnp.concatenate([first[None], second[None]])
    return jnp.where(ahead, both, jnp.concatenate([second[None], first[None]]))


def put(whole, part, *start):
    return lax.dynamic_update_slice(whole, part, start)


def interleave(core, mine, theirs):
    rows, cols = mine.shape[1:]
    whole = jnp.zeros((4, 2, rows, cols), mine.dtype)
    whole = put(whole, mine[:, None], 0, core, 0, 0)
    whole = put(whole, theirs[:, None], 0, 1 - core, 0, 0)
    return whole.reshape(8 * rows, cols)


def refresh_kernel(place_ref, sum_ref, *refs):
    stacks = refs[:10]
    out_ref, whole, inner, held, total, first, sems = refs[10:]
    count, size = held.shape
    tall = size // 4
    half = size // 8

    def copy(k, i):
        slot, other = k // 2, k % 2
        stack, row = slot, 0
        rows = half if i < 3 else half // 2
        if 0 < i < 3:
            row = i * half if slot == 0 else (1 + i) * half + (i - 2) * (half // 2)
        if i >= 3:
            stack = slot + 1
            row = (i - 3) * (half // 2)
            if slot < 3:
                row = half if i == 4 else 2 * half + half // 2
        source = stacks[2 * stack + other].at[pl.ds(row, rows), :]
        start = k * half + (half // 2 if i == 4 else 0)
        target = whole.at[pl.ds(start, rows), pl.ds(min(i, 3) * tall, tall)]
        return pltpu.make_async_copy(source, target, sems.at[k, i])

    def arrived(j):
        for k in (2 * j, 2 * j + 1):
            for i in range(5):
                copy(k, i).wait()

    def span_of(j):
        return pl.ds(pl.multiple_of(j * tall, tall), tall)

    for k in range(8):
        for i in range(5):
            copy(k, i).start()
    squares = size / (16.0 * sum_ref[...])
    square = squares[0, 0]
    last = (math.sqrt(size) * jnp.sqrt(squares))[0, 0]
    arrived(0)
    held[...] = whole[pl.ds(pl.multiple_of(place_ref[0], 16), count), :]
    total[...] = held[...].astype(F32)

    def one_pass(i, carry):
        def towards(j, carry):
            @pl.when(i == 0)
            def _():
                for k in range(1, 4):
                    pl.when(j == k)(functools.partial(arrived, k))

            inner[:, span_of(j)] = dot_nt(held[...], whole[span_of(j), :]).astype(BF)
            return carry

        lax.fori_loop(0, 4, towards, 0)
        keep = jnp.where(i == 1, 0.0, 1.5)
        take = jnp.where(i == 1, square, -0.5 * square)

        def back(j, carry):
            span = span_of(j)
            value = keep * total[:, span] + take * dot_nn(inner[...], whole[:, span])
            total[:, span] = value
            held[:, span] = value.astype(BF)

            @pl.when(i == 0)
            def _():
                first[:, span] = value

            return carry

        lax.fori_loop(0, jnp.where(i == 3, 2, 4), back, 0)
        return carry

    lax.fori_loop(0, 4, one_pass, 0)
    for k in range(2):
        span = slice(k * tall, (k + 1) * tall)
        place = jnp.where(place_ref[1] == 1, k, 1 - k)
        out_ref[place] = last * (1.5 * first[:, span] - 0.5 * total[:, span])


def refresh(places, sums, stacks):
    tall = stacks[0].shape[1]
    size = 4 * tall
    count = size // 16
    in_vmem = pl.BlockSpec(memory_space=pltpu.VMEM)
    in_smem = pl.BlockSpec(memory_space=pltpu.SMEM)
    return pl.pallas_call(
        refresh_kernel,
        out_shape=jax.ShapeDtypeStruct((2, count, tall), F32),
        in_specs=[in_smem] + [in_vmem] + [pl.BlockSpec(memory_space=pl.ANY)] * 10,
        out_specs=in_vmem,
        scratch_shapes=[
            pltpu.VMEM((size, size), BF),
            pltpu.VMEM((count, size), BF),
            pltpu.VMEM((count, size), BF),
            pltpu.VMEM((count, size), F32),
            pltpu.VMEM((count, size), F32),
            pltpu.SemaphoreType.DMA((8, 5)),
        ],
        compiler_params=pltpu.CompilerParams(vmem_limit_bytes=56 * 2**20),
        cost_estimate=pl.CostEstimate(
            flops=15 * count * size * size, bytes_accessed=2 * size * size, transcendentals=0
        ),
    )(places, sums, *stacks)


def side_kernel(place_ref, core_ref, other_ref, cols_ref, rows_ref, power_ref, *refs):
    basis_ref, sum_ref, terms = refs[0], refs[1], refs[2:6]
    power, direction, cols, sems = refs[6:]
    rows, size = power_ref.shape
    step = core_ref.shape[0] // 4

    def copy(k):
        block = pl.ds(pl.multiple_of(place_ref[8 + k], 16), size)
        return pltpu.make_async_copy(cols_ref.at[block, :], cols.at[k], sems.at[k])

    for k in range(4):
        copy(k).start()
    total = jnp.zeros((step - 2 * rows, size), F32)
    for k in range(8):
        source = (core_ref, other_ref)[k // 4]
        start = (k % 4) * step
        place = pl.ds(pl.multiple_of(place_ref[k], 16), rows)
        direction[place, :] = source[start : start + rows, :]
        power[k * rows : (k + 1) * rows, :] = source[start + rows : start + 2 * rows, :]
        total += source[start + 2 * rows : start + step, :].astype(F32)
    sum_ref[...] = jnp.full(sum_ref.shape, jnp.sum(total))
    squares = jnp.zeros((rows, size), F32)
    for k in range(8):
        squares += jnp.square(power[k * rows : (k + 1) * rows, :].astype(F32))
    square = size / (16.0 * jnp.sum(squares))
    keep = power_ref[...]
    value = keep
    for turn in range(4):
        across = dot_nt(value.astype(BF), power[...]).astype(BF)
        moved = square * dot_nn(across, power[...])
        value = moved if turn == 1 else 1.5 * value - 0.5 * moved
        if turn == 0:
            keep = value
    scale = math.sqrt(size) * jnp.sqrt(jnp.full((rows, size), square))
    basis_ref[...] = scale * (1.5 * keep - 0.5 * value)
    back_half = dot_nn(rows_ref[...], direction[...]).astype(BF)
    for k in range(4):
        copy(k).wait()
        terms[k][...] = dot_nt(back_half, cols[k]).astype(BF)


def side(places, extra_core, extra_other, right_cols, left_rows, power_left):
    rows, size = power_left.shape
    in_vmem = pl.BlockSpec(memory_space=pltpu.VMEM)
    term = jax.ShapeDtypeStruct((rows, size), BF)
    sums = jax.ShapeDtypeStruct((8, 128), F32)
    return pl.pallas_call(
        side_kernel,
        out_shape=[jax.ShapeDtypeStruct((rows, size), F32), sums] + [term] * 4,
        in_specs=[pl.BlockSpec(memory_space=pltpu.SMEM)]
        + [in_vmem] * 2
        + [pl.BlockSpec(memory_space=pl.ANY)]
        + [in_vmem] * 2,
        out_specs=[in_vmem] * 6,
        scratch_shapes=[
            pltpu.VMEM((size, size), BF),
            pltpu.VMEM((size, size), BF),
            pltpu.VMEM((4, size, size), BF),
            pltpu.SemaphoreType.DMA((4,)),
        ],
        compiler_params=pltpu.CompilerParams(vmem_limit_bytes=56 * 2**20),
        cost_estimate=pl.CostEstimate(
            flops=26 * rows * size * size, bytes_accessed=12 * size * size, transcendentals=0
        ),
    )(places, extra_core, extra_other, right_cols, left_rows, power_left)


def partial_squares(a):
    squares = jnp.square(a.astype(F32)).reshape(-1, 16, a.shape[1])
    return jnp.sum(squares, axis=0).astype(BF)


def after(block, *others):
    return lax.optimization_barrier((block, *others))[0]


def local_pattern(gradient, moment_one, moment_two, stat_left, stat_right, basis_left, basis_right):
    rows_left = gradient.shape[0]
    rows_right = stat_right.shape[0]
    cols_right = stat_right.shape[1]
    shard_pos = lax.axis_index("shard")
    tensor_pos = lax.axis_index("tensor")
    z, x = shard_pos // 2, shard_pos % 2
    y, core = tensor_pos // 2, tensor_pos % 2
    straight = x == core
    inner = (z == 1) | (z == 2)
    half = rows_right // 2

    left_b = (basis_left / math.sqrt(D)).astype(BF)
    right_b = (basis_right / math.sqrt(FF)).astype(BF)
    stat_b = stat_right.astype(BF)
    part_left = rows_left // 2
    small = jnp.concatenate(
        [gradient, lax.dynamic_slice_in_dim(left_b, y * part_left, part_left, 0)]
    )
    rows_small = small.shape[0]

    turned, small_o1, small_i1, moment_one, moment_two, stat_left = stage(
        turn_over(right_b, straight),
        swap_outer(small),
        swap_inner(small),
        moment_one,
        moment_two,
        stat_left,
    )
    early = jnp.concatenate([moment_one, moment_two, stat_left]).astype(BF)
    got_i, got_o, stat_y, stat_x, early = stage(
        swap_inner(jnp.concatenate([turned, small_o1])),
        swap_outer(jnp.concatenate([turned, small_i1])),
        swap_y(stat_b),
        swap_x(stat_b),
        turn_over(early, straight),
    )
    turned_o1, small_o2 = got_o[:rows_right], got_o[rows_right:]
    turned_i1, small_i2 = got_i[:rows_right], got_i[rows_right:]
    small_1 = ordered_pair(z % 2 == 0, small, small_o1).reshape(2 * rows_small, cols_right)
    to_x = jnp.concatenate([stat_y[half:], small_1])
    to_y = jnp.concatenate([stat_x[:half], small_1])
    got_x, got_y, got_o, turned_i2 = stage(
        swap_x(to_x),
        swap_y(to_y),
        swap_outer(after(jnp.concatenate([turned_i1, small_i2]), to_x, to_y)),
        swap_inner(after(turned_o1, to_x, to_y)),
    )
    turned_o2, small_o3 = got_o[:rows_right], got_o[rows_right:]
    small_2 = ordered_pair(
        z < 2, jnp.where(inner, small_i1, small_o2), jnp.where(inner, small_i2, small_o3)
    ).reshape(2 * rows_small, cols_right)
    stat_xy = jnp.concatenate([got_y[:half], got_x[:half]])
    small_1x, small_1y = got_x[half:], got_y[half:]
    stat_keep = [jnp.where(straight, stat_b, stat_x), jnp.where(straight, stat_y, stat_xy)]
    stat_send = [jnp.where(straight, stat_x, stat_b), jnp.where(straight, stat_xy, stat_y)]
    turned_o3, got_x, got_y, stat_got = stage(
        swap_outer(turned_i2),
        swap_x(jnp.concatenate([small_1y[rows_small:], small_2])),
        swap_y(jnp.concatenate([small_1x[:rows_small], small_2])),
        swap_core(jnp.concatenate(stat_send)),
    )
    small_1xy = jnp.concatenate([got_y[:rows_small], got_x[:rows_small]])
    small_2x, small_2y = got_x[rows_small:], got_y[rows_small:]
    turned_z = in_order(
        z,
        turned,
        turned_o1,
        jnp.where(inner, turned_i1, turned_o2),
        jnp.where(inner, turned_i2, turned_o3),
    )
    stat_rows = jnp.zeros((rows_right, 4 * cols_right), BF)
    stat_rows = put(stat_rows, stat_keep[0], 0, (2 * y + core) * cols_right)
    stat_rows = put(stat_rows, stat_keep[1], 0, (2 - 2 * y + core) * cols_right)
    stat_rows = put(stat_rows, stat_got[:rows_right], 0, (2 * y + 1 - core) * cols_right)
    stat_rows = put(stat_rows, stat_got[rows_right:], 0, (3 - 2 * y - core) * cols_right)
    small_2hi, small_2lo, turned_got = stage(
        swap_x(small_2y[rows_small:]), swap_y(small_2x[:rows_small]), swap_core(turned_z)
    )
    right_cols = interleave(core, turned_z, turned_got)
    grad_core = jnp.zeros((4, 2, rows_left, 2 * cols_right), BF)
    left_all = jnp.zeros((4, 2, 2, part_left, cols_right), BF)
    small_2xy = jnp.concatenate([small_2lo, small_2hi])
    low = 2 * (z // 2)
    for block, at_z, at_x, at_y in (
        (small_1, low, x, y),
        (small_1x, low, 1 - x, y),
        (small_1y, low, x, 1 - y),
        (small_1xy, low, 1 - x, 1 - y),
        (small_2, 2 - low, x, y),
        (small_2x, 2 - low, 1 - x, y),
        (small_2y, 2 - low, x, 1 - y),
        (small_2xy, 2 - low, 1 - x, 1 - y),
    ):
        block = block.reshape(2, 1, rows_small, cols_right)
        grad_core = put(grad_core, block[:, :, :rows_left], at_z, at_x, 0, at_y * cols_right)
        left_all = put(left_all, block[:, :, None, rows_left:], at_z, at_x, at_y, 0, 0)
    grad_core = grad_core.reshape(8 * rows_left, 2 * cols_right)
    left_all = left_all.reshape(8 * rows_left, cols_right)

    grad_other = swap_core(grad_core)
    rows_core = lax.dynamic_slice_in_dim(
        right_cols.reshape(2, 2, cols_right, cols_right), core, 1, 1
    ).reshape(2 * cols_right, cols_right)
    carried = dot_nn(grad_core, rows_core)
    carried = (carried + swap_core(carried.astype(BF)).astype(F32)).astype(BF)

    def grad_block(at_x):
        start = (z // 2) * cols_right + at_x * rows_right
        ours = lax.dynamic_slice_in_dim(grad_core, start, rows_right, 1)
        other = lax.dynamic_slice_in_dim(grad_other, start, rows_right, 1)
        return jnp.where(z % 2 == core, ours, other)

    gram = 0.0
    for part in (grad_core, grad_other):
        rows = lax.dynamic_slice_in_dim(part, 2 * z * rows_left, 2 * rows_left, 0)
        gram = gram + dot_nt(rows, part)
    gram = gram.reshape(2, rows_left, cols_right)
    gram_own = lax.dynamic_index_in_dim(gram, x, 0, False)
    gram_here = lax.dynamic_index_in_dim(gram, core, 0, False)
    share = (1.0 - beta_stat) / D
    picked = grad_block(core)
    power = beta_stat * dot_nn(stat_rows, right_cols) + share * dot_tn(picked, carried)
    power, carried = stage(power.astype(BF), carried)

    here = (2 * z + core) * rows_left
    early = early.astype(F32)
    left_cols = lax.dynamic_slice_in_dim(left_all, here, rows_left, 1)
    rotated = dot_tn(left_cols, carried)
    _, _, direction = adam_moments(rotated, early[:rows_left], early[rows_left : 2 * rows_left])
    stat_t = blend_stat(early[2 * rows_left :], gram_here, FF)
    left_t = dot_nn(stat_t.astype(BF), left_all).astype(BF)
    extra = jnp.concatenate([direction, left_t, partial_squares(power)])

    own_grad = lax.dynamic_slice_in_dim(grad_core, y * cols_right, cols_right, 1)
    new_stat_right = blend_stat(stat_right, dot_tn(grad_block(x), own_grad), D)
    new_stat_left = blend_stat(stat_left, gram_own, FF)
    power_left = dot_nn(new_stat_left.astype(BF), left_all)

    power_x, power_y, near, power_i1, extra = stage(
        swap_x(power),
        swap_y(power),
        swap_outer(power),
        swap_inner(power),
        extra,
    )
    left_rows = lax.dynamic_slice_in_dim(left_all, here, rows_left, 0)
    to_x = jnp.concatenate([power_y[half:], near])
    to_y = jnp.concatenate([power_x[:half], near])
    got_x, got_y, got_o, got_i, new_stat_right, new_stat_left, power_left, left_rows = stage(
        swap_x(to_x),
        swap_y(to_y),
        swap_outer(after(jnp.concatenate([power_i1, extra]), to_x, to_y)),
        swap_inner(after(jnp.concatenate([near, extra]), to_x, to_y)),
        new_stat_right,
        new_stat_left,
        power_left,
        left_rows,
    )
    stack0 = jnp.concatenate([power, power_x, power_y])
    stack1 = jnp.concatenate([near, got_x, got_y])
    near_x, near_y = got_x[half:], got_y[half:]
    power_o2, extra_o1 = got_o[:rows_right], got_o[rows_right:]
    power_i2, extra_i1 = got_i[:rows_right], got_i[rows_right:]
    mid = jnp.where(inner, power_i1, power_o2)
    to_x = jnp.concatenate([near_y[half:], mid])
    to_y = jnp.concatenate([near_x[:half], mid])
    got_x, got_y, got_o, extra_i2, other0 = stage(
        swap_x(to_x),
        swap_y(to_y),
        swap_outer(after(jnp.concatenate([power_i2, extra_i1]), to_x, to_y)),
        swap_inner(after(extra_o1, to_x, to_y)),
        swap_core(stack0),
    )
    stack2 = jnp.concatenate([mid, got_x, got_y])
    mid_x, mid_y = got_x[half:], got_y[half:]
    power_o3, extra_o2 = got_o[:rows_right], got_o[rows_right:]
    far = jnp.where(inner, power_i2, power_o3)
    to_x = jnp.concatenate([mid_y[half:], far])
    to_y = jnp.concatenate([mid_x[:half], far])
    got_x, got_y, extra_o3, other1, rotated = stage(
        swap_x(to_x),
        swap_y(to_y),
        swap_outer(after(extra_i2, to_x, to_y)),
        swap_core(stack1),
        turn_over(rotated.astype(BF), straight),
    )
    stack3 = jnp.concatenate([far, got_x, got_y])
    far_x, far_y = got_x[half:], got_y[half:]
    extra_core = jnp.concatenate(
        [extra, extra_o1, jnp.where(inner, extra_i1, extra_o2), jnp.where(inner, extra_i2, extra_o3)]
    )
    near_place, mid_place, far_place = places_z(z)
    side_places = [
        (2 * at_z + at_x) * rows_left
        for at_x in (core, 1 - core)
        for at_z in (z, near_place, mid_place, far_place)
    ] + [
        ((y + along) % 2 * 2 + (x + across) % 2) * cols_right
        for along in range(2)
        for across in range(2)
    ]
    new_basis_left, sums, *terms = side(
        jnp.stack(side_places),
        extra_core,
        swap_core(extra_core),
        right_cols,
        left_rows,
        power_left,
    )
    got_y, got_x, other2, new_basis_left, sums = stage(
        swap_y(far_x[:half]),
        swap_x(far_y[half:]),
        swap_core(stack2),
        new_basis_left,
        sums,
    )
    stack4 = jnp.concatenate([got_y, got_x])
    other3, other4 = swap_core(stack3), swap_core(stack4)
    sums = sums + swap_x(sums) + swap_y(sums) + swap_diagonal(sums)
    new_moment_one, new_moment_two, _ = adam_moments(
        rotated.astype(F32), moment_one, moment_two
    )

    terms = [
        swap_to(across, along)(terms[2 * along + across])
        for along in range(2)
        for across in range(2)
    ]
    update = sum(term.astype(F32) for term in terms).astype(BF)

    places = jnp.stack(
        [jnp.where(straight, 0, rows_right) + core * half, straight.astype(jnp.int32)]
    )
    stacks = (
        stack0, other0, stack1, other1, stack2, other2, stack3, other3, stack4, other4
    )
    fresh = refresh(places, sums, stacks)
    theirs = swap_core(fresh[1])
    new_basis_right = jnp.zeros((rows_right, cols_right), F32)
    new_basis_right = put(new_basis_right, fresh[0], core * half, 0)
    new_basis_right = put(new_basis_right, theirs, (1 - core) * half, 0)
    return (
        update,
        new_moment_one,
        new_moment_two,
        new_stat_left,
        new_stat_right,
        new_basis_left,
        new_basis_right,
    )


def solution(mesh):
    nz, nx, ny, nc = PATTERN
    fits = (mesh.shape["shard"], mesh.shape["tensor"]) == (nz * nx, ny * nc)
    local = local_pattern if fits else local_general
    placed = (
        P("shard", "tensor"),
        P("shard", "tensor"),
        P("shard", "tensor"),
        P("shard", None),
        P("shard", "tensor"),
        P("shard", None),
        P("shard", "tensor"),
    )
    return jax.shard_map(
        local,
        mesh=mesh,
        in_specs=placed,
        out_specs=(
            P("shard", "tensor"),
            P("shard", "tensor"),
            P("shard", "tensor"),
            P("shard", None),
            P("shard", "tensor"),
            P("shard", None),
            P("shard", "tensor"),
        ),
        check_vma=False,
    )
```

```python
import functools
import math

import jax
import jax.numpy as jnp
from jax import lax
from jax.experimental import pallas as pl
from jax.experimental.pallas import tpu as pltpu
from jax.sharding import PartitionSpec as P

D = 768
FF = 3072
NS_STEPS = 2


beta_one = 0.95
beta_two = 0.95
beta_stat = 0.95
correction = 1.0 - 0.95**10
adam_eps = 1e-08
highest = lax.Precision.HIGHEST


def blend_stat(previous, product, divisor):
    return beta_stat * previous + (1.0 - beta_stat) * (product / divisor)


def adam_moments(rotated, moment_one, moment_two):
    first_moment = beta_one * moment_one + (1.0 - beta_one) * rotated
    second_moment = beta_two * moment_two + (1.0 - beta_two) * (rotated * rotated)
    direction = (
        first_moment / correction / (jnp.sqrt(second_moment / correction) + adam_eps)
    ).astype(jnp.bfloat16)
    return (first_moment, second_moment, direction)


def local_general(gradient, moment_one, moment_two, stat_left, stat_right, basis_left, basis_right):
    rows_left = gradient.shape[0]
    rows_right = stat_right.shape[0]
    cols_right = stat_right.shape[1]
    shard_pos = lax.axis_index("shard")
    tensor_pos = lax.axis_index("tensor")
    row_start = shard_pos * rows_left
    grad_cols = lax.all_gather(gradient, "shard", axis=0, tiled=True)
    left_terms = jnp.dot(gradient, grad_cols.T, preferred_element_type=jnp.float32)
    gram_rows = lax.psum(left_terms.astype(jnp.bfloat16), "tensor").astype(jnp.float32)
    new_stat_left = blend_stat(stat_left, gram_rows, FF)
    grad_whole = lax.all_gather(grad_cols, "tensor", axis=1, tiled=True)
    picked = lax.dynamic_slice_in_dim(grad_whole, shard_pos * rows_right, rows_right, 1)
    gram_block = jnp.dot(picked.T, grad_cols, preferred_element_type=jnp.float32)
    new_stat_right = blend_stat(stat_right, gram_block, D)
    basis_all = lax.all_gather(basis_left, "shard", axis=0, tiled=True)
    left_q_all = basis_all / math.sqrt(D)
    left_qb_all = left_q_all.astype(jnp.bfloat16)
    left_qb_own = lax.dynamic_slice_in_dim(left_qb_all, row_start, rows_left, 0)
    left_cols_own = lax.dynamic_slice_in_dim(left_qb_all, row_start, rows_left, 1)
    half_rotated = jnp.dot(left_cols_own.T, grad_cols, preferred_element_type=jnp.float32).astype(
        jnp.bfloat16
    )
    right_q = basis_right / math.sqrt(FF)
    right_qb = right_q.astype(jnp.bfloat16)
    right_cols_b = lax.all_gather(right_qb, "shard", axis=0, tiled=True)
    half_full = lax.all_gather(half_rotated, "tensor", axis=1, tiled=True)
    rotated = jnp.dot(half_full, right_cols_b, preferred_element_type=jnp.float32)
    new_moment_one, new_moment_two, direction = adam_moments(rotated, moment_one, moment_two)
    back_half = jnp.dot(
        left_qb_own,
        lax.all_gather(direction, "shard", axis=0, tiled=True),
        preferred_element_type=jnp.float32,
    ).astype(jnp.bfloat16)
    back_terms = jnp.dot(back_half, right_cols_b.T, preferred_element_type=jnp.float32)
    update = lax.psum_scatter(back_terms, "tensor", scatter_dimension=1, tiled=True).astype(
        jnp.bfloat16
    )
    stat_rows = lax.all_gather(new_stat_right, "tensor", axis=1, tiled=True)
    power_right = jnp.dot(
        stat_rows,
        lax.all_gather(right_q, "shard", axis=0, tiled=True),
        precision=highest,
        preferred_element_type=jnp.float32,
    )
    power_left = jnp.dot(
        new_stat_left, left_q_all, precision=highest, preferred_element_type=jnp.float32
    )
    local_left = jnp.sum(power_left * power_left)
    local_right = jnp.sum(power_right * power_right)
    total_left = lax.psum(local_left, "shard")
    total_right = lax.psum(local_right, ("shard", "tensor"))
    iterate_left = power_left * (math.sqrt(D) / (4.0 * jnp.sqrt(total_left)))
    for iteration in range(NS_STEPS):
        partial_gram = jnp.dot(
            iterate_left.T, iterate_left, precision=highest, preferred_element_type=jnp.float32
        )
        gram_left = lax.psum(partial_gram.astype(jnp.bfloat16), "shard").astype(jnp.float32)
        iterate_left = 1.5 * iterate_left - 0.5 * jnp.dot(
            iterate_left, gram_left, precision=highest, preferred_element_type=jnp.float32
        )
    iterate_right = power_right * (math.sqrt(FF) / (4.0 * jnp.sqrt(total_right)))
    row_ids = shard_pos * rows_right + lax.broadcasted_iota(jnp.int32, (rows_right, cols_right), 0)
    col_ids = tensor_pos * cols_right + lax.broadcasted_iota(jnp.int32, (rows_right, cols_right), 1)
    identity_tile = (row_ids == col_ids).astype(jnp.float32)
    for iteration in range(NS_STEPS):
        rounded_iterate = iterate_right.astype(jnp.bfloat16)
        iterate_rows = lax.all_gather(rounded_iterate, "tensor", axis=1, tiled=True)
        gram_right = lax.psum_scatter(
            jnp.dot(iterate_rows.T, rounded_iterate, preferred_element_type=jnp.float32).astype(
                jnp.bfloat16
            ),
            "shard",
            scatter_dimension=0,
            tiled=True,
        ).astype(jnp.float32)
        mixing = (1.5 * identity_tile - 0.5 * gram_right).astype(jnp.bfloat16)
        iterate_right = jnp.dot(
            iterate_rows,
            lax.all_gather(mixing, "shard", axis=0, tiled=True),
            preferred_element_type=jnp.float32,
        )
    return (
        update,
        new_moment_one,
        new_moment_two,
        new_stat_left,
        new_stat_right,
        iterate_left * math.sqrt(D),
        iterate_right * math.sqrt(FF),
    )


BF = jnp.bfloat16
F32 = jnp.float32
AXES = ("shard", "tensor")
PATTERN = (4, 2, 2, 2)


def dot_nn(a, b):
    return jnp.dot(a, b, preferred_element_type=F32)


def dot_nt(a, b):
    return lax.dot_general(a, b, (((1,), (1,)), ((), ())), preferred_element_type=F32)


def dot_tn(a, b):
    return lax.dot_general(a, b, (((0,), (0,)), ((), ())), preferred_element_type=F32)


def pairs(move):
    nz, nx, ny, nc = PATTERN
    out = []
    for z in range(nz):
        for x in range(nx):
            for y in range(ny):
                for c in range(nc):
                    to = move(z, x, y, c)
                    if 0 <= to[0] < nz:
                        source = ((z * nx + x) * ny + y) * nc + c
                        target = ((to[0] * nx + to[1]) * ny + to[2]) * nc + to[3]
                        out.append((source, target))
    return out


def swap_x(a):
    return lax.ppermute(a, AXES, pairs(lambda z, x, y, c: (z, 1 - x, y, c)))


def swap_y(a):
    return lax.ppermute(a, AXES, pairs(lambda z, x, y, c: (z, x, 1 - y, c)))


def swap_core(a):
    return lax.ppermute(a, AXES, pairs(lambda z, x, y, c: (z, x, y, 1 - c)))


def swap_outer(a):
    return lax.ppermute(a, AXES, pairs(lambda z, x, y, c: (z + 1 - 2 * (z % 2), x, y, c)))


def swap_inner(a):
    return lax.ppermute(a, AXES, pairs(lambda z, x, y, c: (3 - z if 0 < z < 3 else -1, x, y, c)))


def turn_over(a, straight):
    crossed = pairs(lambda z, x, y, c: (z if x != c else -1, 1 - x, y, 1 - c))
    return jnp.where(straight, a, lax.ppermute(a, AXES, crossed))


def stage(*parts):
    return lax.optimization_barrier(parts)


def exchange(*pairs_of):
    blocks = lax.optimization_barrier(tuple(block for _, block in pairs_of))
    return [send(block) for (send, _), block in zip(pairs_of, blocks)]


def swap_diagonal(a):
    return lax.ppermute(a, AXES, pairs(lambda z, x, y, c: (z, 1 - x, 1 - y, c)))


def swap_to(across, along):
    return lambda a: lax.ppermute(
        a, AXES, pairs(lambda z, x, y, c: (z, c, (y + along) % 2, (x + across) % 2))
    )


def places_z(z):
    return z + 1 - 2 * (z % 2), jnp.where(z < 2, 2, 1), jnp.where(z < 2, 3, 0)


def in_order(z, own, near, mid, far):
    whole = jnp.zeros((4,) + own.shape, own.dtype)
    for block, place in zip((own, near, mid, far), (z,) + places_z(z)):
        whole = lax.dynamic_update_slice(whole, block[None], (place,) + (0,) * own.ndim)
    return whole


def ordered_pair(ahead, first, second):
    both = jnp.concatenate([first[None], second[None]])
    return jnp.where(ahead, both, jnp.concatenate([second[None], first[None]]))


def put(whole, part, *start):
    return lax.dynamic_update_slice(whole, part, start)


def interleave(core, mine, theirs):
    rows, cols = mine.shape[1:]
    whole = jnp.zeros((4, 2, rows, cols), mine.dtype)
    whole = put(whole, mine[:, None], 0, core, 0, 0)
    whole = put(whole, theirs[:, None], 0, 1 - core, 0, 0)
    return whole.reshape(8 * rows, cols)


def refresh_kernel(place_ref, *refs):
    sums, stacks, (mine_ref, theirs_ref) = refs[:4], refs[4:14], refs[14:16]
    whole, inner, held, total, first, sems = refs[16:]
    count, size = held.shape
    tall = size // 4
    wide = size // 2
    half = size // 8

    def copy(k, i):
        slot, other = k // 2, k % 2
        rows = half if i < 3 else half // 2
        if i < 3:
            stack = slot
            row = i * half + (i * (half // 2) if slot in (1, 2) else 0)
        elif slot < 2:
            stack = slot + 1
            row = half if i == 4 else 2 * half + half // 2
        else:
            stack = 4
            row = (i - 3) * half + (slot - 2) * (half // 2)
        source = stacks[2 * stack + other].at[pl.ds(row, rows), :]
        start = k * half + (half // 2 if i == 4 else 0)
        target = whole.at[pl.ds(start, rows), pl.ds(min(i, 3) * tall, tall)]
        return pltpu.make_async_copy(source, target, sems.at[k, i])

    def arrived(j):
        for k in (2 * j, 2 * j + 1):
            for i in range(5):
                copy(k, i).wait()

    spans = [slice(0, wide), slice(wide, size)]

    for k in range(8):
        for i in range(5):
            copy(k, i).start()
    squares = size / (16.0 * sum(part[...] for part in sums))
    square = squares[0, 0]
    last = (math.sqrt(size) * jnp.sqrt(squares))[0, 0]
    arrived(0)
    held[...] = whole[pl.ds(pl.multiple_of(place_ref[0], 16), count), :]
    total[...] = held[...].astype(F32)

    for j in range(4):
        if j:
            arrived(j)
        rows = slice(j * tall, (j + 1) * tall)
        inner[:, rows] = dot_nt(held[...], whole[rows, :]).astype(BF)

    def one_pass(i, carry):
        @pl.when(i > 0)
        def _():
            for span in spans:
                inner[:, span] = dot_nt(held[...], whole[span, :]).astype(BF)

        keep = jnp.where(i == 1, 0.0, 1.5)
        take = jnp.where(i == 1, square, -0.5 * square)

        def back(span):
            value = keep * total[:, span] + take * dot_nn(inner[...], whole[:, span])
            total[:, span] = value
            held[:, span] = value.astype(BF)

            @pl.when(i == 0)
            def _():
                first[:, span] = value

        back(spans[0])
        pl.when(i < 3)(functools.partial(back, spans[1]))
        return carry

    lax.fori_loop(0, 4, one_pass, 0)
    for k, flag in ((0, 1), (1, 0)):
        span = slice(k * tall, (k + 1) * tall)
        value = last * (1.5 * first[:, span] - 0.5 * total[:, span])

        @pl.when(place_ref[1] == flag)
        def _():
            mine_ref[...] = value

        @pl.when(place_ref[1] != flag)
        def _():
            theirs_ref[...] = value


def refresh(places, sums, stacks):
    tall = stacks[0].shape[1]
    size = 4 * tall
    count = size // 16
    in_vmem = pl.BlockSpec(memory_space=pltpu.VMEM)
    in_smem = pl.BlockSpec(memory_space=pltpu.SMEM)
    return pl.pallas_call(
        refresh_kernel,
        out_shape=[jax.ShapeDtypeStruct((count, tall), F32)] * 2,
        in_specs=[in_smem] + [in_vmem] * 4 + [pl.BlockSpec(memory_space=pl.ANY)] * 10,
        out_specs=[in_vmem] * 2,
        scratch_shapes=[
            pltpu.VMEM((size, size), BF),
            pltpu.VMEM((count, size), BF),
            pltpu.VMEM((count, size), BF),
            pltpu.VMEM((count, size), F32),
            pltpu.VMEM((count, size), F32),
            pltpu.SemaphoreType.DMA((8, 5)),
        ],
        compiler_params=pltpu.CompilerParams(vmem_limit_bytes=56 * 2**20),
        cost_estimate=pl.CostEstimate(
            flops=15 * count * size * size, bytes_accessed=2 * size * size, transcendentals=0
        ),
    )(places, *sums, *stacks)


def side_kernel(place_ref, core_ref, other_ref, cols_ref, rows_ref, power_ref, *refs):
    basis_ref, sum_ref, terms = refs[0], refs[1], refs[2:6]
    power, direction, cols, sems = refs[6:]
    rows, size = power_ref.shape
    step = core_ref.shape[0] // 4

    def copy(k):
        block = pl.ds(pl.multiple_of(place_ref[8 + k], 16), size)
        return pltpu.make_async_copy(cols_ref.at[block, :], cols.at[k], sems.at[k])

    for k in range(4):
        copy(k).start()
    total = jnp.zeros((step - 2 * rows, size), F32)
    for k in range(8):
        source = (core_ref, other_ref)[k // 4]
        start = (k % 4) * step
        place = pl.ds(pl.multiple_of(place_ref[k], 16), rows)
        direction[place, :] = source[start : start + rows, :]
        power[k * rows : (k + 1) * rows, :] = source[start + rows : start + 2 * rows, :]
        total += source[start + 2 * rows : start + step, :].astype(F32)
    sum_ref[...] = jnp.full(sum_ref.shape, jnp.sum(total))
    squares = jnp.zeros((rows, size), F32)
    for k in range(8):
        squares += jnp.square(power[k * rows : (k + 1) * rows, :].astype(F32))
    square = size / (16.0 * jnp.sum(squares))
    keep = power_ref[...]
    value = keep
    for turn in range(4):
        across = dot_nt(value.astype(BF), power[...]).astype(BF)
        moved = square * dot_nn(across, power[...])
        value = moved if turn == 1 else 1.5 * value - 0.5 * moved
        if turn == 0:
            keep = value
    scale = math.sqrt(size) * jnp.sqrt(jnp.full((rows, size), square))
    basis_ref[...] = scale * (1.5 * keep - 0.5 * value)
    back_half = dot_nn(rows_ref[...], direction[...]).astype(BF)
    for k in range(4):
        copy(k).wait()
        terms[k][...] = dot_nt(back_half, cols[k]).astype(BF)


def side(places, extra_core, extra_other, right_cols, left_rows, power_left):
    rows, size = power_left.shape
    in_vmem = pl.BlockSpec(memory_space=pltpu.VMEM)
    term = jax.ShapeDtypeStruct((rows, size), BF)
    sums = jax.ShapeDtypeStruct((8, 128), F32)
    return pl.pallas_call(
        side_kernel,
        out_shape=[jax.ShapeDtypeStruct((rows, size), F32), sums] + [term] * 4,
        in_specs=[pl.BlockSpec(memory_space=pltpu.SMEM)]
        + [in_vmem] * 2
        + [pl.BlockSpec(memory_space=pl.ANY)]
        + [in_vmem] * 2,
        out_specs=[in_vmem] * 6,
        scratch_shapes=[
            pltpu.VMEM((size, size), BF),
            pltpu.VMEM((size, size), BF),
            pltpu.VMEM((4, size, size), BF),
            pltpu.SemaphoreType.DMA((4,)),
        ],
        compiler_params=pltpu.CompilerParams(vmem_limit_bytes=56 * 2**20),
        cost_estimate=pl.CostEstimate(
            flops=26 * rows * size * size, bytes_accessed=12 * size * size, transcendentals=0
        ),
    )(places, extra_core, extra_other, right_cols, left_rows, power_left)


def partial_squares(a):
    squares = jnp.square(a.astype(F32)).reshape(-1, 16, a.shape[1])
    return jnp.sum(squares, axis=0).astype(BF)


def after(block, *others):
    return lax.optimization_barrier((block, *others))[0]


def local_pattern(gradient, moment_one, moment_two, stat_left, stat_right, basis_left, basis_right):
    rows_left = gradient.shape[0]
    rows_right = stat_right.shape[0]
    cols_right = stat_right.shape[1]
    shard_pos = lax.axis_index("shard")
    tensor_pos = lax.axis_index("tensor")
    z, x = shard_pos // 2, shard_pos % 2
    y, core = tensor_pos // 2, tensor_pos % 2
    straight = x == core
    inner = (z == 1) | (z == 2)
    half = rows_right // 2

    left_b = (basis_left / math.sqrt(D)).astype(BF)
    right_b = (basis_right / math.sqrt(FF)).astype(BF)
    stat_b = stat_right.astype(BF)
    part_left = rows_left // 2
    small = jnp.concatenate(
        [gradient, lax.dynamic_slice_in_dim(left_b, y * part_left, part_left, 0)]
    )
    rows_small = small.shape[0]

    turned, small_o1, small_i1, moment_one, moment_two, stat_left = stage(
        turn_over(right_b, straight),
        swap_outer(small),
        swap_inner(small),
        moment_one,
        moment_two,
        stat_left,
    )
    early = jnp.concatenate([moment_one, moment_two, stat_left]).astype(BF)
    got_i, got_o, stat_y, stat_x, early = stage(
        swap_inner(jnp.concatenate([turned, small_o1])),
        swap_outer(jnp.concatenate([turned, small_i1])),
        swap_y(stat_b),
        swap_x(stat_b),
        turn_over(early, straight),
    )
    turned_o1, small_o2 = got_o[:rows_right], got_o[rows_right:]
    turned_i1, small_i2 = got_i[:rows_right], got_i[rows_right:]
    small_1 = ordered_pair(z % 2 == 0, small, small_o1).reshape(2 * rows_small, cols_right)
    to_x = jnp.concatenate([stat_y[half:], small_1])
    to_y = jnp.concatenate([stat_x[:half], small_1])
    got_x, got_y, got_o, turned_i2 = stage(
        swap_x(to_x),
        swap_y(to_y),
        swap_outer(after(jnp.concatenate([turned_i1, small_i2]), to_x, to_y)),
        swap_inner(after(turned_o1, to_x, to_y)),
    )
    turned_o2, small_o3 = got_o[:rows_right], got_o[rows_right:]
    small_2 = ordered_pair(
        z < 2, jnp.where(inner, small_i1, small_o2), jnp.where(inner, small_i2, small_o3)
    ).reshape(2 * rows_small, cols_right)
    stat_xy = jnp.concatenate([got_y[:half], got_x[:half]])
    small_1x, small_1y = got_x[half:], got_y[half:]
    stat_keep = [jnp.where(straight, stat_b, stat_x), jnp.where(straight, stat_y, stat_xy)]
    stat_send = [jnp.where(straight, stat_x, stat_b), jnp.where(straight, stat_xy, stat_y)]
    turned_o3, got_x, got_y, stat_got = stage(
        swap_outer(turned_i2),
        swap_x(jnp.concatenate([small_1y[rows_small:], small_2])),
        swap_y(jnp.concatenate([small_1x[:rows_small], small_2])),
        swap_core(jnp.concatenate(stat_send)),
    )
    small_1xy = jnp.concatenate([got_y[:rows_small], got_x[:rows_small]])
    small_2x, small_2y = got_x[rows_small:], got_y[rows_small:]
    turned_z = in_order(
        z,
        turned,
        turned_o1,
        jnp.where(inner, turned_i1, turned_o2),
        jnp.where(inner, turned_i2, turned_o3),
    )
    stat_rows = jnp.zeros((rows_right, 4 * cols_right), BF)
    stat_rows = put(stat_rows, stat_keep[0], 0, (2 * y + core) * cols_right)
    stat_rows = put(stat_rows, stat_keep[1], 0, (2 - 2 * y + core) * cols_right)
    stat_rows = put(stat_rows, stat_got[:rows_right], 0, (2 * y + 1 - core) * cols_right)
    stat_rows = put(stat_rows, stat_got[rows_right:], 0, (3 - 2 * y - core) * cols_right)
    small_2hi, small_2lo, turned_got = stage(
        swap_x(small_2y[rows_small:]), swap_y(small_2x[:rows_small]), swap_core(turned_z)
    )
    right_cols = interleave(core, turned_z, turned_got)
    grad_core = jnp.zeros((4, 2, rows_left, 2 * cols_right), BF)
    left_all = jnp.zeros((4, 2, 2, part_left, cols_right), BF)
    small_2xy = jnp.concatenate([small_2lo, small_2hi])
    low = 2 * (z // 2)
    for block, at_z, at_x, at_y in (
        (small_1, low, x, y),
        (small_1x, low, 1 - x, y),
        (small_1y, low, x, 1 - y),
        (small_1xy, low, 1 - x, 1 - y),
        (small_2, 2 - low, x, y),
        (small_2x, 2 - low, 1 - x, y),
        (small_2y, 2 - low, x, 1 - y),
        (small_2xy, 2 - low, 1 - x, 1 - y),
    ):
        block = block.reshape(2, 1, rows_small, cols_right)
        grad_core = put(grad_core, block[:, :, :rows_left], at_z, at_x, 0, at_y * cols_right)
        left_all = put(left_all, block[:, :, None, rows_left:], at_z, at_x, at_y, 0, 0)
    grad_core = grad_core.reshape(8 * rows_left, 2 * cols_right)
    left_all = left_all.reshape(8 * rows_left, cols_right)

    grad_other = swap_core(grad_core)
    rows_core = lax.dynamic_slice_in_dim(
        right_cols.reshape(2, 2, cols_right, cols_right), core, 1, 1
    ).reshape(2 * cols_right, cols_right)
    carried = dot_nn(grad_core, rows_core)
    carried = (carried + swap_core(carried.astype(BF)).astype(F32)).astype(BF)

    def grad_block(at_x):
        start = (z // 2) * cols_right + at_x * rows_right
        ours = lax.dynamic_slice_in_dim(grad_core, start, rows_right, 1)
        other = lax.dynamic_slice_in_dim(grad_other, start, rows_right, 1)
        return jnp.where(z % 2 == core, ours, other)

    gram = 0.0
    for part in (grad_core, grad_other):
        rows = lax.dynamic_slice_in_dim(part, 2 * z * rows_left, 2 * rows_left, 0)
        gram = gram + dot_nt(rows, part)
    gram = gram.reshape(2, rows_left, cols_right)
    gram_own = lax.dynamic_index_in_dim(gram, x, 0, False)
    gram_here = lax.dynamic_index_in_dim(gram, core, 0, False)
    share = (1.0 - beta_stat) / D
    picked = grad_block(core)
    power = beta_stat * dot_nn(stat_rows, right_cols) + share * dot_tn(picked, carried)
    power, carried = stage(power.astype(BF), carried)

    here = (2 * z + core) * rows_left
    early = early.astype(F32)
    left_cols = lax.dynamic_slice_in_dim(left_all, here, rows_left, 1)
    rotated = dot_tn(left_cols, carried)
    _, _, direction = adam_moments(rotated, early[:rows_left], early[rows_left : 2 * rows_left])
    stat_t = blend_stat(early[2 * rows_left :], gram_here, FF)
    left_t = dot_nn(stat_t.astype(BF), left_all).astype(BF)
    extra = jnp.concatenate([direction, left_t, partial_squares(power)])

    own_grad = lax.dynamic_slice_in_dim(grad_core, y * cols_right, cols_right, 1)
    new_stat_right = blend_stat(stat_right, dot_tn(grad_block(x), own_grad), D)
    new_stat_left = blend_stat(stat_left, gram_own, FF)
    power_left = dot_nn(new_stat_left.astype(BF), left_all)

    power_x, power_y, near, power_i1, extra = stage(
        swap_x(power),
        swap_y(power),
        swap_outer(power),
        swap_inner(power),
        extra,
    )
    near_place, mid_place, far_place = places_z(z)
    side_places = jnp.stack(
        [
            (2 * at_z + at_x) * rows_left
            for at_x in (core, 1 - core)
            for at_z in (z, near_place, mid_place, far_place)
        ]
        + [
            ((y + along) % 2 * 2 + (x + across) % 2) * cols_right
            for along in range(2)
            for across in range(2)
        ]
    )
    places = jnp.stack(
        [jnp.where(straight, 0, rows_right) + core * half, straight.astype(jnp.int32)]
    )
    left_rows = lax.dynamic_slice_in_dim(left_all, here, rows_left, 0)
    to_x = jnp.concatenate([power_y[half:], near])
    to_y = jnp.concatenate([power_x[:half], near])
    (
        got_x,
        got_y,
        got_o,
        got_i,
        new_stat_right,
        new_stat_left,
        power_left,
        left_rows,
        side_places,
        places,
    ) = stage(
        swap_x(to_x),
        swap_y(to_y),
        swap_outer(after(jnp.concatenate([power_i1, extra]), to_x, to_y)),
        swap_inner(after(jnp.concatenate([near, extra]), to_x, to_y)),
        new_stat_right,
        new_stat_left,
        power_left,
        left_rows,
        side_places,
        places,
    )
    stack0 = jnp.concatenate([power, power_x, power_y])
    stack1 = jnp.concatenate([near, got_x, got_y])
    near_x, near_y = got_x[half:], got_y[half:]
    power_o2, extra_o1 = got_o[:rows_right], got_o[rows_right:]
    power_i2, extra_i1 = got_i[:rows_right], got_i[rows_right:]
    mid = jnp.where(inner, power_i1, power_o2)
    to_x = jnp.concatenate([near_y[half:], mid])
    to_y = jnp.concatenate([near_x[:half], mid])
    got_x, got_y, got_o, extra_i2, other0 = stage(
        *exchange(
            (swap_x, to_x),
            (swap_y, to_y),
            (swap_outer, jnp.concatenate([power_i2, extra_i1])),
            (swap_inner, extra_o1),
        ),
        swap_core(stack0),
    )
    stack2 = jnp.concatenate([mid, got_x, got_y])
    mid_x, mid_y = got_x[half:], got_y[half:]
    power_o3, extra_o2 = got_o[:rows_right], got_o[rows_right:]
    far = jnp.where(inner, power_i2, power_o3)
    got_x, got_y, extra_o3, other1, rotated = stage(
        swap_x(far),
        swap_y(far),
        swap_outer(extra_i2),
        swap_core(stack1),
        turn_over(rotated.astype(BF), straight),
    )
    far_x, far_y = got_x, got_y
    stack3 = jnp.concatenate([far, far_x, far_y])
    extra_core = jnp.concatenate(
        [extra, extra_o1, jnp.where(inner, extra_i1, extra_o2), jnp.where(inner, extra_i2, extra_o3)]
    )
    extra_other = swap_core(extra_core)
    stack3 = after(stack3, extra_other)
    new_basis_left, sums, *terms = side(
        side_places,
        extra_core,
        extra_other,
        right_cols,
        left_rows,
        power_left,
    )
    got_y, got_x, other2, new_basis_left, sums = stage(
        swap_y(jnp.concatenate([mid_x[:half], far_x[:half]])),
        swap_x(jnp.concatenate([mid_y[half:], far_y[half:]])),
        swap_core(stack2),
        new_basis_left,
        sums,
    )
    stack4 = jnp.concatenate([got_y, got_x])
    other3, other4 = swap_core(stack3), swap_core(stack4)
    sums = (sums, swap_x(sums), swap_y(sums), swap_diagonal(sums))
    new_moment_one, new_moment_two, _ = adam_moments(
        rotated.astype(F32), moment_one, moment_two
    )

    terms = [
        swap_to(across, along)(terms[2 * along + across])
        for along in range(2)
        for across in range(2)
    ]
    update = sum(term.astype(F32) for term in terms).astype(BF)

    stacks = (
        stack0, other0, stack1, other1, stack2, other2, stack3, other3, stack4, other4
    )
    mine, theirs = refresh(places, sums, stacks)
    theirs = swap_core(theirs)
    new_basis_right = jnp.zeros((rows_right, cols_right), F32)
    new_basis_right = put(new_basis_right, mine, core * half, 0)
    new_basis_right = put(new_basis_right, theirs, (1 - core) * half, 0)
    return (
        update,
        new_moment_one,
        new_moment_two,
        new_stat_left,
        new_stat_right,
        new_basis_left,
        new_basis_right,
    )


def solution(mesh):
    nz, nx, ny, nc = PATTERN
    fits = (mesh.shape["shard"], mesh.shape["tensor"]) == (nz * nx, ny * nc)
    local = local_pattern if fits else local_general
    placed = (
        P("shard", "tensor"),
        P("shard", "tensor"),
        P("shard", "tensor"),
        P("shard", None),
        P("shard", "tensor"),
        P("shard", None),
        P("shard", "tensor"),
    )
    return jax.shard_map(
        local,
        mesh=mesh,
        in_specs=placed,
        out_specs=(
            P("shard", "tensor"),
            P("shard", "tensor"),
            P("shard", "tensor"),
            P("shard", None),
            P("shard", "tensor"),
            P("shard", None),
            P("shard", "tensor"),
        ),
        check_vma=False,
    )
```

```python
import functools
import math

import jax
import jax.numpy as jnp
from jax import lax
from jax.experimental import pallas as pl
from jax.experimental.pallas import tpu as pltpu
from jax.sharding import PartitionSpec as P

D = 768
FF = 3072
NS_STEPS = 2


beta_one = 0.95
beta_two = 0.95
beta_stat = 0.95
correction = 1.0 - 0.95**10
adam_eps = 1e-08
highest = lax.Precision.HIGHEST


def blend_stat(previous, product, divisor):
    return beta_stat * previous + (1.0 - beta_stat) * (product / divisor)


def adam_moments(rotated, moment_one, moment_two):
    first_moment = beta_one * moment_one + (1.0 - beta_one) * rotated
    second_moment = beta_two * moment_two + (1.0 - beta_two) * (rotated * rotated)
    direction = (
        first_moment / correction / (jnp.sqrt(second_moment / correction) + adam_eps)
    ).astype(jnp.bfloat16)
    return (first_moment, second_moment, direction)


def local_general(gradient, moment_one, moment_two, stat_left, stat_right, basis_left, basis_right):
    rows_left = gradient.shape[0]
    rows_right = stat_right.shape[0]
    cols_right = stat_right.shape[1]
    shard_pos = lax.axis_index("shard")
    tensor_pos = lax.axis_index("tensor")
    row_start = shard_pos * rows_left
    grad_cols = lax.all_gather(gradient, "shard", axis=0, tiled=True)
    left_terms = jnp.dot(gradient, grad_cols.T, preferred_element_type=jnp.float32)
    gram_rows = lax.psum(left_terms.astype(jnp.bfloat16), "tensor").astype(jnp.float32)
    new_stat_left = blend_stat(stat_left, gram_rows, FF)
    grad_whole = lax.all_gather(grad_cols, "tensor", axis=1, tiled=True)
    picked = lax.dynamic_slice_in_dim(grad_whole, shard_pos * rows_right, rows_right, 1)
    gram_block = jnp.dot(picked.T, grad_cols, preferred_element_type=jnp.float32)
    new_stat_right = blend_stat(stat_right, gram_block, D)
    basis_all = lax.all_gather(basis_left, "shard", axis=0, tiled=True)
    left_q_all = basis_all / math.sqrt(D)
    left_qb_all = left_q_all.astype(jnp.bfloat16)
    left_qb_own = lax.dynamic_slice_in_dim(left_qb_all, row_start, rows_left, 0)
    left_cols_own = lax.dynamic_slice_in_dim(left_qb_all, row_start, rows_left, 1)
    half_rotated = jnp.dot(left_cols_own.T, grad_cols, preferred_element_type=jnp.float32).astype(
        jnp.bfloat16
    )
    right_q = basis_right / math.sqrt(FF)
    right_qb = right_q.astype(jnp.bfloat16)
    right_cols_b = lax.all_gather(right_qb, "shard", axis=0, tiled=True)
    half_full = lax.all_gather(half_rotated, "tensor", axis=1, tiled=True)
    rotated = jnp.dot(half_full, right_cols_b, preferred_element_type=jnp.float32)
    new_moment_one, new_moment_two, direction = adam_moments(rotated, moment_one, moment_two)
    back_half = jnp.dot(
        left_qb_own,
        lax.all_gather(direction, "shard", axis=0, tiled=True),
        preferred_element_type=jnp.float32,
    ).astype(jnp.bfloat16)
    back_terms = jnp.dot(back_half, right_cols_b.T, preferred_element_type=jnp.float32)
    update = lax.psum_scatter(back_terms, "tensor", scatter_dimension=1, tiled=True).astype(
        jnp.bfloat16
    )
    stat_rows = lax.all_gather(new_stat_right, "tensor", axis=1, tiled=True)
    power_right = jnp.dot(
        stat_rows,
        lax.all_gather(right_q, "shard", axis=0, tiled=True),
        precision=highest,
        preferred_element_type=jnp.float32,
    )
    power_left = jnp.dot(
        new_stat_left, left_q_all, precision=highest, preferred_element_type=jnp.float32
    )
    local_left = jnp.sum(power_left * power_left)
    local_right = jnp.sum(power_right * power_right)
    total_left = lax.psum(local_left, "shard")
    total_right = lax.psum(local_right, ("shard", "tensor"))
    iterate_left = power_left * (math.sqrt(D) / (4.0 * jnp.sqrt(total_left)))
    for iteration in range(NS_STEPS):
        partial_gram = jnp.dot(
            iterate_left.T, iterate_left, precision=highest, preferred_element_type=jnp.float32
        )
        gram_left = lax.psum(partial_gram.astype(jnp.bfloat16), "shard").astype(jnp.float32)
        iterate_left = 1.5 * iterate_left - 0.5 * jnp.dot(
            iterate_left, gram_left, precision=highest, preferred_element_type=jnp.float32
        )
    iterate_right = power_right * (math.sqrt(FF) / (4.0 * jnp.sqrt(total_right)))
    row_ids = shard_pos * rows_right + lax.broadcasted_iota(jnp.int32, (rows_right, cols_right), 0)
    col_ids = tensor_pos * cols_right + lax.broadcasted_iota(jnp.int32, (rows_right, cols_right), 1)
    identity_tile = (row_ids == col_ids).astype(jnp.float32)
    for iteration in range(NS_STEPS):
        rounded_iterate = iterate_right.astype(jnp.bfloat16)
        iterate_rows = lax.all_gather(rounded_iterate, "tensor", axis=1, tiled=True)
        gram_right = lax.psum_scatter(
            jnp.dot(iterate_rows.T, rounded_iterate, preferred_element_type=jnp.float32).astype(
                jnp.bfloat16
            ),
            "shard",
            scatter_dimension=0,
            tiled=True,
        ).astype(jnp.float32)
        mixing = (1.5 * identity_tile - 0.5 * gram_right).astype(jnp.bfloat16)
        iterate_right = jnp.dot(
            iterate_rows,
            lax.all_gather(mixing, "shard", axis=0, tiled=True),
            preferred_element_type=jnp.float32,
        )
    return (
        update,
        new_moment_one,
        new_moment_two,
        new_stat_left,
        new_stat_right,
        iterate_left * math.sqrt(D),
        iterate_right * math.sqrt(FF),
    )


BF = jnp.bfloat16
F32 = jnp.float32
AXES = ("shard", "tensor")
PATTERN = (4, 2, 2, 2)


def dot_nn(a, b):
    return jnp.dot(a, b, preferred_element_type=F32)


def dot_nt(a, b):
    return lax.dot_general(a, b, (((1,), (1,)), ((), ())), preferred_element_type=F32)


def dot_tn(a, b):
    return lax.dot_general(a, b, (((0,), (0,)), ((), ())), preferred_element_type=F32)


def pairs(move):
    nz, nx, ny, nc = PATTERN
    out = []
    for z in range(nz):
        for x in range(nx):
            for y in range(ny):
                for c in range(nc):
                    to = move(z, x, y, c)
                    if 0 <= to[0] < nz:
                        source = ((z * nx + x) * ny + y) * nc + c
                        target = ((to[0] * nx + to[1]) * ny + to[2]) * nc + to[3]
                        out.append((source, target))
    return out


def swap_x(a):
    return lax.ppermute(a, AXES, pairs(lambda z, x, y, c: (z, 1 - x, y, c)))


def swap_y(a):
    return lax.ppermute(a, AXES, pairs(lambda z, x, y, c: (z, x, 1 - y, c)))


def swap_core(a):
    return lax.ppermute(a, AXES, pairs(lambda z, x, y, c: (z, x, y, 1 - c)))


def swap_outer(a):
    return lax.ppermute(a, AXES, pairs(lambda z, x, y, c: (z + 1 - 2 * (z % 2), x, y, c)))


def swap_inner(a):
    return lax.ppermute(a, AXES, pairs(lambda z, x, y, c: (3 - z if 0 < z < 3 else -1, x, y, c)))


def turn_over(a, straight):
    crossed = pairs(lambda z, x, y, c: (z if x != c else -1, 1 - x, y, 1 - c))
    return jnp.where(straight, a, lax.ppermute(a, AXES, crossed))


def stage(*parts):
    return lax.optimization_barrier(parts)


def swap_diagonal(a):
    return lax.ppermute(a, AXES, pairs(lambda z, x, y, c: (z, 1 - x, 1 - y, c)))


def swap_to(across, along):
    return lambda a: lax.ppermute(
        a, AXES, pairs(lambda z, x, y, c: (z, c, (y + along) % 2, (x + across) % 2))
    )


def places_z(z):
    return z + 1 - 2 * (z % 2), jnp.where(z < 2, 2, 1), jnp.where(z < 2, 3, 0)


def in_order(z, own, near, mid, far):
    whole = jnp.zeros((4,) + own.shape, own.dtype)
    for block, place in zip((own, near, mid, far), (z,) + places_z(z)):
        whole = lax.dynamic_update_slice(whole, block[None], (place,) + (0,) * own.ndim)
    return whole


def ordered_pair(ahead, first, second):
    both = jnp.concatenate([first[None], second[None]])
    return jnp.where(ahead, both, jnp.concatenate([second[None], first[None]]))


def put(whole, part, *start):
    return lax.dynamic_update_slice(whole, part, start)


def interleave(core, mine, theirs):
    rows, cols = mine.shape[1:]
    whole = jnp.zeros((4, 2, rows, cols), mine.dtype)
    whole = put(whole, mine[:, None], 0, core, 0, 0)
    whole = put(whole, theirs[:, None], 0, 1 - core, 0, 0)
    return whole.reshape(8 * rows, cols)


def refresh_kernel(place_ref, *refs):
    sums, stacks, (mine_ref, theirs_ref) = refs[:4], refs[4:14], refs[14:16]
    whole, inner, held, total, first, sems = refs[16:]
    count, size = held.shape
    tall = size // 4
    wide = size // 2
    half = size // 8

    def copy(k, i):
        slot, other = k // 2, k % 2
        rows = half if i < 3 else half // 2
        if i < 3:
            stack = slot
            row = i * half + (i * (half // 2) if slot in (1, 2) else 0)
        elif slot < 2:
            stack = slot + 1
            row = half if i == 4 else 2 * half + half // 2
        else:
            stack = 4
            row = (i - 3) * half + (slot - 2) * (half // 2)
        source = stacks[2 * stack + other].at[pl.ds(row, rows), :]
        start = k * half + (half // 2 if i == 4 else 0)
        target = whole.at[pl.ds(start, rows), pl.ds(min(i, 3) * tall, tall)]
        return pltpu.make_async_copy(source, target, sems.at[k, i])

    def arrived(j):
        for k in (2 * j, 2 * j + 1):
            for i in range(5):
                copy(k, i).wait()

    spans = [slice(0, wide), slice(wide, size)]

    for k in range(8):
        for i in range(5):
            copy(k, i).start()
    squares = size / (16.0 * sum(part[...] for part in sums))
    square = squares[0, 0]
    last = (math.sqrt(size) * jnp.sqrt(squares))[0, 0]
    arrived(0)
    held[...] = whole[pl.ds(pl.multiple_of(place_ref[0], 16), count), :]
    total[...] = held[...].astype(F32)

    for j in range(4):
        if j:
            arrived(j)
        rows = slice(j * tall, (j + 1) * tall)
        inner[:, rows] = dot_nt(held[...], whole[rows, :]).astype(BF)

    def one_pass(i, carry):
        @pl.when(i > 0)
        def _():
            for span in spans:
                inner[:, span] = dot_nt(held[...], whole[span, :]).astype(BF)

        keep = jnp.where(i == 1, 0.0, 1.5)
        take = jnp.where(i == 1, square, -0.5 * square)

        def back(span):
            value = keep * total[:, span] + take * dot_nn(inner[...], whole[:, span])
            total[:, span] = value
            held[:, span] = value.astype(BF)

            @pl.when(i == 0)
            def _():
                first[:, span] = value

        back(spans[0])
        pl.when(i < 3)(functools.partial(back, spans[1]))
        return carry

    lax.fori_loop(0, 4, one_pass, 0)
    for k, flag in ((0, 1), (1, 0)):
        span = slice(k * tall, (k + 1) * tall)
        value = last * (1.5 * first[:, span] - 0.5 * total[:, span])

        @pl.when(place_ref[1] == flag)
        def _():
            mine_ref[...] = value

        @pl.when(place_ref[1] != flag)
        def _():
            theirs_ref[...] = value


def refresh(places, sums, stacks):
    tall = stacks[0].shape[1]
    size = 4 * tall
    count = size // 16
    in_vmem = pl.BlockSpec(memory_space=pltpu.VMEM)
    in_smem = pl.BlockSpec(memory_space=pltpu.SMEM)
    return pl.pallas_call(
        refresh_kernel,
        out_shape=[jax.ShapeDtypeStruct((count, tall), F32)] * 2,
        in_specs=[in_smem] + [in_vmem] * 4 + [pl.BlockSpec(memory_space=pl.ANY)] * 10,
        out_specs=[in_vmem] * 2,
        scratch_shapes=[
            pltpu.VMEM((size, size), BF),
            pltpu.VMEM((count, size), BF),
            pltpu.VMEM((count, size), BF),
            pltpu.VMEM((count, size), F32),
            pltpu.VMEM((count, size), F32),
            pltpu.SemaphoreType.DMA((8, 5)),
        ],
        compiler_params=pltpu.CompilerParams(vmem_limit_bytes=56 * 2**20),
        cost_estimate=pl.CostEstimate(
            flops=15 * count * size * size, bytes_accessed=2 * size * size, transcendentals=0
        ),
    )(places, *sums, *stacks)


def side_kernel(place_ref, core_ref, other_ref, cols_ref, rows_ref, power_ref, *refs):
    basis_ref, sum_ref, terms = refs[0], refs[1], refs[2:6]
    power, direction, cols, sems = refs[6:]
    rows, size = power_ref.shape
    step = core_ref.shape[0] // 4

    def copy(k):
        block = pl.ds(pl.multiple_of(place_ref[8 + k], 16), size)
        return pltpu.make_async_copy(cols_ref.at[block, :], cols.at[k], sems.at[k])

    for k in range(4):
        copy(k).start()
    total = jnp.zeros((step - 2 * rows, size), F32)
    for k in range(8):
        source = (core_ref, other_ref)[k // 4]
        start = (k % 4) * step
        place = pl.ds(pl.multiple_of(place_ref[k], 16), rows)
        direction[place, :] = source[start : start + rows, :]
        power[k * rows : (k + 1) * rows, :] = source[start + rows : start + 2 * rows, :]
        total += source[start + 2 * rows : start + step, :].astype(F32)
    sum_ref[...] = jnp.full(sum_ref.shape, jnp.sum(total))
    squares = jnp.zeros((rows, size), F32)
    for k in range(8):
        squares += jnp.square(power[k * rows : (k + 1) * rows, :].astype(F32))
    square = size / (16.0 * jnp.sum(squares))
    keep = power_ref[...]
    value = keep
    for turn in range(4):
        across = dot_nt(value.astype(BF), power[...]).astype(BF)
        moved = square * dot_nn(across, power[...])
        value = moved if turn == 1 else 1.5 * value - 0.5 * moved
        if turn == 0:
            keep = value
    scale = math.sqrt(size) * jnp.sqrt(jnp.full((rows, size), square))
    basis_ref[...] = scale * (1.5 * keep - 0.5 * value)
    back_half = dot_nn(rows_ref[...], direction[...]).astype(BF)
    for k in range(4):
        copy(k).wait()
        terms[k][...] = dot_nt(back_half, cols[k]).astype(BF)


def side(places, extra_core, extra_other, right_cols, left_rows, power_left):
    rows, size = power_left.shape
    in_vmem = pl.BlockSpec(memory_space=pltpu.VMEM)
    term = jax.ShapeDtypeStruct((rows, size), BF)
    sums = jax.ShapeDtypeStruct((8, 128), F32)
    return pl.pallas_call(
        side_kernel,
        out_shape=[jax.ShapeDtypeStruct((rows, size), F32), sums] + [term] * 4,
        in_specs=[pl.BlockSpec(memory_space=pltpu.SMEM)]
        + [in_vmem] * 2
        + [pl.BlockSpec(memory_space=pl.ANY)]
        + [in_vmem] * 2,
        out_specs=[in_vmem] * 6,
        scratch_shapes=[
            pltpu.VMEM((size, size), BF),
            pltpu.VMEM((size, size), BF),
            pltpu.VMEM((4, size, size), BF),
            pltpu.SemaphoreType.DMA((4,)),
        ],
        compiler_params=pltpu.CompilerParams(vmem_limit_bytes=56 * 2**20),
        cost_estimate=pl.CostEstimate(
            flops=26 * rows * size * size, bytes_accessed=12 * size * size, transcendentals=0
        ),
    )(places, extra_core, extra_other, right_cols, left_rows, power_left)


def partial_squares(a):
    squares = jnp.square(a.astype(F32)).reshape(-1, 16, a.shape[1])
    return jnp.sum(squares, axis=0).astype(BF)


def after(block, *others):
    return lax.optimization_barrier((block, *others))[0]


def local_pattern(gradient, moment_one, moment_two, stat_left, stat_right, basis_left, basis_right):
    rows_left = gradient.shape[0]
    rows_right = stat_right.shape[0]
    cols_right = stat_right.shape[1]
    shard_pos = lax.axis_index("shard")
    tensor_pos = lax.axis_index("tensor")
    z, x = shard_pos // 2, shard_pos % 2
    y, core = tensor_pos // 2, tensor_pos % 2
    straight = x == core
    inner = (z == 1) | (z == 2)
    half = rows_right // 2

    left_b = (basis_left / math.sqrt(D)).astype(BF)
    right_b = (basis_right / math.sqrt(FF)).astype(BF)
    stat_b = stat_right.astype(BF)
    part_left = rows_left // 2
    small = jnp.concatenate(
        [gradient, lax.dynamic_slice_in_dim(left_b, y * part_left, part_left, 0)]
    )
    rows_small = small.shape[0]

    turned, small_o1, small_i1, moment_one, moment_two, stat_left = stage(
        turn_over(right_b, straight),
        swap_outer(small),
        swap_inner(small),
        moment_one,
        moment_two,
        stat_left,
    )
    early = jnp.concatenate([moment_one, moment_two, stat_left]).astype(BF)
    got_i, got_o, stat_y, stat_x, early = stage(
        swap_inner(jnp.concatenate([turned, small_o1])),
        swap_outer(jnp.concatenate([turned, small_i1])),
        swap_y(stat_b),
        swap_x(stat_b),
        turn_over(early, straight),
    )
    turned_o1, small_o2 = got_o[:rows_right], got_o[rows_right:]
    turned_i1, small_i2 = got_i[:rows_right], got_i[rows_right:]
    small_1 = ordered_pair(z % 2 == 0, small, small_o1).reshape(2 * rows_small, cols_right)
    to_x = jnp.concatenate([stat_y[half:], small_1])
    to_y = jnp.concatenate([stat_x[:half], small_1])
    got_x, got_y, got_o, turned_i2 = stage(
        swap_x(to_x),
        swap_y(to_y),
        swap_outer(after(jnp.concatenate([turned_i1, small_i2]), to_x, to_y)),
        swap_inner(after(turned_o1, to_x, to_y)),
    )
    turned_o2, small_o3 = got_o[:rows_right], got_o[rows_right:]
    small_2 = ordered_pair(
        z < 2, jnp.where(inner, small_i1, small_o2), jnp.where(inner, small_i2, small_o3)
    ).reshape(2 * rows_small, cols_right)
    stat_xy = jnp.concatenate([got_y[:half], got_x[:half]])
    small_1x, small_1y = got_x[half:], got_y[half:]
    stat_keep = [jnp.where(straight, stat_b, stat_x), jnp.where(straight, stat_y, stat_xy)]
    stat_send = [jnp.where(straight, stat_x, stat_b), jnp.where(straight, stat_xy, stat_y)]
    turned_o3, got_x, got_y, stat_got = stage(
        swap_outer(turned_i2),
        swap_x(jnp.concatenate([small_1y[rows_small:], small_2])),
        swap_y(jnp.concatenate([small_1x[:rows_small], small_2])),
        swap_core(jnp.concatenate(stat_send)),
    )
    small_1xy = jnp.concatenate([got_y[:rows_small], got_x[:rows_small]])
    small_2x, small_2y = got_x[rows_small:], got_y[rows_small:]
    turned_z = in_order(
        z,
        turned,
        turned_o1,
        jnp.where(inner, turned_i1, turned_o2),
        jnp.where(inner, turned_i2, turned_o3),
    )
    stat_rows = jnp.zeros((rows_right, 4 * cols_right), BF)
    stat_rows = put(stat_rows, stat_keep[0], 0, (2 * y + core) * cols_right)
    stat_rows = put(stat_rows, stat_keep[1], 0, (2 - 2 * y + core) * cols_right)
    stat_rows = put(stat_rows, stat_got[:rows_right], 0, (2 * y + 1 - core) * cols_right)
    stat_rows = put(stat_rows, stat_got[rows_right:], 0, (3 - 2 * y - core) * cols_right)
    small_2hi, small_2lo, turned_got = stage(
        swap_x(small_2y[rows_small:]), swap_y(small_2x[:rows_small]), swap_core(turned_z)
    )
    right_cols = interleave(core, turned_z, turned_got)
    grad_core = jnp.zeros((4, 2, rows_left, 2 * cols_right), BF)
    left_all = jnp.zeros((4, 2, 2, part_left, cols_right), BF)
    small_2xy = jnp.concatenate([small_2lo, small_2hi])
    low = 2 * (z // 2)
    for block, at_z, at_x, at_y in (
        (small_1, low, x, y),
        (small_1x, low, 1 - x, y),
        (small_1y, low, x, 1 - y),
        (small_1xy, low, 1 - x, 1 - y),
        (small_2, 2 - low, x, y),
        (small_2x, 2 - low, 1 - x, y),
        (small_2y, 2 - low, x, 1 - y),
        (small_2xy, 2 - low, 1 - x, 1 - y),
    ):
        block = block.reshape(2, 1, rows_small, cols_right)
        grad_core = put(grad_core, block[:, :, :rows_left], at_z, at_x, 0, at_y * cols_right)
        left_all = put(left_all, block[:, :, None, rows_left:], at_z, at_x, at_y, 0, 0)
    grad_core = grad_core.reshape(8 * rows_left, 2 * cols_right)
    left_all = left_all.reshape(8 * rows_left, cols_right)

    grad_other = swap_core(grad_core)
    rows_core = lax.dynamic_slice_in_dim(
        right_cols.reshape(2, 2, cols_right, cols_right), core, 1, 1
    ).reshape(2 * cols_right, cols_right)
    carried = dot_nn(grad_core, rows_core)
    carried = (carried + swap_core(carried.astype(BF)).astype(F32)).astype(BF)

    def grad_block(at_x):
        start = (z // 2) * cols_right + at_x * rows_right
        ours = lax.dynamic_slice_in_dim(grad_core, start, rows_right, 1)
        other = lax.dynamic_slice_in_dim(grad_other, start, rows_right, 1)
        return jnp.where(z % 2 == core, ours, other)

    gram = 0.0
    for part in (grad_core, grad_other):
        rows = lax.dynamic_slice_in_dim(part, 2 * z * rows_left, 2 * rows_left, 0)
        gram = gram + dot_nt(rows, part)
    gram = gram.reshape(2, rows_left, cols_right)
    gram_own = lax.dynamic_index_in_dim(gram, x, 0, False)
    gram_here = lax.dynamic_index_in_dim(gram, core, 0, False)
    share = (1.0 - beta_stat) / D
    picked = grad_block(core)
    power = beta_stat * dot_nn(stat_rows, right_cols) + share * dot_tn(picked, carried)
    power, carried = stage(power.astype(BF), carried)

    here = (2 * z + core) * rows_left
    early = early.astype(F32)
    left_cols = lax.dynamic_slice_in_dim(left_all, here, rows_left, 1)
    rotated = dot_tn(left_cols, carried)
    _, _, direction = adam_moments(rotated, early[:rows_left], early[rows_left : 2 * rows_left])
    stat_t = blend_stat(early[2 * rows_left :], gram_here, FF)
    left_t = dot_nn(stat_t.astype(BF), left_all).astype(BF)
    extra = jnp.concatenate([direction, left_t, partial_squares(power)])

    own_grad = lax.dynamic_slice_in_dim(grad_core, y * cols_right, cols_right, 1)
    new_stat_right = blend_stat(stat_right, dot_tn(grad_block(x), own_grad), D)
    new_stat_left = blend_stat(stat_left, gram_own, FF)
    power_left = dot_nn(new_stat_left.astype(BF), left_all)

    power_x, power_y, near, power_i1, extra = stage(
        swap_x(power),
        swap_y(power),
        swap_outer(power),
        swap_inner(power),
        extra,
    )
    near_place, mid_place, far_place = places_z(z)
    side_places = jnp.stack(
        [
            (2 * at_z + at_x) * rows_left
            for at_x in (core, 1 - core)
            for at_z in (z, near_place, mid_place, far_place)
        ]
        + [
            ((y + along) % 2 * 2 + (x + across) % 2) * cols_right
            for along in range(2)
            for across in range(2)
        ]
    )
    places = jnp.stack(
        [jnp.where(straight, 0, rows_right) + core * half, straight.astype(jnp.int32)]
    )
    left_rows = lax.dynamic_slice_in_dim(left_all, here, rows_left, 0)
    to_x = jnp.concatenate([power_y[half:], near])
    to_y = jnp.concatenate([power_x[:half], near])
    (
        got_o,
        got_i,
        got_x,
        got_y,
        new_stat_right,
        new_stat_left,
        power_left,
        left_rows,
        side_places,
        places,
    ) = stage(
        swap_outer(jnp.concatenate([power_i1, extra])),
        swap_inner(jnp.concatenate([near, extra])),
        swap_x(to_x),
        swap_y(to_y),
        new_stat_right,
        new_stat_left,
        power_left,
        left_rows,
        side_places,
        places,
    )
    stack0 = jnp.concatenate([power, power_x, power_y])
    stack1 = jnp.concatenate([near, got_x, got_y])
    near_x, near_y = got_x[half:], got_y[half:]
    power_o2, extra_o1 = got_o[:rows_right], got_o[rows_right:]
    power_i2, extra_i1 = got_i[:rows_right], got_i[rows_right:]
    mid = jnp.where(inner, power_i1, power_o2)
    to_x = jnp.concatenate([near_y[half:], mid])
    to_y = jnp.concatenate([near_x[:half], mid])
    got_x, got_y, got_o, extra_i2, other0 = stage(
        swap_x(to_x),
        swap_y(to_y),
        swap_outer(jnp.concatenate([power_i2, extra_i1])),
        swap_inner(extra_o1),
        swap_core(stack0),
    )
    stack2 = jnp.concatenate([mid, got_x, got_y])
    mid_x, mid_y = got_x[half:], got_y[half:]
    power_o3, extra_o2 = got_o[:rows_right], got_o[rows_right:]
    far = jnp.where(inner, power_i2, power_o3)
    got_x, got_y, extra_o3, other1, rotated = stage(
        swap_x(far),
        swap_y(far),
        swap_outer(extra_i2),
        swap_core(stack1),
        turn_over(rotated.astype(BF), straight),
    )
    far_x, far_y = got_x, got_y
    stack3 = jnp.concatenate([far, far_x, far_y])
    extra_core = jnp.concatenate(
        [extra, extra_o1, jnp.where(inner, extra_i1, extra_o2), jnp.where(inner, extra_i2, extra_o3)]
    )
    extra_other = swap_core(extra_core)
    stack3 = after(stack3, extra_other)
    new_basis_left, sums, *terms = side(
        side_places,
        extra_core,
        extra_other,
        right_cols,
        left_rows,
        power_left,
    )
    got_y, got_x, other2, new_basis_left, sums = stage(
        swap_y(jnp.concatenate([mid_x[:half], far_x[:half]])),
        swap_x(jnp.concatenate([mid_y[half:], far_y[half:]])),
        swap_core(stack2),
        new_basis_left,
        sums,
    )
    stack4 = jnp.concatenate([got_y, got_x])
    other3, other4 = swap_core(stack3), swap_core(stack4)
    sums = (sums, swap_x(sums), swap_y(sums), swap_diagonal(sums))
    new_moment_one, new_moment_two, _ = adam_moments(
        rotated.astype(F32), moment_one, moment_two
    )

    terms = [
        swap_to(across, along)(terms[2 * along + across])
        for along in range(2)
        for across in range(2)
    ]
    update = sum(term.astype(F32) for term in terms).astype(BF)

    stacks = (
        stack0, other0, stack1, other1, stack2, other2, stack3, other3, stack4, other4
    )
    mine, theirs = refresh(places, sums, stacks)
    theirs = swap_core(theirs)
    new_basis_right = jnp.zeros((rows_right, cols_right), F32)
    new_basis_right = put(new_basis_right, mine, core * half, 0)
    new_basis_right = put(new_basis_right, theirs, (1 - core) * half, 0)
    return (
        update,
        new_moment_one,
        new_moment_two,
        new_stat_left,
        new_stat_right,
        new_basis_left,
        new_basis_right,
    )


def solution(mesh):
    nz, nx, ny, nc = PATTERN
    fits = (mesh.shape["shard"], mesh.shape["tensor"]) == (nz * nx, ny * nc)
    local = local_pattern if fits else local_general
    placed = (
        P("shard", "tensor"),
        P("shard", "tensor"),
        P("shard", "tensor"),
        P("shard", None),
        P("shard", "tensor"),
        P("shard", None),
        P("shard", "tensor"),
    )
    return jax.shard_map(
        local,
        mesh=mesh,
        in_specs=placed,
        out_specs=(
            P("shard", "tensor"),
            P("shard", "tensor"),
            P("shard", "tensor"),
            P("shard", None),
            P("shard", "tensor"),
            P("shard", None),
            P("shard", "tensor"),
        ),
        check_vma=False,
    )
```

```python
import functools
import math

import jax
import jax.numpy as jnp
from jax import lax
from jax.experimental import pallas as pl
from jax.experimental.pallas import tpu as pltpu
from jax.sharding import PartitionSpec as P

D = 768
FF = 3072
NS_STEPS = 2


beta_one = 0.95
beta_two = 0.95
beta_stat = 0.95
correction = 1.0 - 0.95**10
adam_eps = 1e-08
highest = lax.Precision.HIGHEST


def blend_stat(previous, product, divisor):
    return beta_stat * previous + (1.0 - beta_stat) * (product / divisor)


def adam_moments(rotated, moment_one, moment_two):
    first_moment = beta_one * moment_one + (1.0 - beta_one) * rotated
    second_moment = beta_two * moment_two + (1.0 - beta_two) * (rotated * rotated)
    direction = (
        first_moment / correction / (jnp.sqrt(second_moment / correction) + adam_eps)
    ).astype(jnp.bfloat16)
    return (first_moment, second_moment, direction)


def local_general(gradient, moment_one, moment_two, stat_left, stat_right, basis_left, basis_right):
    rows_left = gradient.shape[0]
    rows_right = stat_right.shape[0]
    cols_right = stat_right.shape[1]
    shard_pos = lax.axis_index("shard")
    tensor_pos = lax.axis_index("tensor")
    row_start = shard_pos * rows_left
    grad_cols = lax.all_gather(gradient, "shard", axis=0, tiled=True)
    left_terms = jnp.dot(gradient, grad_cols.T, preferred_element_type=jnp.float32)
    gram_rows = lax.psum(left_terms.astype(jnp.bfloat16), "tensor").astype(jnp.float32)
    new_stat_left = blend_stat(stat_left, gram_rows, FF)
    grad_whole = lax.all_gather(grad_cols, "tensor", axis=1, tiled=True)
    picked = lax.dynamic_slice_in_dim(grad_whole, shard_pos * rows_right, rows_right, 1)
    gram_block = jnp.dot(picked.T, grad_cols, preferred_element_type=jnp.float32)
    new_stat_right = blend_stat(stat_right, gram_block, D)
    basis_all = lax.all_gather(basis_left, "shard", axis=0, tiled=True)
    left_q_all = basis_all / math.sqrt(D)
    left_qb_all = left_q_all.astype(jnp.bfloat16)
    left_qb_own = lax.dynamic_slice_in_dim(left_qb_all, row_start, rows_left, 0)
    left_cols_own = lax.dynamic_slice_in_dim(left_qb_all, row_start, rows_left, 1)
    half_rotated = jnp.dot(left_cols_own.T, grad_cols, preferred_element_type=jnp.float32).astype(
        jnp.bfloat16
    )
    right_q = basis_right / math.sqrt(FF)
    right_qb = right_q.astype(jnp.bfloat16)
    right_cols_b = lax.all_gather(right_qb, "shard", axis=0, tiled=True)
    half_full = lax.all_gather(half_rotated, "tensor", axis=1, tiled=True)
    rotated = jnp.dot(half_full, right_cols_b, preferred_element_type=jnp.float32)
    new_moment_one, new_moment_two, direction = adam_moments(rotated, moment_one, moment_two)
    back_half = jnp.dot(
        left_qb_own,
        lax.all_gather(direction, "shard", axis=0, tiled=True),
        preferred_element_type=jnp.float32,
    ).astype(jnp.bfloat16)
    back_terms = jnp.dot(back_half, right_cols_b.T, preferred_element_type=jnp.float32)
    update = lax.psum_scatter(back_terms, "tensor", scatter_dimension=1, tiled=True).astype(
        jnp.bfloat16
    )
    stat_rows = lax.all_gather(new_stat_right, "tensor", axis=1, tiled=True)
    power_right = jnp.dot(
        stat_rows,
        lax.all_gather(right_q, "shard", axis=0, tiled=True),
        precision=highest,
        preferred_element_type=jnp.float32,
    )
    power_left = jnp.dot(
        new_stat_left, left_q_all, precision=highest, preferred_element_type=jnp.float32
    )
    local_left = jnp.sum(power_left * power_left)
    local_right = jnp.sum(power_right * power_right)
    total_left = lax.psum(local_left, "shard")
    total_right = lax.psum(local_right, ("shard", "tensor"))
    iterate_left = power_left * (math.sqrt(D) / (4.0 * jnp.sqrt(total_left)))
    for iteration in range(NS_STEPS):
        partial_gram = jnp.dot(
            iterate_left.T, iterate_left, precision=highest, preferred_element_type=jnp.float32
        )
        gram_left = lax.psum(partial_gram.astype(jnp.bfloat16), "shard").astype(jnp.float32)
        iterate_left = 1.5 * iterate_left - 0.5 * jnp.dot(
            iterate_left, gram_left, precision=highest, preferred_element_type=jnp.float32
        )
    iterate_right = power_right * (math.sqrt(FF) / (4.0 * jnp.sqrt(total_right)))
    row_ids = shard_pos * rows_right + lax.broadcasted_iota(jnp.int32, (rows_right, cols_right), 0)
    col_ids = tensor_pos * cols_right + lax.broadcasted_iota(jnp.int32, (rows_right, cols_right), 1)
    identity_tile = (row_ids == col_ids).astype(jnp.float32)
    for iteration in range(NS_STEPS):
        rounded_iterate = iterate_right.astype(jnp.bfloat16)
        iterate_rows = lax.all_gather(rounded_iterate, "tensor", axis=1, tiled=True)
        gram_right = lax.psum_scatter(
            jnp.dot(iterate_rows.T, rounded_iterate, preferred_element_type=jnp.float32).astype(
                jnp.bfloat16
            ),
            "shard",
            scatter_dimension=0,
            tiled=True,
        ).astype(jnp.float32)
        mixing = (1.5 * identity_tile - 0.5 * gram_right).astype(jnp.bfloat16)
        iterate_right = jnp.dot(
            iterate_rows,
            lax.all_gather(mixing, "shard", axis=0, tiled=True),
            preferred_element_type=jnp.float32,
        )
    return (
        update,
        new_moment_one,
        new_moment_two,
        new_stat_left,
        new_stat_right,
        iterate_left * math.sqrt(D),
        iterate_right * math.sqrt(FF),
    )


BF = jnp.bfloat16
F32 = jnp.float32
AXES = ("shard", "tensor")
PATTERN = (4, 2, 2, 2)


def dot_nn(a, b):
    return jnp.dot(a, b, preferred_element_type=F32)


def dot_nt(a, b):
    return lax.dot_general(a, b, (((1,), (1,)), ((), ())), preferred_element_type=F32)


def dot_tn(a, b):
    return lax.dot_general(a, b, (((0,), (0,)), ((), ())), preferred_element_type=F32)


def pairs(move):
    nz, nx, ny, nc = PATTERN
    out = []
    for z in range(nz):
        for x in range(nx):
            for y in range(ny):
                for c in range(nc):
                    to = move(z, x, y, c)
                    if 0 <= to[0] < nz:
                        source = ((z * nx + x) * ny + y) * nc + c
                        target = ((to[0] * nx + to[1]) * ny + to[2]) * nc + to[3]
                        out.append((source, target))
    return out


def swap_x(a):
    return lax.ppermute(a, AXES, pairs(lambda z, x, y, c: (z, 1 - x, y, c)))


def swap_y(a):
    return lax.ppermute(a, AXES, pairs(lambda z, x, y, c: (z, x, 1 - y, c)))


def swap_core(a):
    return lax.ppermute(a, AXES, pairs(lambda z, x, y, c: (z, x, y, 1 - c)))


def swap_outer(a):
    return lax.ppermute(a, AXES, pairs(lambda z, x, y, c: (z + 1 - 2 * (z % 2), x, y, c)))


def swap_inner(a):
    return lax.ppermute(a, AXES, pairs(lambda z, x, y, c: (3 - z if 0 < z < 3 else -1, x, y, c)))


def turn_over(a, straight):
    crossed = pairs(lambda z, x, y, c: (z if x != c else -1, 1 - x, y, 1 - c))
    return jnp.where(straight, a, lax.ppermute(a, AXES, crossed))


def stage(*parts):
    return lax.optimization_barrier(parts)


def swap_diagonal(a):
    return lax.ppermute(a, AXES, pairs(lambda z, x, y, c: (z, 1 - x, 1 - y, c)))


def swap_to(across, along):
    return lambda a: lax.ppermute(
        a, AXES, pairs(lambda z, x, y, c: (z, c, (y + along) % 2, (x + across) % 2))
    )


def places_z(z):
    return z + 1 - 2 * (z % 2), jnp.where(z < 2, 2, 1), jnp.where(z < 2, 3, 0)


def in_order(z, own, near, mid, far):
    whole = jnp.zeros((4,) + own.shape, own.dtype)
    for block, place in zip((own, near, mid, far), (z,) + places_z(z)):
        whole = lax.dynamic_update_slice(whole, block[None], (place,) + (0,) * own.ndim)
    return whole


def ordered_pair(ahead, first, second):
    both = jnp.concatenate([first[None], second[None]])
    return jnp.where(ahead, both, jnp.concatenate([second[None], first[None]]))


def put(whole, part, *start):
    return lax.dynamic_update_slice(whole, part, start)


def interleave(core, mine, theirs):
    rows, cols = mine.shape[1:]
    whole = jnp.zeros((4, 2, rows, cols), mine.dtype)
    whole = put(whole, mine[:, None], 0, core, 0, 0)
    whole = put(whole, theirs[:, None], 0, 1 - core, 0, 0)
    return whole.reshape(8 * rows, cols)


def refresh_kernel(place_ref, *refs):
    sums, stacks, (mine_ref, theirs_ref) = refs[:4], refs[4:14], refs[14:16]
    whole, inner, held, total, first, sems = refs[16:]
    count, size = held.shape
    tall = size // 4
    wide = size // 2
    half = size // 8

    def copy(k, i):
        slot, other = k // 2, k % 2
        rows = half if i < 3 else half // 2
        if i < 3:
            stack = slot
            row = i * half + (i * (half // 2) if slot in (1, 2) else 0)
        elif slot < 2:
            stack = slot + 1
            row = half if i == 4 else 2 * half + half // 2
        else:
            stack = 4
            row = (i - 3) * half + (slot - 2) * (half // 2)
        source = stacks[2 * stack + other].at[pl.ds(row, rows), :]
        start = k * half + (half // 2 if i == 4 else 0)
        target = whole.at[pl.ds(start, rows), pl.ds(min(i, 3) * tall, tall)]
        return pltpu.make_async_copy(source, target, sems.at[k, i])

    def arrived(j):
        for k in (2 * j, 2 * j + 1):
            for i in range(5):
                copy(k, i).wait()

    spans = [slice(0, wide), slice(wide, size)]

    for k in range(8):
        for i in range(5):
            copy(k, i).start()
    squares = size / (16.0 * sum(part[...] for part in sums))
    square = squares[0, 0]
    last = (math.sqrt(size) * jnp.sqrt(squares))[0, 0]
    arrived(0)
    held[...] = whole[pl.ds(pl.multiple_of(place_ref[0], 16), count), :]
    total[...] = held[...].astype(F32)

    for j in range(4):
        if j:
            arrived(j)
        rows = slice(j * tall, (j + 1) * tall)
        inner[:, rows] = dot_nt(held[...], whole[rows, :]).astype(BF)

    def one_pass(i, carry):
        @pl.when(i > 0)
        def _():
            for span in spans:
                inner[:, span] = dot_nt(held[...], whole[span, :]).astype(BF)

        keep = jnp.where(i == 1, 0.0, 1.5)
        take = jnp.where(i == 1, square, -0.5 * square)

        def back(span):
            value = keep * total[:, span] + take * dot_nn(inner[...], whole[:, span])
            total[:, span] = value
            held[:, span] = value.astype(BF)

            @pl.when(i == 0)
            def _():
                first[:, span] = value

        back(spans[0])
        pl.when(i < 3)(functools.partial(back, spans[1]))
        return carry

    lax.fori_loop(0, 4, one_pass, 0)
    for k, flag in ((0, 1), (1, 0)):
        span = slice(k * tall, (k + 1) * tall)
        value = last * (1.5 * first[:, span] - 0.5 * total[:, span])

        @pl.when(place_ref[1] == flag)
        def _():
            mine_ref[...] = value

        @pl.when(place_ref[1] != flag)
        def _():
            theirs_ref[...] = value


def refresh(places, sums, stacks):
    tall = stacks[0].shape[1]
    size = 4 * tall
    count = size // 16
    in_vmem = pl.BlockSpec(memory_space=pltpu.VMEM)
    in_smem = pl.BlockSpec(memory_space=pltpu.SMEM)
    return pl.pallas_call(
        refresh_kernel,
        out_shape=[jax.ShapeDtypeStruct((count, tall), F32)] * 2,
        in_specs=[in_smem] + [in_vmem] * 4 + [pl.BlockSpec(memory_space=pl.ANY)] * 10,
        out_specs=[in_vmem] * 2,
        scratch_shapes=[
            pltpu.VMEM((size, size), BF),
            pltpu.VMEM((count, size), BF),
            pltpu.VMEM((count, size), BF),
            pltpu.VMEM((count, size), F32),
            pltpu.VMEM((count, size), F32),
            pltpu.SemaphoreType.DMA((8, 5)),
        ],
        compiler_params=pltpu.CompilerParams(vmem_limit_bytes=56 * 2**20),
        cost_estimate=pl.CostEstimate(
            flops=15 * count * size * size, bytes_accessed=2 * size * size, transcendentals=0
        ),
    )(places, *sums, *stacks)


def side_kernel(place_ref, core_ref, other_ref, cols_ref, rows_ref, power_ref, *refs):
    basis_ref, sum_ref, terms = refs[0], refs[1], refs[2:6]
    power, direction, cols, sems = refs[6:]
    rows, size = power_ref.shape
    step = core_ref.shape[0] // 4

    def copy(k):
        block = pl.ds(pl.multiple_of(place_ref[8 + k], 16), size)
        return pltpu.make_async_copy(cols_ref.at[block, :], cols.at[k], sems.at[k])

    for k in range(4):
        copy(k).start()
    total = jnp.zeros((step - 2 * rows, size), F32)
    for k in range(8):
        source = (core_ref, other_ref)[k // 4]
        start = (k % 4) * step
        place = pl.ds(pl.multiple_of(place_ref[k], 16), rows)
        direction[place, :] = source[start : start + rows, :]
        power[k * rows : (k + 1) * rows, :] = source[start + rows : start + 2 * rows, :]
        total += source[start + 2 * rows : start + step, :].astype(F32)
    sum_ref[...] = jnp.full(sum_ref.shape, jnp.sum(total))
    squares = jnp.zeros((rows, size), F32)
    for k in range(8):
        squares += jnp.square(power[k * rows : (k + 1) * rows, :].astype(F32))
    square = size / (16.0 * jnp.sum(squares))
    keep = power_ref[...]
    value = keep
    for turn in range(4):
        across = dot_nt(value.astype(BF), power[...]).astype(BF)
        moved = square * dot_nn(across, power[...])
        value = moved if turn == 1 else 1.5 * value - 0.5 * moved
        if turn == 0:
            keep = value
    scale = math.sqrt(size) * jnp.sqrt(jnp.full((rows, size), square))
    basis_ref[...] = scale * (1.5 * keep - 0.5 * value)
    back_half = dot_nn(rows_ref[...], direction[...]).astype(BF)
    for k in range(4):
        copy(k).wait()
        terms[k][...] = dot_nt(back_half, cols[k]).astype(BF)


def side(places, extra_core, extra_other, right_cols, left_rows, power_left):
    rows, size = power_left.shape
    in_vmem = pl.BlockSpec(memory_space=pltpu.VMEM)
    term = jax.ShapeDtypeStruct((rows, size), BF)
    sums = jax.ShapeDtypeStruct((8, 128), F32)
    return pl.pallas_call(
        side_kernel,
        out_shape=[jax.ShapeDtypeStruct((rows, size), F32), sums] + [term] * 4,
        in_specs=[pl.BlockSpec(memory_space=pltpu.SMEM)]
        + [in_vmem] * 2
        + [pl.BlockSpec(memory_space=pl.ANY)]
        + [in_vmem] * 2,
        out_specs=[in_vmem] * 6,
        scratch_shapes=[
            pltpu.VMEM((size, size), BF),
            pltpu.VMEM((size, size), BF),
            pltpu.VMEM((4, size, size), BF),
            pltpu.SemaphoreType.DMA((4,)),
        ],
        compiler_params=pltpu.CompilerParams(vmem_limit_bytes=56 * 2**20),
        cost_estimate=pl.CostEstimate(
            flops=26 * rows * size * size, bytes_accessed=12 * size * size, transcendentals=0
        ),
    )(places, extra_core, extra_other, right_cols, left_rows, power_left)


def partial_squares(a):
    squares = jnp.square(a.astype(F32)).reshape(-1, 16, a.shape[1])
    return jnp.sum(squares, axis=0).astype(BF)


def after(block, *others):
    return lax.optimization_barrier((block, *others))[0]


def local_pattern(gradient, moment_one, moment_two, stat_left, stat_right, basis_left, basis_right):
    rows_left = gradient.shape[0]
    rows_right = stat_right.shape[0]
    cols_right = stat_right.shape[1]
    shard_pos = lax.axis_index("shard")
    tensor_pos = lax.axis_index("tensor")
    z, x = shard_pos // 2, shard_pos % 2
    y, core = tensor_pos // 2, tensor_pos % 2
    straight = x == core
    inner = (z == 1) | (z == 2)
    half = rows_right // 2

    left_b = (basis_left / math.sqrt(D)).astype(BF)
    right_b = (basis_right / math.sqrt(FF)).astype(BF)
    stat_b = stat_right.astype(BF)
    part_left = rows_left // 2
    small = jnp.concatenate(
        [gradient, lax.dynamic_slice_in_dim(left_b, y * part_left, part_left, 0)]
    )
    rows_small = small.shape[0]

    turned, small_o1, small_i1, moment_one, moment_two, stat_left = stage(
        turn_over(right_b, straight),
        swap_outer(small),
        swap_inner(small),
        moment_one,
        moment_two,
        stat_left,
    )
    early = jnp.concatenate([moment_one, moment_two, stat_left]).astype(BF)
    got_i, got_o, stat_y, stat_x, early = stage(
        swap_inner(jnp.concatenate([turned, small_o1])),
        swap_outer(jnp.concatenate([turned, small_i1])),
        swap_y(stat_b),
        swap_x(stat_b),
        turn_over(early, straight),
    )
    turned_o1, small_o2 = got_o[:rows_right], got_o[rows_right:]
    turned_i1, small_i2 = got_i[:rows_right], got_i[rows_right:]
    small_1 = ordered_pair(z % 2 == 0, small, small_o1).reshape(2 * rows_small, cols_right)
    to_x = jnp.concatenate([stat_y[half:], small_1])
    to_y = jnp.concatenate([stat_x[:half], small_1])
    got_x, got_y, got_o, turned_i2 = stage(
        swap_x(to_x),
        swap_y(to_y),
        swap_outer(jnp.concatenate([turned_i1, small_i2])),
        swap_inner(turned_o1),
    )
    turned_o2, small_o3 = got_o[:rows_right], got_o[rows_right:]
    small_2 = ordered_pair(
        z < 2, jnp.where(inner, small_i1, small_o2), jnp.where(inner, small_i2, small_o3)
    ).reshape(2 * rows_small, cols_right)
    stat_xy = jnp.concatenate([got_y[:half], got_x[:half]])
    small_1x, small_1y = got_x[half:], got_y[half:]
    stat_keep = [jnp.where(straight, stat_b, stat_x), jnp.where(straight, stat_y, stat_xy)]
    stat_send = [jnp.where(straight, stat_x, stat_b), jnp.where(straight, stat_xy, stat_y)]
    turned_o3, got_x, got_y, stat_got = stage(
        swap_outer(turned_i2),
        swap_x(jnp.concatenate([small_1y[rows_small:], small_2])),
        swap_y(jnp.concatenate([small_1x[:rows_small], small_2])),
        swap_core(jnp.concatenate(stat_send)),
    )
    small_1xy = jnp.concatenate([got_y[:rows_small], got_x[:rows_small]])
    small_2x, small_2y = got_x[rows_small:], got_y[rows_small:]
    turned_z = in_order(
        z,
        turned,
        turned_o1,
        jnp.where(inner, turned_i1, turned_o2),
        jnp.where(inner, turned_i2, turned_o3),
    )
    stat_rows = jnp.zeros((rows_right, 4 * cols_right), BF)
    stat_rows = put(stat_rows, stat_keep[0], 0, (2 * y + core) * cols_right)
    stat_rows = put(stat_rows, stat_keep[1], 0, (2 - 2 * y + core) * cols_right)
    stat_rows = put(stat_rows, stat_got[:rows_right], 0, (2 * y + 1 - core) * cols_right)
    stat_rows = put(stat_rows, stat_got[rows_right:], 0, (3 - 2 * y - core) * cols_right)
    small_2hi, small_2lo, turned_got = stage(
        swap_x(small_2y[rows_small:]), swap_y(small_2x[:rows_small]), swap_core(turned_z)
    )
    right_cols = interleave(core, turned_z, turned_got)
    grad_core = jnp.zeros((4, 2, rows_left, 2 * cols_right), BF)
    left_all = jnp.zeros((4, 2, 2, part_left, cols_right), BF)
    small_2xy = jnp.concatenate([small_2lo, small_2hi])
    low = 2 * (z // 2)
    for block, at_z, at_x, at_y in (
        (small_1, low, x, y),
        (small_1x, low, 1 - x, y),
        (small_1y, low, x, 1 - y),
        (small_1xy, low, 1 - x, 1 - y),
        (small_2, 2 - low, x, y),
        (small_2x, 2 - low, 1 - x, y),
        (small_2y, 2 - low, x, 1 - y),
        (small_2xy, 2 - low, 1 - x, 1 - y),
    ):
        block = block.reshape(2, 1, rows_small, cols_right)
        grad_core = put(grad_core, block[:, :, :rows_left], at_z, at_x, 0, at_y * cols_right)
        left_all = put(left_all, block[:, :, None, rows_left:], at_z, at_x, at_y, 0, 0)
    grad_core = grad_core.reshape(8 * rows_left, 2 * cols_right)
    left_all = left_all.reshape(8 * rows_left, cols_right)

    grad_other = swap_core(grad_core)
    rows_core = lax.dynamic_slice_in_dim(
        right_cols.reshape(2, 2, cols_right, cols_right), core, 1, 1
    ).reshape(2 * cols_right, cols_right)
    carried = dot_nn(grad_core, rows_core)
    carried = (carried + swap_core(carried.astype(BF)).astype(F32)).astype(BF)

    def grad_block(at_x):
        start = (z // 2) * cols_right + at_x * rows_right
        ours = lax.dynamic_slice_in_dim(grad_core, start, rows_right, 1)
        other = lax.dynamic_slice_in_dim(grad_other, start, rows_right, 1)
        return jnp.where(z % 2 == core, ours, other)

    gram = 0.0
    for part in (grad_core, grad_other):
        rows = lax.dynamic_slice_in_dim(part, 2 * z * rows_left, 2 * rows_left, 0)
        gram = gram + dot_nt(rows, part)
    gram = gram.reshape(2, rows_left, cols_right)
    gram_own = lax.dynamic_index_in_dim(gram, x, 0, False)
    gram_here = lax.dynamic_index_in_dim(gram, core, 0, False)
    share = (1.0 - beta_stat) / D
    picked = grad_block(core)
    power = beta_stat * dot_nn(stat_rows, right_cols) + share * dot_tn(picked, carried)
    power, carried = stage(power.astype(BF), carried)

    here = (2 * z + core) * rows_left
    early = early.astype(F32)
    left_cols = lax.dynamic_slice_in_dim(left_all, here, rows_left, 1)
    rotated = dot_tn(left_cols, carried)
    _, _, direction = adam_moments(rotated, early[:rows_left], early[rows_left : 2 * rows_left])
    stat_t = blend_stat(early[2 * rows_left :], gram_here, FF)
    left_t = dot_nn(stat_t.astype(BF), left_all).astype(BF)
    extra = jnp.concatenate([direction, left_t, partial_squares(power)])

    own_grad = lax.dynamic_slice_in_dim(grad_core, y * cols_right, cols_right, 1)
    new_stat_right = blend_stat(stat_right, dot_tn(grad_block(x), own_grad), D)
    new_stat_left = blend_stat(stat_left, gram_own, FF)
    power_left = dot_nn(new_stat_left.astype(BF), left_all)

    power_x, power_y, near, power_i1, extra = stage(
        swap_x(power),
        swap_y(power),
        swap_outer(power),
        swap_inner(power),
        extra,
    )
    near_place, mid_place, far_place = places_z(z)
    side_places = jnp.stack(
        [
            (2 * at_z + at_x) * rows_left
            for at_x in (core, 1 - core)
            for at_z in (z, near_place, mid_place, far_place)
        ]
        + [
            ((y + along) % 2 * 2 + (x + across) % 2) * cols_right
            for along in range(2)
            for across in range(2)
        ]
    )
    places = jnp.stack(
        [jnp.where(straight, 0, rows_right) + core * half, straight.astype(jnp.int32)]
    )
    left_rows = lax.dynamic_slice_in_dim(left_all, here, rows_left, 0)
    to_x = jnp.concatenate([power_y[half:], near])
    to_y = jnp.concatenate([power_x[:half], near])
    (
        got_o,
        got_i,
        got_x,
        got_y,
        new_stat_right,
        new_stat_left,
        power_left,
        left_rows,
        side_places,
        places,
    ) = stage(
        swap_outer(jnp.concatenate([power_i1, extra])),
        swap_inner(jnp.concatenate([near, extra])),
        swap_x(to_x),
        swap_y(to_y),
        new_stat_right,
        new_stat_left,
        power_left,
        left_rows,
        side_places,
        places,
    )
    stack0 = jnp.concatenate([power, power_x, power_y])
    stack1 = jnp.concatenate([near, got_x, got_y])
    near_x, near_y = got_x[half:], got_y[half:]
    power_o2, extra_o1 = got_o[:rows_right], got_o[rows_right:]
    power_i2, extra_i1 = got_i[:rows_right], got_i[rows_right:]
    mid = jnp.where(inner, power_i1, power_o2)
    to_x = jnp.concatenate([near_y[half:], mid])
    to_y = jnp.concatenate([near_x[:half], mid])
    got_x, got_y, got_o, extra_i2, other0 = stage(
        swap_x(to_x),
        swap_y(to_y),
        swap_outer(jnp.concatenate([power_i2, extra_i1])),
        swap_inner(extra_o1),
        swap_core(stack0),
    )
    stack2 = jnp.concatenate([mid, got_x, got_y])
    mid_x, mid_y = got_x[half:], got_y[half:]
    power_o3, extra_o2 = got_o[:rows_right], got_o[rows_right:]
    far = jnp.where(inner, power_i2, power_o3)
    got_x, got_y, extra_o3, other1, rotated = stage(
        swap_x(far),
        swap_y(far),
        swap_outer(extra_i2),
        swap_core(stack1),
        turn_over(rotated.astype(BF), straight),
    )
    far_x, far_y = got_x, got_y
    stack3 = jnp.concatenate([far, far_x, far_y])
    extra_core = jnp.concatenate(
        [extra, extra_o1, jnp.where(inner, extra_i1, extra_o2), jnp.where(inner, extra_i2, extra_o3)]
    )
    extra_other = swap_core(extra_core)
    stack3 = after(stack3, extra_other)
    new_basis_left, sums, *terms = side(
        side_places,
        extra_core,
        extra_other,
        right_cols,
        left_rows,
        power_left,
    )
    got_y, got_x, other2, new_basis_left, sums = stage(
        swap_y(jnp.concatenate([mid_x[:half], far_x[:half]])),
        swap_x(jnp.concatenate([mid_y[half:], far_y[half:]])),
        swap_core(stack2),
        new_basis_left,
        sums,
    )
    stack4 = jnp.concatenate([got_y, got_x])
    other3, other4 = swap_core(stack3), swap_core(stack4)
    sums = (sums, swap_x(sums), swap_y(sums), swap_diagonal(sums))
    new_moment_one, new_moment_two, _ = adam_moments(
        rotated.astype(F32), moment_one, moment_two
    )

    terms = [
        swap_to(across, along)(terms[2 * along + across])
        for along in range(2)
        for across in range(2)
    ]
    update = sum(term.astype(F32) for term in terms).astype(BF)

    stacks = (
        stack0, other0, stack1, other1, stack2, other2, stack3, other3, stack4, other4
    )
    mine, theirs = refresh(places, sums, stacks)
    theirs = swap_core(theirs)
    new_basis_right = jnp.zeros((rows_right, cols_right), F32)
    new_basis_right = put(new_basis_right, mine, core * half, 0)
    new_basis_right = put(new_basis_right, theirs, (1 - core) * half, 0)
    return (
        update,
        new_moment_one,
        new_moment_two,
        new_stat_left,
        new_stat_right,
        new_basis_left,
        new_basis_right,
    )


def solution(mesh):
    nz, nx, ny, nc = PATTERN
    fits = (mesh.shape["shard"], mesh.shape["tensor"]) == (nz * nx, ny * nc)
    local = local_pattern if fits else local_general
    placed = (
        P("shard", "tensor"),
        P("shard", "tensor"),
        P("shard", "tensor"),
        P("shard", None),
        P("shard", "tensor"),
        P("shard", None),
        P("shard", "tensor"),
    )
    return jax.shard_map(
        local,
        mesh=mesh,
        in_specs=placed,
        out_specs=(
            P("shard", "tensor"),
            P("shard", "tensor"),
            P("shard", "tensor"),
            P("shard", None),
            P("shard", "tensor"),
            P("shard", None),
            P("shard", "tensor"),
        ),
        check_vma=False,
    )
```
